32 devices in a mesh: depth: 4 (over z), tile: 8 (over y, x, core).
Axes of the slice: x: 2, y: 2, z: 4, core: 2. Of those that a mesh axis runs over, the one named last changes fastest.
Arguments:
- field: bfloat16 [192, 1152, 1152], P(('depth', 'tile')), may hold values from -6 to 6
- transfer: float32 [4, 16], replicated, may hold values from 0 to 1
- bin_order: int32 [16], replicated, may hold values from 0 to 15, each once
- light_angles: float32 [2], replicated, may hold values from -0.6 to 1.4, as said below
Outputs:
- image: float32 [4, 1152, 1152], P(None, 'tile', 'depth')
The draws below stay inside these ranges and needn't reach their ends.
Inputs may be any that keep to these rules, and one draw needn't show every extreme that they name: `bin_order`: a permutation of 0 .. 15. `light_angles`: azimuth first, then polar angle, in radians.
All inputs are finite; a program needn't handle non-finite values.
Results may differ from the reference program's by a relative error of at most 0.0003.
Values may be sent and summed in bfloat16 or wider, within the bound.
No kernel may reach another device: no remote copies, remote signals or barrier semaphores. Data moves between devices by JAX's collectives and lax.ppermute only.
A program may use at most 320 MiB of HBM per device.

```python
import jax
import jax.numpy as jnp
from jax import lax

NY = 1152
NZ = 1152
NB = 16
NX = 192
N_TILE = 8


def draw_light_angles(key, part):
    key = jax.random.fold_in(key, 7)
    unit = jax.random.uniform(key, (2,), jnp.float32)
    azimuth = -0.6 + 1.2 * unit[0]
    polar = 0.7 + 0.5 * unit[1]
    return jnp.stack([azimuth, polar]).astype(jnp.float32)


def block_scale(rng, extent, cuts, smallest, high):
    gain, own = 1.0, jax.random.fold_in(rng, 6)
    for dim, blocks in cuts:
        heights = jnp.exp(jax.random.uniform(jax.random.fold_in(own, dim), (blocks,), jnp.float32, smallest / len(cuts), high / len(cuts)))
        gain = gain * jnp.repeat(heights, extent[dim] // blocks).reshape([-1 if axis == dim else 1 for axis in range(len(extent))])
    return gain


def normal_values(stream_key, shape, scale, reach, pieces=(), held_as=jnp.bfloat16):
    values = jax.random.normal(stream_key, shape, jnp.float32) * scale
    if len(pieces) > 0:
        values = block_scale(stream_key, shape, pieces, -0.22, 0.18) * values
    return jnp.clip(values, min=-reach, max=reach).astype(held_as)


def setup_inputs(seed: int = 0) -> dict:
    arg_keys = jax.random.split(jax.random.key(seed), 5)
    return {
        "field": normal_values(arg_keys[0], (NX, NY, NZ), 1.0, 6.0, ((0, 32),)),
        "transfer": jnp.clip(jax.random.uniform(arg_keys[1], (4, NB), jnp.float32, 0.0, 1.0), 0.0, 1.0),
        "bin_order": jax.random.permutation(arg_keys[2], NB).astype(jnp.int32),
        "light_angles": draw_light_angles(jax.random.fold_in(arg_keys[4], 71), 0),
    }


def classify(padded, transfer, bin_order, light_angles):
    table = jnp.take(transfer, bin_order, axis=1)
    centre = padded[1:-1, 1:-1, :]
    grad_x = (padded[2:, 1:-1, :] - padded[:-2, 1:-1, :]) * 0.5
    grad_y = (padded[1:-1, 2:, :] - padded[1:-1, :-2, :]) * 0.5
    zpadded = jnp.pad(centre, ((0, 0), (0, 0), (1, 1)))
    grad_z = (zpadded[:, :, 2:] - zpadded[:, :, :-2]) * 0.5
    azimuth = light_angles[0]
    polar = light_angles[1]
    light_x = jnp.cos(azimuth) * jnp.sin(polar)
    light_y = jnp.sin(azimuth) * jnp.sin(polar)
    light_z = jnp.cos(polar)
    length = jnp.sqrt(grad_x * grad_x + grad_y * grad_y + grad_z * grad_z)
    facing = jnp.abs(grad_x * light_x + grad_y * light_y + grad_z * light_z)
    shade = 0.3 + 0.7 * facing / jnp.maximum(length, 1.0)
    bins = table.shape[1]
    position = jnp.clip((centre + 3.0) / 6.0, 0.0, 1.0) * (bins - 1)
    red = jnp.zeros_like(centre)
    green = jnp.zeros_like(centre)
    blue = jnp.zeros_like(centre)
    opacity = jnp.zeros_like(centre)
    for level in range(bins):
        weight = jnp.maximum(0.0, 1.0 - jnp.abs(position - level))
        red = red + weight * table[0, level]
        green = green + weight * table[1, level]
        blue = blue + weight * table[2, level]
        opacity = opacity + weight * table[3, level]
    alpha = 0.01 * opacity
    scaled = 0.15 * shade
    return (jnp.stack([red * scaled, green * scaled, blue * scaled]), alpha)

def march(emission, alpha):
    through = jnp.cumprod(1.0 - alpha, axis=0)
    before = jnp.concatenate([jnp.ones_like(through[:1]), through[:-1]], axis=0)
    colour = lax.optimization_barrier(jnp.sum(emission * before[None], axis=1))
    return jnp.concatenate([colour, through[-1][None]], axis=0)

def reference(field, transfer, bin_order, light_angles):
    padded = jnp.pad(field, ((1, 1), (1, 1), (0, 0)))
    blocks = NY // N_TILE

    def render(index):
        start = (index * blocks).astype(jnp.int32)
        piece = lax.dynamic_slice_in_dim(padded, start, blocks + 2, 1).astype(jnp.float32)
        emission, alpha = classify(piece, transfer, bin_order, light_angles)
        partial_image = march(emission, alpha)
        return jnp.concatenate([partial_image[:3], 1.0 - partial_image[3:]], axis=0)
    stacked = lax.map(render, jnp.arange(N_TILE, dtype=jnp.int32))
    return jnp.transpose(stacked, (1, 0, 2, 3)).reshape(4, NY, NZ)
```

```python
import functools
import math

import jax
import jax.numpy as jnp
from jax import lax
from jax.experimental import pallas as pl
from jax.experimental.pallas import tpu as pltpu
from jax.sharding import PartitionSpec as P

LANES = 128
CODES = 32700.0
VMEM_LIMIT = 56 * 1024 * 1024


def unit_rows(rows):
    return 48 if rows % 48 == 0 else rows


def encode(values):
    top = functools.reduce(jnp.maximum, values)
    top = jnp.max(top, axis=0, keepdims=True)
    exponent = jnp.ceil(jnp.log2(jnp.maximum(top, 1e-30)))
    factor = jnp.exp2(-exponent) * CODES
    codes = [(v * factor + 0.5).astype(jnp.int32).astype(jnp.int16) for v in values]
    row = jnp.broadcast_to(exponent, (16, exponent.shape[1]))
    return codes, row.astype(jnp.int32).astype(jnp.int16)


def decode(codes, row):
    exponent = row.astype(jnp.int32).astype(jnp.float32)[0:1]
    scale = jnp.exp2(exponent) * (1.0 / CODES)
    return [c.astype(jnp.int32).astype(jnp.float32) * scale for c in codes]


def over(front, back):
    clear = 1.0 - front[3]
    return [f + clear * b for f, b in zip(front, back)]


def render_kernel(ctl, light, table, main, above, below, before, after, send, keep, cells, slopes, image, edge, *, groups, units, unit, block, rows, offset, total):
    i = pl.program_id(0)
    half = (groups // 2) * units
    rest = lax.rem(i, half)
    sending = i < half
    parity = jnp.where(sending, 1 - ctl[0], ctl[0])
    group = 2 * (rest // units) + parity
    start = group * rows + offset + lax.rem(rest, units) * unit
    layers = main.shape[0]
    width = main.shape[2]
    if block == unit:
        shift = 0
    else:
        shift = pl.multiple_of(lax.rem(start, block), 8)

    lane = lax.broadcasted_iota(jnp.int32, (8, width), 1)
    first_lane = lane == 0
    last_lane = lane == width - 1

    def load_layer(layer, carry):
        if block != unit:
            edge[...] = main[layer].astype(jnp.float32)
        for r in range(0, unit, 16):
            n = min(16, unit - r)
            if block == unit:
                wide = main[layer, r:r + n, :].astype(jnp.float32)
            else:
                wide = edge[pl.ds(shift + r, n), :]
            for q in range(0, n, 8):
                x = wide[q:q + 8]
                left = jnp.where(first_lane, 0.0, pltpu.roll(x, 1, 1))
                right = jnp.where(last_lane, 0.0, pltpu.roll(x, width - 1, 1))
                cells[layer + 1, 8 + r + q:16 + r + q, :] = x
                slopes[layer, r + q:r + q + 8, :] = right - left
        up = above[layer].astype(jnp.float32)
        down = below[layer].astype(jnp.float32)
        if block == unit:
            up = up[8:16]
            down = down[0:8]
        else:
            up = jnp.where(lax.rem(start, 16) == 0, up[8:16], up[0:8])
            down = jnp.where(lax.rem(start + unit, 16) == 0, down[0:8], down[8:16])
        cells[layer + 1, 0:8, :] = jnp.where(start > 0, up, 0.0)
        cells[layer + 1, 8 + unit:16 + unit, :] = jnp.where(start + unit < total, down, 0.0)
        return carry

    lax.fori_loop(0, layers, load_layer, 0)
    cells[0, 8:8 + unit, :] = before[0].astype(jnp.float32)
    cells[layers + 1, 8:8 + unit, :] = after[0].astype(jnp.float32)

    lx, ly, lz = light[0], light[1], light[2]
    step = 16 if unit % 16 == 0 else 8
    tables = [jnp.broadcast_to(table[k:k + 1, :], (step, LANES)) for k in range(8)]

    def strip(c, carry):
        cols = pl.ds(pl.multiple_of(c * LANES, LANES), LANES)
        for r in range(0, unit, step):
            low = cells[0, 8 + r:8 + r + step, cols]
            here = cells[1, 8 + r:8 + r + step, cols]
            clear = None
            for layer in range(layers):
                high = cells[layer + 2, 8 + r:8 + r + step, cols]
                gx = high - low
                gy = cells[layer + 1, 9 + r:9 + r + step, cols] - cells[layer + 1, 7 + r:7 + r + step, cols]
                gz = slopes[layer, r:r + step, cols]
                facing = jnp.abs(gx * lx + gy * ly + gz * lz)
                square = gx * gx + gy * gy + gz * gz
                shade = 0.045 + facing * lax.rsqrt(jnp.maximum(square, 4.0))
                position = jnp.clip(here * 2.5 + 7.5, 0.0, 15.0)
                index = position.astype(jnp.int32)
                part = position - index.astype(jnp.float32)
                tf = [
                    jnp.take_along_axis(tables[k], index, axis=1, mode="promise_in_bounds")
                    + part * jnp.take_along_axis(tables[4 + k], index, axis=1, mode="promise_in_bounds")
                    for k in range(4)
                ]
                if clear is None:
                    total_colour = [tf[k] * shade for k in range(3)]
                    clear = 1.0 - tf[3]
                else:
                    seen = shade * clear
                    total_colour = [total_colour[k] + tf[k] * seen for k in range(3)]
                    clear = clear - clear * tf[3]
                low, here = here, high
            for k in range(3):
                image[k, r:r + step, cols] = total_colour[k]
            image[3, r:r + step, cols] = 1.0 - clear
        return carry

    lax.fori_loop(0, width // LANES, strip, 0)
    put_unit(image, send, keep, sending, unit, width)


def put_unit(image, send, keep, sending, unit, width):
    @pl.when(sending)
    def _():
        def strip(c, carry):
            cols = pl.ds(pl.multiple_of(c * LANES, LANES), LANES)
            codes, row = encode([image[k, :, cols] for k in range(4)])
            for k in range(4):
                send[0, k * unit:(k + 1) * unit, cols] = codes[k]
            send[0, 4 * unit:4 * unit + 16, cols] = row
            return carry

        lax.fori_loop(0, width // LANES, strip, 0)

    @pl.when(jnp.logical_not(sending))
    def _():
        keep[0] = image[...]


def get_unit(ctl, mine, got, cols, unit):
    theirs = decode(
        [got[0, k * unit:(k + 1) * unit, cols] for k in range(4)],
        got[0, 4 * unit:4 * unit + 16, cols],
    )
    ours = [mine[0, k, :, cols] for k in range(4)]
    behind = ctl[1] == 1
    front = [jnp.where(behind, t, o) for t, o in zip(theirs, ours)]
    back = [jnp.where(behind, o, t) for t, o in zip(theirs, ours)]
    return over(front, back)


def merge_kernel(ctl, mine, got, send, keep, image, *, groups, units, unit):
    i = pl.program_id(0)
    width = mine.shape[3]

    def strip(c, carry):
        cols = pl.ds(pl.multiple_of(c * LANES, LANES), LANES)
        merged = get_unit(ctl, mine, got, cols, unit)
        for k in range(4):
            image[k, :, cols] = merged[k]
        return carry

    lax.fori_loop(0, width // LANES, strip, 0)
    put_unit(image, send, keep, i < (groups // 2) * units, unit, width)


def last_merge_kernel(ctl, mine, got, send, image, *, unit, blocks):
    width = mine.shape[3]

    def strip(c, carry):
        cols = pl.ds(pl.multiple_of(c * LANES, LANES), LANES)
        merged = get_unit(ctl, mine, got, cols, unit)
        for k in range(4):
            image[k, :, cols] = merged[k]
        return carry

    lax.fori_loop(0, width // LANES, strip, 0)
    part = width // blocks
    for b in range(blocks):
        wide = jnp.concatenate([image[k, :, b * part:(b + 1) * part] for k in range(4)], axis=1)
        codes, row = encode([wide])
        send[b, 0, 0:unit, :] = codes[0]
        send[b, 0, unit:unit + 16, :] = row


def compose_kernel(got, out, *, unit, blocks):
    part = out.shape[2]
    total = None
    for b in range(blocks):
        wide = decode([got[b, 0, 0:unit, :]], got[b, 0, unit:unit + 16, :])[0]
        layer = [wide[:, k * part:(k + 1) * part] for k in range(4)]
        total = layer if total is None else over(total, layer)
    for k in range(4):
        out[k] = total[k]


def params():
    return pltpu.CompilerParams(vmem_limit_bytes=VMEM_LIMIT, dimension_semantics=("arbitrary",))


def unit_index(groups, units, bit):
    half = (groups // 2) * units

    def index(i, ctl):
        rest = lax.rem(i, half)
        parity = jnp.where(i < half, 1 - ctl[bit], ctl[bit])
        return (2 * (rest // units) + parity) * units + lax.rem(rest, units)

    return index


def split_outputs(groups, units, unit, width):
    half = (groups // 2) * units
    shapes = [
        jax.ShapeDtypeStruct((half, 4 * unit + 16, width), jnp.int16),
        jax.ShapeDtypeStruct((half, 4, unit, width), jnp.float32),
    ]
    specs = [
        pl.BlockSpec((1, 4 * unit + 16, width), lambda i, ctl: (jnp.minimum(i, half - 1), 0, 0)),
        pl.BlockSpec((1, 4, unit, width), lambda i, ctl: (jnp.maximum(i - half, 0), 0, 0, 0)),
    ]
    return shapes, specs


def render(ctl, light, table, field, before, after, *, groups, units, unit, rows, offset):
    layers, total, width = field.shape
    block = math.lcm(unit, 16)
    half = (groups // 2) * units
    index = unit_index(groups, units, 0)

    def start(i, ctl):
        unit_at = index(i, ctl)
        return (unit_at // units) * rows + offset + lax.rem(unit_at, units) * unit

    def main_at(i, ctl):
        return (0, start(i, ctl) // block, 0)

    def above_at(i, ctl):
        return (0, jnp.maximum(start(i, ctl) - 1, 0) // 16, 0)

    def below_at(i, ctl):
        return (0, jnp.minimum(start(i, ctl) + unit, total - 1) // 16, 0)

    shapes, specs = split_outputs(groups, units, unit, width)
    kernel = functools.partial(
        render_kernel, groups=groups, units=units, unit=unit, block=block, rows=rows, offset=offset, total=total
    )
    cells = layers * 2 * half * unit * width
    return pl.pallas_call(
        kernel,
        grid_spec=pltpu.PrefetchScalarGridSpec(
            num_scalar_prefetch=1,
            grid=(2 * half,),
            in_specs=[
                pl.BlockSpec(memory_space=pltpu.SMEM),
                pl.BlockSpec((8, LANES), lambda i, ctl: (0, 0)),
                pl.BlockSpec((layers, block, width), main_at),
                pl.BlockSpec((layers, 16, width), above_at),
                pl.BlockSpec((layers, 16, width), below_at),
                pl.BlockSpec((1, unit, width), lambda i, ctl: (index(i, ctl), 0, 0)),
                pl.BlockSpec((1, unit, width), lambda i, ctl: (index(i, ctl), 0, 0)),
            ],
            out_specs=specs,
            scratch_shapes=[
                pltpu.VMEM((layers + 2, unit + 16, width), jnp.float32),
                pltpu.VMEM((layers, unit, width), jnp.float32),
                pltpu.VMEM((4, unit, width), jnp.float32),
                pltpu.VMEM((block, width), jnp.float32),
            ],
        ),
        out_shape=shapes,
        compiler_params=params(),
        cost_estimate=pl.CostEstimate(flops=50 * cells, bytes_accessed=6 * cells, transcendentals=cells),
        name="render",
    )(ctl, light, table, field, field, field, before, after)


def merge(ctl, mine, got, *, groups, units, unit):
    width = mine.shape[3]
    half = (groups // 2) * units
    index = unit_index(groups, units, 0)
    shapes, specs = split_outputs(groups, units, unit, width)
    cells = 4 * 2 * half * unit * width
    return pl.pallas_call(
        functools.partial(merge_kernel, groups=groups, units=units, unit=unit),
        grid_spec=pltpu.PrefetchScalarGridSpec(
            num_scalar_prefetch=1,
            grid=(2 * half,),
            in_specs=[
                pl.BlockSpec((1, 4, unit, width), lambda i, ctl: (index(i, ctl), 0, 0, 0)),
                pl.BlockSpec((1, 4 * unit + 16, width), lambda i, ctl: (index(i, ctl), 0, 0)),
            ],
            out_specs=specs,
            scratch_shapes=[pltpu.VMEM((4, unit, width), jnp.float32)],
        ),
        out_shape=shapes,
        compiler_params=params(),
        cost_estimate=pl.CostEstimate(flops=8 * cells, bytes_accessed=9 * cells, transcendentals=0),
        name="merge",
    )(ctl, mine, got)


def last_merge(ctl, mine, got, *, units, unit, blocks):
    width = mine.shape[3]
    cells = 4 * units * unit * width
    return pl.pallas_call(
        functools.partial(last_merge_kernel, unit=unit, blocks=blocks),
        grid_spec=pltpu.PrefetchScalarGridSpec(
            num_scalar_prefetch=1,
            grid=(units,),
            in_specs=[
                pl.BlockSpec((1, 4, unit, width), lambda i, ctl: (i, 0, 0, 0)),
                pl.BlockSpec((1, 4 * unit + 16, width), lambda i, ctl: (i, 0, 0)),
            ],
            out_specs=pl.BlockSpec((blocks, 1, unit + 16, 4 * width // blocks), lambda i, ctl: (0, i, 0, 0)),
            scratch_shapes=[pltpu.VMEM((4, unit, width), jnp.float32)],
        ),
        out_shape=jax.ShapeDtypeStruct((blocks, units, unit + 16, 4 * width // blocks), jnp.int16),
        compiler_params=params(),
        cost_estimate=pl.CostEstimate(flops=8 * cells, bytes_accessed=9 * cells, transcendentals=0),
        name="last_merge",
    )(ctl, mine, got)


def compose(got, *, unit):
    blocks, units = got.shape[:2]
    part = got.shape[3] // 4
    cells = 4 * units * unit * part * blocks
    return pl.pallas_call(
        functools.partial(compose_kernel, unit=unit, blocks=blocks),
        grid=(units,),
        in_specs=[pl.BlockSpec((blocks, 1, unit + 16, 4 * part), lambda i: (0, i, 0, 0))],
        out_specs=pl.BlockSpec((4, unit, part), lambda i: (0, i, 0)),
        out_shape=jax.ShapeDtypeStruct((4, units * unit, part), jnp.float32),
        compiler_params=params(),
        cost_estimate=pl.CostEstimate(flops=8 * cells, bytes_accessed=3 * cells, transcendentals=0),
        name="compose",
    )(got)


def chunk_units(units):
    return [1] * units


def per_device(field, transfer, bin_order, light_angles):
    tiles = lax.axis_size("tile")
    blocks = lax.axis_size("depth")
    devices = tiles * blocks
    layers, total, width = field.shape
    rows = total // tiles
    unit = unit_rows(rows)
    levels = tiles.bit_length() - 1

    table = jnp.take(transfer, bin_order, axis=1)
    table = table * jnp.array([[1.0], [1.0], [1.0], [0.01]], jnp.float32)
    bins = table.shape[1]
    slope = jnp.concatenate([table[:, 1:] - table[:, :-1], jnp.zeros_like(table[:, :1])], axis=1)
    table = jnp.pad(jnp.concatenate([table, slope], axis=0), ((0, 0), (0, LANES - bins)))
    azimuth, polar = light_angles[0], light_angles[1]
    light = 0.105 * jnp.stack(
        [jnp.cos(azimuth) * jnp.sin(polar), jnp.sin(azimuth) * jnp.sin(polar), jnp.cos(polar)]
    )

    tile = lax.axis_index("tile")
    bits = [((tile >> b) & 1).astype(jnp.int32) for b in range(levels)]
    controls = [jnp.stack([bits[min(b, levels - 1)], bits[max(b - 1, 0)]]) for b in range(levels + 1)]
    up = [(i, i + 1) for i in range(devices - 1)]
    down = [(j, i) for i, j in up]
    both = ("depth", "tile")
    first = field[0].reshape(tiles, rows, width)
    last = field[layers - 1].reshape(tiles, rows, width)

    pieces = []
    offset = 0
    for units in chunk_units(rows // unit):
        size = units * unit
        halo = lambda layer: layer[:, offset:offset + size].reshape(tiles * units, unit, width)
        before = lax.ppermute(halo(last), both, up)
        after = lax.ppermute(halo(first), both, down)
        send, keep = render(
            controls[0], light, table, field, before, after,
            groups=tiles, units=units, unit=unit, rows=rows, offset=offset,
        )
        groups = tiles // 2
        for level in range(levels):
            pairs = [(i, i ^ (1 << level)) for i in range(tiles)]
            got = lax.ppermute(send, "tile", pairs)
            if level + 1 < levels:
                send, keep = merge(controls[level + 1], keep, got, groups=groups, units=units, unit=unit)
                groups //= 2
        blocked = last_merge(controls[levels], keep, got, units=units, unit=unit, blocks=blocks)
        blocked = lax.all_to_all(blocked, "depth", split_axis=0, concat_axis=0, tiled=True)
        pieces.append(compose(blocked, unit=unit))
        offset += size
    return jnp.concatenate(pieces, axis=1) if len(pieces) > 1 else pieces[0]


def solution(mesh):
    in_specs = (P(("depth", "tile"), None, None), P(), P(), P())
    out_specs = P(None, "tile", "depth")
    return jax.shard_map(
        per_device, mesh=mesh, in_specs=in_specs, out_specs=out_specs, check_vma=False
    )
```

```python
import functools
import math

import jax
import jax.numpy as jnp
from jax import lax
from jax.experimental import pallas as pl
from jax.experimental.pallas import tpu as pltpu
from jax.sharding import PartitionSpec as P

LANES = 128
CODES = 32700.0
VMEM_LIMIT = 56 * 1024 * 1024


def unit_rows(rows):
    return 48 if rows % 48 == 0 else rows


def encode(values):
    top = functools.reduce(jnp.maximum, values)
    top = jnp.max(top, axis=0, keepdims=True)
    exponent = jnp.ceil(jnp.log2(jnp.maximum(top, 1e-30)))
    factor = jnp.exp2(-exponent) * CODES
    codes = [(v * factor + 0.5).astype(jnp.int32).astype(jnp.int16) for v in values]
    row = jnp.broadcast_to(exponent, (16, exponent.shape[1]))
    return codes, row.astype(jnp.int32).astype(jnp.int16)


def decode(codes, row):
    exponent = row.astype(jnp.int32).astype(jnp.float32)[0:1]
    scale = jnp.exp2(exponent) * (1.0 / CODES)
    return [c.astype(jnp.int32).astype(jnp.float32) * scale for c in codes]


def over(front, back):
    clear = 1.0 - front[3]
    return [f + clear * b for f, b in zip(front, back)]


def lookup(table, index):
    numbers = lax.GatherDimensionNumbers(
        offset_dims=(), collapsed_slice_dims=(1,), start_index_map=(1,),
        operand_batching_dims=(0,), start_indices_batching_dims=(0,),
    )
    return lax.gather(
        table, index[..., None], numbers, slice_sizes=(1, 1), mode=lax.GatherScatterMode.PROMISE_IN_BOUNDS
    )


def padded_rows(unit):
    return -(-unit // 16) * 16


def each_strip(width, body):
    strips = width // LANES
    together = 3 if strips % 3 == 0 else 1

    def step(c, carry):
        for k in range(together):
            body(pl.multiple_of((c * together + k) * LANES, LANES))
        return carry

    lax.fori_loop(0, strips // together, step, 0)


def render_kernel(ctl, light, table, row_band, column_band, main, above, below, before, after, send, keep, cells, image, stage, ends, *, groups, units, unit, block, rows, offset, total):
    i = pl.program_id(0)
    half = (groups // 2) * units
    rest = lax.rem(i, half)
    sending = i < half
    parity = jnp.where(sending, 1 - ctl[0], ctl[0])
    group = 2 * (rest // units) + parity
    start = group * rows + offset + lax.rem(rest, units) * unit
    layers = main.shape[0]
    width = main.shape[2]
    tall = padded_rows(unit)
    aligned = block == unit
    inner = slice(LANES, LANES + width)

    @pl.when(i == 0)
    def _():
        cells[:, :, 0:LANES] = jnp.zeros((layers, tall + 32, LANES), jnp.bfloat16)
        cells[:, :, LANES + width:] = jnp.zeros((layers, tall + 32, LANES), jnp.bfloat16)

    def load_layer(layer, carry):
        up = above[layer].astype(jnp.float32)
        down = below[layer].astype(jnp.float32)
        up = jnp.where(start > 0, up, 0.0)
        down = jnp.where(start + unit < total, down, 0.0)
        if aligned:
            cells[layer, 0:16, inner] = up.astype(jnp.bfloat16)
            cells[layer, 16:16 + unit, inner] = main[layer]
            cells[layer, 16 + unit:32 + unit, inner] = down.astype(jnp.bfloat16)
        else:
            shift = pl.multiple_of(lax.rem(start, block), 8)
            stage[0:block, :] = main[layer].astype(jnp.float32)
            body = stage[pl.ds(shift, unit), :]
            up = jnp.where(lax.rem(start, 16) == 0, up[8:16], up[0:8])
            down = jnp.where(lax.rem(start + unit, 16) == 0, down[0:8], down[8:16])
            stage[0:8, :] = jnp.zeros((8, width), jnp.float32)
            stage[8:16, :] = up
            stage[16:16 + unit, :] = body
            stage[16 + unit:24 + unit, :] = down
            stage[24 + unit:tall + 32, :] = jnp.zeros((tall + 8 - unit, width), jnp.float32)
            cells[layer, :, inner] = stage[0:tall + 32, :].astype(jnp.bfloat16)
        return carry

    lax.fori_loop(0, layers, load_layer, 0)
    if not aligned:
        ends[0, 0:unit, :] = before[0].astype(jnp.float32)
        ends[1, 0:unit, :] = after[0].astype(jnp.float32)

    lx, ly, lz = light[0], light[1], light[2]
    step = 16
    tables = [jnp.broadcast_to(table[k:k + 1, :], (step, LANES)) for k in range(8)]

    def strip(c, carry):
        at = pl.multiple_of(c * LANES, LANES)
        cols = pl.ds(at, LANES)
        shifted = pl.ds(pl.multiple_of(at + LANES, LANES), LANES)
        window = pl.ds(at, 3 * LANES)
        spans = [slice(r, r + step) for r in range(0, tall, step)]
        inside = [slice(16 + r, 16 + r + step) for r in range(0, tall, step)]
        if aligned:
            low = [before[0, s, cols].astype(jnp.float32) for s in spans]
            far = [after[0, s, cols].astype(jnp.float32) for s in spans]
        else:
            low = [ends[0, s, cols] for s in spans]
            far = [ends[1, s, cols] for s in spans]
        here = [cells[0, s, shifted].astype(jnp.float32) for s in inside]
        clear = [None] * len(spans)
        colour = [None] * len(spans)
        for layer in range(layers):
            slope_y = jnp.dot(row_band[...], cells[layer, :, shifted], preferred_element_type=jnp.float32)
            slope_z = jnp.dot(cells[layer, 16:16 + tall, window], column_band[...], preferred_element_type=jnp.float32)
            for n, s in enumerate(spans):
                if layer + 1 < layers:
                    high = cells[layer + 1, inside[n], shifted].astype(jnp.float32)
                else:
                    high = far[n]
                gx = high - low[n]
                gy = slope_y[s]
                gz = slope_z[s]
                facing = jnp.abs(gx * lx + gy * ly + gz * lz)
                square = gx * gx + gy * gy + gz * gz
                shade = 0.045 + facing * lax.rsqrt(jnp.maximum(square, 4.0))
                position = jnp.clip(here[n] * 2.5 + 7.5, 0.0, 15.0)
                index = position.astype(jnp.int32)
                part = position - index.astype(jnp.float32)
                tf = [lookup(tables[k], index) + part * lookup(tables[4 + k], index) for k in range(4)]
                if layer == 0:
                    colour[n] = [tf[k] * shade for k in range(3)]
                    clear[n] = 1.0 - tf[3]
                else:
                    seen = shade * clear[n]
                    colour[n] = [colour[n][k] + tf[k] * seen for k in range(3)]
                    clear[n] = clear[n] - clear[n] * tf[3]
                low[n], here[n] = here[n], high
        for n, s in enumerate(spans):
            for k in range(3):
                image[k, s, cols] = colour[n][k]
            image[3, s, cols] = 1.0 - clear[n]
        return carry

    lax.fori_loop(0, width // LANES, strip, 0)

    @pl.when(sending)
    def _():
        def put(at):
            cols = pl.ds(at, LANES)
            put_codes(send, [image[k, 0:unit, cols] for k in range(4)], cols, unit)

        each_strip(width, put)

    @pl.when(jnp.logical_not(sending))
    def _():
        keep[0] = image[:, 0:unit, :]


def put_codes(send, values, cols, unit):
    codes, row = encode(values)
    for k in range(4):
        send[0, k * unit:(k + 1) * unit, cols] = codes[k]
    send[0, 4 * unit:4 * unit + 16, cols] = row


def get_unit(ctl, mine, got, cols, unit):
    theirs = decode(
        [got[0, k * unit:(k + 1) * unit, cols] for k in range(4)],
        got[0, 4 * unit:4 * unit + 16, cols],
    )
    ours = [mine[0, k, :, cols] for k in range(4)]
    behind = ctl[1] == 1
    front = [jnp.where(behind, t, o) for t, o in zip(theirs, ours)]
    back = [jnp.where(behind, o, t) for t, o in zip(theirs, ours)]
    return over(front, back)


def merge_kernel(ctl, mine, got, send, keep, *, groups, units, unit):
    i = pl.program_id(0)
    width = mine.shape[3]
    sending = i < (groups // 2) * units

    @pl.when(sending)
    def _():
        def put(at):
            cols = pl.ds(at, LANES)
            put_codes(send, get_unit(ctl, mine, got, cols, unit), cols, unit)

        each_strip(width, put)

    @pl.when(jnp.logical_not(sending))
    def _():
        def put(at):
            cols = pl.ds(at, LANES)
            merged = get_unit(ctl, mine, got, cols, unit)
            for k in range(4):
                keep[0, k, :, cols] = merged[k]

        each_strip(width, put)


def last_merge_kernel(ctl, mine, got, send, image, *, unit, blocks):
    width = mine.shape[3]

    def put(at):
        cols = pl.ds(at, LANES)
        merged = get_unit(ctl, mine, got, cols, unit)
        for k in range(4):
            image[k, :, cols] = merged[k]

    each_strip(width, put)
    part = width // blocks
    for b in range(blocks):
        wide = jnp.concatenate([image[k, :, b * part:(b + 1) * part] for k in range(4)], axis=1)
        codes, row = encode([wide])
        send[b, 0, 0:unit, :] = codes[0]
        send[b, 0, unit:unit + 16, :] = row


def compose_kernel(got, out, *, unit, blocks):
    part = out.shape[2]
    total = None
    for b in range(blocks):
        wide = decode([got[b, 0, 0:unit, :]], got[b, 0, unit:unit + 16, :])[0]
        layer = [wide[:, k * part:(k + 1) * part] for k in range(4)]
        total = layer if total is None else over(total, layer)
    for k in range(4):
        out[k] = total[k]


def params():
    return pltpu.CompilerParams(vmem_limit_bytes=VMEM_LIMIT, dimension_semantics=("arbitrary",))


def unit_index(groups, units, bit):
    half = (groups // 2) * units

    def index(i, ctl):
        rest = lax.rem(i, half)
        parity = jnp.where(i < half, 1 - ctl[bit], ctl[bit])
        return (2 * (rest // units) + parity) * units + lax.rem(rest, units)

    return index


def split_outputs(groups, units, unit, width):
    half = (groups // 2) * units
    shapes = [
        jax.ShapeDtypeStruct((half, 4 * unit + 16, width), jnp.int16),
        jax.ShapeDtypeStruct((half, 4, unit, width), jnp.float32),
    ]
    specs = [
        pl.BlockSpec((1, 4 * unit + 16, width), lambda i, ctl: (jnp.minimum(i, half - 1), 0, 0)),
        pl.BlockSpec((1, 4, unit, width), lambda i, ctl: (jnp.maximum(i - half, 0), 0, 0, 0)),
    ]
    return shapes, specs


def band(shape, dim, offset):
    place = lax.broadcasted_iota(jnp.int32, shape, dim) - lax.broadcasted_iota(jnp.int32, shape, 1 - dim) - offset
    return jnp.where(place == 1, 1.0, jnp.where(place == -1, -1.0, 0.0)).astype(jnp.bfloat16)


def render(ctl, light, table, field, before, after, *, groups, units, unit, rows, offset):
    layers, total, width = field.shape
    block = math.lcm(unit, 16)
    tall = padded_rows(unit)
    row_band = band((tall, tall + 32), 1, 16)
    column_band = band((3 * LANES, LANES), 0, LANES)
    half = (groups // 2) * units
    index = unit_index(groups, units, 0)

    def start(i, ctl):
        unit_at = index(i, ctl)
        return (unit_at // units) * rows + offset + lax.rem(unit_at, units) * unit

    def main_at(i, ctl):
        return (0, start(i, ctl) // block, 0)

    def above_at(i, ctl):
        return (0, jnp.maximum(start(i, ctl) - 1, 0) // 16, 0)

    def below_at(i, ctl):
        return (0, jnp.minimum(start(i, ctl) + unit, total - 1) // 16, 0)

    shapes, specs = split_outputs(groups, units, unit, width)
    kernel = functools.partial(
        render_kernel, groups=groups, units=units, unit=unit, block=block, rows=rows, offset=offset, total=total
    )
    cells = layers * 2 * half * unit * width
    return pl.pallas_call(
        kernel,
        grid_spec=pltpu.PrefetchScalarGridSpec(
            num_scalar_prefetch=1,
            grid=(2 * half,),
            in_specs=[
                pl.BlockSpec(memory_space=pltpu.SMEM),
                pl.BlockSpec((8, LANES), lambda i, ctl: (0, 0)),
                pl.BlockSpec((tall, tall + 32), lambda i, ctl: (0, 0)),
                pl.BlockSpec((3 * LANES, LANES), lambda i, ctl: (0, 0)),
                pl.BlockSpec((layers, block, width), main_at),
                pl.BlockSpec((layers, 16, width), above_at),
                pl.BlockSpec((layers, 16, width), below_at),
                pl.BlockSpec((1, unit, width), lambda i, ctl: (index(i, ctl), 0, 0)),
                pl.BlockSpec((1, unit, width), lambda i, ctl: (index(i, ctl), 0, 0)),
            ],
            out_specs=specs,
            scratch_shapes=[
                pltpu.VMEM((layers, tall + 32, width + 2 * LANES), jnp.bfloat16),
                pltpu.VMEM((4, tall, width), jnp.float32),
                pltpu.VMEM((max(block, tall + 32), width) if block != unit else (8, LANES), jnp.float32),
                pltpu.VMEM((2, tall, width) if block != unit else (1, 8, LANES), jnp.float32),
            ],
        ),
        out_shape=shapes,
        compiler_params=params(),
        cost_estimate=pl.CostEstimate(flops=50 * cells, bytes_accessed=6 * cells, transcendentals=cells),
        name="render",
    )(ctl, light, table, row_band, column_band, field, field, field, before, after)


def merge(ctl, mine, got, *, groups, units, unit):
    width = mine.shape[3]
    half = (groups // 2) * units
    index = unit_index(groups, units, 0)
    shapes, specs = split_outputs(groups, units, unit, width)
    cells = 4 * 2 * half * unit * width
    return pl.pallas_call(
        functools.partial(merge_kernel, groups=groups, units=units, unit=unit),
        grid_spec=pltpu.PrefetchScalarGridSpec(
            num_scalar_prefetch=1,
            grid=(2 * half,),
            in_specs=[
                pl.BlockSpec((1, 4, unit, width), lambda i, ctl: (index(i, ctl), 0, 0, 0)),
                pl.BlockSpec((1, 4 * unit + 16, width), lambda i, ctl: (index(i, ctl), 0, 0)),
            ],
            out_specs=specs,
        ),
        out_shape=shapes,
        compiler_params=params(),
        cost_estimate=pl.CostEstimate(flops=8 * cells, bytes_accessed=9 * cells, transcendentals=0),
        name="merge",
    )(ctl, mine, got)


def last_merge(ctl, mine, got, *, units, unit, blocks):
    width = mine.shape[3]
    cells = 4 * units * unit * width
    return pl.pallas_call(
        functools.partial(last_merge_kernel, unit=unit, blocks=blocks),
        grid_spec=pltpu.PrefetchScalarGridSpec(
            num_scalar_prefetch=1,
            grid=(units,),
            in_specs=[
                pl.BlockSpec((1, 4, unit, width), lambda i, ctl: (i, 0, 0, 0)),
                pl.BlockSpec((1, 4 * unit + 16, width), lambda i, ctl: (i, 0, 0)),
            ],
            out_specs=pl.BlockSpec((blocks, 1, unit + 16, 4 * width // blocks), lambda i, ctl: (0, i, 0, 0)),
            scratch_shapes=[pltpu.VMEM((4, unit, width), jnp.float32)],
        ),
        out_shape=jax.ShapeDtypeStruct((blocks, units, unit + 16, 4 * width // blocks), jnp.int16),
        compiler_params=params(),
        cost_estimate=pl.CostEstimate(flops=8 * cells, bytes_accessed=9 * cells, transcendentals=0),
        name="last_merge",
    )(ctl, mine, got)


def compose(got, *, unit):
    blocks, units = got.shape[:2]
    part = got.shape[3] // 4
    cells = 4 * units * unit * part * blocks
    return pl.pallas_call(
        functools.partial(compose_kernel, unit=unit, blocks=blocks),
        grid=(units,),
        in_specs=[pl.BlockSpec((blocks, 1, unit + 16, 4 * part), lambda i: (0, i, 0, 0))],
        out_specs=pl.BlockSpec((4, unit, part), lambda i: (0, i, 0)),
        out_shape=jax.ShapeDtypeStruct((4, units * unit, part), jnp.float32),
        compiler_params=params(),
        cost_estimate=pl.CostEstimate(flops=8 * cells, bytes_accessed=3 * cells, transcendentals=0),
        name="compose",
    )(got)


def chunk_units(units):
    return [1] * units


def per_device(field, transfer, bin_order, light_angles):
    tiles = lax.axis_size("tile")
    blocks = lax.axis_size("depth")
    devices = tiles * blocks
    layers, total, width = field.shape
    rows = total // tiles
    unit = unit_rows(rows)
    levels = tiles.bit_length() - 1

    table = jnp.take(transfer, bin_order, axis=1)
    table = table * jnp.array([[1.0], [1.0], [1.0], [0.01]], jnp.float32)
    bins = table.shape[1]
    slope = jnp.concatenate([table[:, 1:] - table[:, :-1], jnp.zeros_like(table[:, :1])], axis=1)
    table = jnp.pad(jnp.concatenate([table, slope], axis=0), ((0, 0), (0, LANES - bins)))
    azimuth, polar = light_angles[0], light_angles[1]
    light = 0.105 * jnp.stack(
        [jnp.cos(azimuth) * jnp.sin(polar), jnp.sin(azimuth) * jnp.sin(polar), jnp.cos(polar)]
    )

    tile = lax.axis_index("tile")
    bits = [((tile >> b) & 1).astype(jnp.int32) for b in range(levels)]
    controls = [jnp.stack([bits[min(b, levels - 1)], bits[max(b - 1, 0)]]) for b in range(levels + 1)]
    up = [(i, i + 1) for i in range(devices - 1)]
    down = [(j, i) for i, j in up]
    both = ("depth", "tile")
    first = field[0].reshape(tiles, rows, width)
    last = field[layers - 1].reshape(tiles, rows, width)

    sizes = chunk_units(rows // unit)
    count = len(sizes)
    starts = [sum(sizes[:n]) * unit for n in range(count)]
    halos = []
    for n, units in enumerate(sizes):
        def cut(layer):
            part = layer[:, starts[n]:starts[n] + units * unit]
            return part.reshape(tiles * units, unit, width)

        ends = (cut(last), cut(first))
        if n > 0:
            ends, _ = lax.optimization_barrier((ends, halos[n - 1]))
        halos.append((lax.ppermute(ends[0], both, up), lax.ppermute(ends[1], both, down)))

    def exchange(send, level):
        return lax.ppermute(send, "tile", [(i, i ^ (1 << level)) for i in range(tiles)])

    merged = []
    pieces = []
    for n, units in enumerate(sizes):
        control = controls[0]
        if n >= 2:
            control, _ = lax.optimization_barrier((control, merged[n - 2]))
        before, after = halos[n]
        send, keep = render(
            control, light, table, field, before, after,
            groups=tiles, units=units, unit=unit, rows=rows, offset=starts[n],
        )
        groups = tiles // 2
        got = exchange(send, 0)
        for level in range(1, levels):
            send, keep = merge(controls[level], keep, got, groups=groups, units=units, unit=unit)
            if level == 1:
                merged.append(send)
            groups //= 2
            got = exchange(send, level)
        blocked = last_merge(controls[levels], keep, got, units=units, unit=unit, blocks=blocks)
        blocked = lax.all_to_all(blocked, "depth", split_axis=0, concat_axis=0, tiled=True)
        pieces.append(compose(blocked, unit=unit))
    return jnp.concatenate(pieces, axis=1) if count > 1 else pieces[0]


def solution(mesh):
    in_specs = (P(("depth", "tile"), None, None), P(), P(), P())
    out_specs = P(None, "tile", "depth")
    return jax.shard_map(
        per_device, mesh=mesh, in_specs=in_specs, out_specs=out_specs, check_vma=False
    )
```

```python
import functools
import math

import jax
import jax.numpy as jnp
from jax import lax
from jax.experimental import pallas as pl
from jax.experimental.pallas import tpu as pltpu
from jax.sharding import PartitionSpec as P

LANES = 128
CODES = 32700.0
VMEM_LIMIT = 56 * 1024 * 1024


def unit_rows(rows):
    return 48 if rows % 48 == 0 else rows


def encode(values):
    top = functools.reduce(jnp.maximum, values)
    top = jnp.max(top, axis=0, keepdims=True)
    exponent = jnp.ceil(jnp.log2(jnp.maximum(top, 1e-30)))
    factor = jnp.exp2(-exponent) * CODES
    codes = [(v * factor + 0.5).astype(jnp.int32).astype(jnp.int16) for v in values]
    row = jnp.broadcast_to(exponent, (16, exponent.shape[1]))
    return codes, row.astype(jnp.int32).astype(jnp.int16)


def decode(codes, row):
    exponent = row.astype(jnp.int32).astype(jnp.float32)[0:1]
    scale = jnp.exp2(exponent) * (1.0 / CODES)
    return [c.astype(jnp.int32).astype(jnp.float32) * scale for c in codes]


def over(front, back):
    clear = 1.0 - front[3]
    return [f + clear * b for f, b in zip(front, back)]


def choose(bins, whole):
    place = whole.astype(jnp.bfloat16)
    one, zero = jnp.ones_like(place), jnp.zeros_like(place)
    return jnp.concatenate([jnp.where(place == k, one, zero) for k in range(bins)], axis=0)


def padded_rows(unit):
    return -(-unit // 16) * 16


def each_strip(width, body):
    strips = width // LANES
    together = 3 if strips % 3 == 0 else 1

    def step(c, carry):
        for k in range(together):
            body(pl.multiple_of((c * together + k) * LANES, LANES))
        return carry

    lax.fori_loop(0, strips // together, step, 0)


def render_kernel(ctl, light, table, row_band, column_band, main, above, below, before, after, send, keep, cells, image, stage, ends, *, groups, units, unit, block, rows, offset, total):
    i = pl.program_id(0)
    half = (groups // 2) * units
    rest = lax.rem(i, half)
    sending = i < half
    parity = jnp.where(sending, 1 - ctl[0], ctl[0])
    group = 2 * (rest // units) + parity
    start = group * rows + offset + lax.rem(rest, units) * unit
    layers = main.shape[0]
    width = main.shape[2]
    tall = padded_rows(unit)
    aligned = block == unit
    inner = slice(LANES, LANES + width)

    @pl.when(i == 0)
    def _():
        cells[:, :, 0:LANES] = jnp.zeros((layers, tall + 32, LANES), jnp.bfloat16)
        cells[:, :, LANES + width:] = jnp.zeros((layers, tall + 32, LANES), jnp.bfloat16)

    def load_layer(layer, carry):
        up = above[layer].astype(jnp.float32)
        down = below[layer].astype(jnp.float32)
        up = jnp.where(start > 0, up, 0.0)
        down = jnp.where(start + unit < total, down, 0.0)
        if aligned:
            cells[layer, 0:16, inner] = up.astype(jnp.bfloat16)
            cells[layer, 16:16 + unit, inner] = main[layer]
            cells[layer, 16 + unit:32 + unit, inner] = down.astype(jnp.bfloat16)
        else:
            shift = pl.multiple_of(lax.rem(start, block), 8)
            stage[0:block, :] = main[layer].astype(jnp.float32)
            body = stage[pl.ds(shift, unit), :]
            up = jnp.where(lax.rem(start, 16) == 0, up[8:16], up[0:8])
            down = jnp.where(lax.rem(start + unit, 16) == 0, down[0:8], down[8:16])
            stage[0:8, :] = jnp.zeros((8, width), jnp.float32)
            stage[8:16, :] = up
            stage[16:16 + unit, :] = body
            stage[16 + unit:24 + unit, :] = down
            stage[24 + unit:tall + 32, :] = jnp.zeros((tall + 8 - unit, width), jnp.float32)
            cells[layer, :, inner] = stage[0:tall + 32, :].astype(jnp.bfloat16)
        return carry

    lax.fori_loop(0, layers, load_layer, 0)
    if not aligned:
        ends[0, 0:unit, :] = before[0].astype(jnp.float32)
        ends[1, 0:unit, :] = after[0].astype(jnp.float32)

    lx, ly, lz = light[0], light[1], light[2]
    step = 16
    bins = table.shape[1] // (2 * step)

    def strip(c, carry):
        at = pl.multiple_of(c * LANES, LANES)
        cols = pl.ds(at, LANES)
        shifted = pl.ds(pl.multiple_of(at + LANES, LANES), LANES)
        window = pl.ds(at, 3 * LANES)
        spans = [slice(r, r + step) for r in range(0, tall, step)]
        inside = [slice(16 + r, 16 + r + step) for r in range(0, tall, step)]
        if aligned:
            low = [before[0, s, cols].astype(jnp.float32) for s in spans]
            far = [after[0, s, cols].astype(jnp.float32) for s in spans]
        else:
            low = [ends[0, s, cols] for s in spans]
            far = [ends[1, s, cols] for s in spans]
        here = [cells[0, s, shifted].astype(jnp.float32) for s in inside]
        clear = [None] * len(spans)
        colour = [None] * len(spans)
        for first in range(0, layers, 2):
            pair = range(first, min(first + 2, layers))
            slope_y = [jnp.dot(row_band[...], cells[l, :, shifted], preferred_element_type=jnp.float32) for l in pair]
            slope_z = [jnp.dot(cells[l, 16:16 + tall, window], column_band[...], preferred_element_type=jnp.float32) for l in pair]
            for n, s in enumerate(spans):
                parts, picks, shades = [], [], []
                for m, layer in enumerate(pair):
                    if layer + 1 < layers:
                        high = cells[layer + 1, inside[n], shifted].astype(jnp.float32)
                    else:
                        high = far[n]
                    position = jnp.clip(here[n] * 2.5 + 7.5, 0.0, 15.0)
                    whole = jnp.floor(position)
                    parts.append(position - whole)
                    picks.append(choose(bins, whole))
                    gx = high - low[n]
                    gy = slope_y[m][s]
                    gz = slope_z[m][s]
                    facing = jnp.abs(gx * lx + gy * ly + gz * lz)
                    square = gx * gx + gy * gy + gz * gz
                    shades.append(0.045 + facing * lax.rsqrt(jnp.maximum(square, 4.0)))
                    low[n], here[n] = here[n], high
                pick = jnp.concatenate(picks, axis=1) if len(picks) > 1 else picks[0]
                found = jnp.dot(table[...], jnp.concatenate([pick, pick], axis=0), preferred_element_type=jnp.float32)
                for m, layer in enumerate(pair):
                    lanes = slice(m * LANES, (m + 1) * LANES)
                    tf = [
                        found[k * step:(k + 1) * step, lanes] + parts[m] * found[(4 + k) * step:(5 + k) * step, lanes]
                        for k in range(4)
                    ]
                    shade = shades[m]
                    if layer == 0:
                        colour[n] = [tf[k] * shade for k in range(3)]
                        clear[n] = 1.0 - tf[3]
                    else:
                        seen = shade * clear[n]
                        colour[n] = [colour[n][k] + tf[k] * seen for k in range(3)]
                        clear[n] = clear[n] - clear[n] * tf[3]
        for n, s in enumerate(spans):
            for k in range(3):
                image[k, s, cols] = colour[n][k]
            image[3, s, cols] = 1.0 - clear[n]
        return carry

    lax.fori_loop(0, width // LANES, strip, 0)

    @pl.when(sending)
    def _():
        def put(at):
            cols = pl.ds(at, LANES)
            put_codes(send, [image[k, 0:unit, cols] for k in range(4)], cols, unit)

        each_strip(width, put)

    @pl.when(jnp.logical_not(sending))
    def _():
        keep[0] = image[:, 0:unit, :]


def put_codes(send, values, cols, unit):
    codes, row = encode(values)
    for k in range(4):
        send[0, k * unit:(k + 1) * unit, cols] = codes[k]
    send[0, 4 * unit:4 * unit + 16, cols] = row


def get_unit(ctl, mine, got, cols, unit):
    theirs = decode(
        [got[0, k * unit:(k + 1) * unit, cols] for k in range(4)],
        got[0, 4 * unit:4 * unit + 16, cols],
    )
    ours = [mine[0, k, :, cols] for k in range(4)]
    behind = ctl[1] == 1
    front = [jnp.where(behind, t, o) for t, o in zip(theirs, ours)]
    back = [jnp.where(behind, o, t) for t, o in zip(theirs, ours)]
    return over(front, back)


def merge_kernel(ctl, mine, got, send, keep, *, groups, units, unit):
    i = pl.program_id(0)
    width = mine.shape[3]
    sending = i < (groups // 2) * units

    @pl.when(sending)
    def _():
        def put(at):
            cols = pl.ds(at, LANES)
            put_codes(send, get_unit(ctl, mine, got, cols, unit), cols, unit)

        each_strip(width, put)

    @pl.when(jnp.logical_not(sending))
    def _():
        def put(at):
            cols = pl.ds(at, LANES)
            merged = get_unit(ctl, mine, got, cols, unit)
            for k in range(4):
                keep[0, k, :, cols] = merged[k]

        each_strip(width, put)


def last_merge_kernel(ctl, mine, got, send, image, *, unit, blocks):
    width = mine.shape[3]

    def put(at):
        cols = pl.ds(at, LANES)
        merged = get_unit(ctl, mine, got, cols, unit)
        for k in range(4):
            image[k, :, cols] = merged[k]

    each_strip(width, put)
    part = width // blocks
    for b in range(blocks):
        wide = jnp.concatenate([image[k, :, b * part:(b + 1) * part] for k in range(4)], axis=1)
        codes, row = encode([wide])
        send[b, 0, 0:unit, :] = codes[0]
        send[b, 0, unit:unit + 16, :] = row


def compose_kernel(got, out, *, unit, blocks):
    part = out.shape[2]
    total = None
    for b in range(blocks):
        wide = decode([got[b, 0, 0:unit, :]], got[b, 0, unit:unit + 16, :])[0]
        layer = [wide[:, k * part:(k + 1) * part] for k in range(4)]
        total = layer if total is None else over(total, layer)
    for k in range(4):
        out[k] = total[k]


def params():
    return pltpu.CompilerParams(vmem_limit_bytes=VMEM_LIMIT, dimension_semantics=("arbitrary",))


def unit_index(groups, units, bit):
    half = (groups // 2) * units

    def index(i, ctl):
        rest = lax.rem(i, half)
        parity = jnp.where(i < half, 1 - ctl[bit], ctl[bit])
        return (2 * (rest // units) + parity) * units + lax.rem(rest, units)

    return index


def split_outputs(groups, units, unit, width):
    half = (groups // 2) * units
    shapes = [
        jax.ShapeDtypeStruct((half, 4 * unit + 16, width), jnp.int16),
        jax.ShapeDtypeStruct((half, 4, unit, width), jnp.float32),
    ]
    specs = [
        pl.BlockSpec((1, 4 * unit + 16, width), lambda i, ctl: (jnp.minimum(i, half - 1), 0, 0)),
        pl.BlockSpec((1, 4, unit, width), lambda i, ctl: (jnp.maximum(i - half, 0), 0, 0, 0)),
    ]
    return shapes, specs


def band(shape, dim, offset):
    place = lax.broadcasted_iota(jnp.int32, shape, dim) - lax.broadcasted_iota(jnp.int32, shape, 1 - dim) - offset
    return jnp.where(place == 1, 1.0, jnp.where(place == -1, -1.0, 0.0)).astype(jnp.bfloat16)


def render(ctl, light, table, field, before, after, *, groups, units, unit, rows, offset):
    layers, total, width = field.shape
    block = math.lcm(unit, 16)
    tall = padded_rows(unit)
    row_band = band((tall, tall + 32), 1, 16)
    column_band = band((3 * LANES, LANES), 0, LANES)
    half = (groups // 2) * units
    index = unit_index(groups, units, 0)

    def start(i, ctl):
        unit_at = index(i, ctl)
        return (unit_at // units) * rows + offset + lax.rem(unit_at, units) * unit

    def main_at(i, ctl):
        return (0, start(i, ctl) // block, 0)

    def above_at(i, ctl):
        return (0, jnp.maximum(start(i, ctl) - 1, 0) // 16, 0)

    def below_at(i, ctl):
        return (0, jnp.minimum(start(i, ctl) + unit, total - 1) // 16, 0)

    shapes, specs = split_outputs(groups, units, unit, width)
    kernel = functools.partial(
        render_kernel, groups=groups, units=units, unit=unit, block=block, rows=rows, offset=offset, total=total
    )
    cells = layers * 2 * half * unit * width
    return pl.pallas_call(
        kernel,
        grid_spec=pltpu.PrefetchScalarGridSpec(
            num_scalar_prefetch=1,
            grid=(2 * half,),
            in_specs=[
                pl.BlockSpec(memory_space=pltpu.SMEM),
                pl.BlockSpec(table.shape, lambda i, ctl: (0, 0)),
                pl.BlockSpec((tall, tall + 32), lambda i, ctl: (0, 0)),
                pl.BlockSpec((3 * LANES, LANES), lambda i, ctl: (0, 0)),
                pl.BlockSpec((layers, block, width), main_at),
                pl.BlockSpec((layers, 16, width), above_at),
                pl.BlockSpec((layers, 16, width), below_at),
                pl.BlockSpec((1, unit, width), lambda i, ctl: (index(i, ctl), 0, 0)),
                pl.BlockSpec((1, unit, width), lambda i, ctl: (index(i, ctl), 0, 0)),
            ],
            out_specs=specs,
            scratch_shapes=[
                pltpu.VMEM((layers, tall + 32, width + 2 * LANES), jnp.bfloat16),
                pltpu.VMEM((4, tall, width), jnp.float32),
                pltpu.VMEM((max(block, tall + 32), width) if block != unit else (8, LANES), jnp.float32),
                pltpu.VMEM((2, tall, width) if block != unit else (1, 8, LANES), jnp.float32),
            ],
        ),
        out_shape=shapes,
        compiler_params=params(),
        cost_estimate=pl.CostEstimate(flops=16384 * cells, bytes_accessed=6 * cells, transcendentals=cells),
        name="render",
    )(ctl, light, table, row_band, column_band, field, field, field, before, after)


def merge(ctl, mine, got, *, groups, units, unit):
    width = mine.shape[3]
    half = (groups // 2) * units
    index = unit_index(groups, units, 0)
    shapes, specs = split_outputs(groups, units, unit, width)
    cells = 4 * 2 * half * unit * width
    return pl.pallas_call(
        functools.partial(merge_kernel, groups=groups, units=units, unit=unit),
        grid_spec=pltpu.PrefetchScalarGridSpec(
            num_scalar_prefetch=1,
            grid=(2 * half,),
            in_specs=[
                pl.BlockSpec((1, 4, unit, width), lambda i, ctl: (index(i, ctl), 0, 0, 0)),
                pl.BlockSpec((1, 4 * unit + 16, width), lambda i, ctl: (index(i, ctl), 0, 0)),
            ],
            out_specs=specs,
        ),
        out_shape=shapes,
        compiler_params=params(),
        cost_estimate=pl.CostEstimate(flops=8 * cells, bytes_accessed=9 * cells, transcendentals=0),
        name="merge",
    )(ctl, mine, got)


def last_merge(ctl, mine, got, *, units, unit, blocks):
    width = mine.shape[3]
    cells = 4 * units * unit * width
    return pl.pallas_call(
        functools.partial(last_merge_kernel, unit=unit, blocks=blocks),
        grid_spec=pltpu.PrefetchScalarGridSpec(
            num_scalar_prefetch=1,
            grid=(units,),
            in_specs=[
                pl.BlockSpec((1, 4, unit, width), lambda i, ctl: (i, 0, 0, 0)),
                pl.BlockSpec((1, 4 * unit + 16, width), lambda i, ctl: (i, 0, 0)),
            ],
            out_specs=pl.BlockSpec((blocks, 1, unit + 16, 4 * width // blocks), lambda i, ctl: (0, i, 0, 0)),
            scratch_shapes=[pltpu.VMEM((4, unit, width), jnp.float32)],
        ),
        out_shape=jax.ShapeDtypeStruct((blocks, units, unit + 16, 4 * width // blocks), jnp.int16),
        compiler_params=params(),
        cost_estimate=pl.CostEstimate(flops=8 * cells, bytes_accessed=9 * cells, transcendentals=0),
        name="last_merge",
    )(ctl, mine, got)


def compose(got, *, unit):
    blocks, units = got.shape[:2]
    part = got.shape[3] // 4
    cells = 4 * units * unit * part * blocks
    return pl.pallas_call(
        functools.partial(compose_kernel, unit=unit, blocks=blocks),
        grid=(units,),
        in_specs=[pl.BlockSpec((blocks, 1, unit + 16, 4 * part), lambda i: (0, i, 0, 0))],
        out_specs=pl.BlockSpec((4, unit, part), lambda i: (0, i, 0)),
        out_shape=jax.ShapeDtypeStruct((4, units * unit, part), jnp.float32),
        compiler_params=params(),
        cost_estimate=pl.CostEstimate(flops=8 * cells, bytes_accessed=3 * cells, transcendentals=0),
        name="compose",
    )(got)


def chunk_units(units):
    return [1] * units


def per_device(field, transfer, bin_order, light_angles):
    tiles = lax.axis_size("tile")
    blocks = lax.axis_size("depth")
    devices = tiles * blocks
    layers, total, width = field.shape
    rows = total // tiles
    unit = unit_rows(rows)
    levels = tiles.bit_length() - 1

    table = jnp.take(transfer, bin_order, axis=1)
    table = table * jnp.array([[1.0], [1.0], [1.0], [0.01]], jnp.float32)
    bins = table.shape[1]
    slope = jnp.concatenate([table[:, 1:] - table[:, :-1], jnp.zeros_like(table[:, :1])], axis=1)
    table = jnp.concatenate([table, slope], axis=0)
    spread = jnp.eye(16, dtype=jnp.float32)
    table = (table[:, None, :, None] * spread[None, :, None, :]).reshape(8 * 16, bins * 16)
    coarse = lax.reduce_precision(table, exponent_bits=8, mantissa_bits=7)
    table = jnp.concatenate([coarse, table - coarse], axis=1).astype(jnp.bfloat16)
    azimuth, polar = light_angles[0], light_angles[1]
    light = 0.105 * jnp.stack(
        [jnp.cos(azimuth) * jnp.sin(polar), jnp.sin(azimuth) * jnp.sin(polar), jnp.cos(polar)]
    )

    tile = lax.axis_index("tile")
    bits = [((tile >> b) & 1).astype(jnp.int32) for b in range(levels)]
    controls = [jnp.stack([bits[min(b, levels - 1)], bits[max(b - 1, 0)]]) for b in range(levels + 1)]
    up = [(i, i + 1) for i in range(devices - 1)]
    down = [(j, i) for i, j in up]
    both = ("depth", "tile")
    first = field[0].reshape(tiles, rows, width)
    last = field[layers - 1].reshape(tiles, rows, width)

    sizes = chunk_units(rows // unit)
    count = len(sizes)
    starts = [sum(sizes[:n]) * unit for n in range(count)]
    halos = []
    for n, units in enumerate(sizes):
        def cut(layer):
            part = layer[:, starts[n]:starts[n] + units * unit]
            return part.reshape(tiles * units, unit, width)

        ends = (cut(last), cut(first))
        if n > 0:
            ends, _ = lax.optimization_barrier((ends, halos[n - 1]))
        halos.append((lax.ppermute(ends[0], both, up), lax.ppermute(ends[1], both, down)))

    def exchange(send, level):
        return lax.ppermute(send, "tile", [(i, i ^ (1 << level)) for i in range(tiles)])

    merged = []
    pieces = []
    for n, units in enumerate(sizes):
        control = controls[0]
        if n >= 2:
            control, _ = lax.optimization_barrier((control, merged[n - 2]))
        before, after = halos[n]
        send, keep = render(
            control, light, table, field, before, after,
            groups=tiles, units=units, unit=unit, rows=rows, offset=starts[n],
        )
        groups = tiles // 2
        got = exchange(send, 0)
        for level in range(1, levels):
            send, keep = merge(controls[level], keep, got, groups=groups, units=units, unit=unit)
            if level == 1:
                merged.append(send)
            groups //= 2
            got = exchange(send, level)
        blocked = last_merge(controls[levels], keep, got, units=units, unit=unit, blocks=blocks)
        blocked = lax.all_to_all(blocked, "depth", split_axis=0, concat_axis=0, tiled=True)
        pieces.append(compose(blocked, unit=unit))
    return jnp.concatenate(pieces, axis=1) if count > 1 else pieces[0]


def solution(mesh):
    in_specs = (P(("depth", "tile"), None, None), P(), P(), P())
    out_specs = P(None, "tile", "depth")
    return jax.shard_map(
        per_device, mesh=mesh, in_specs=in_specs, out_specs=out_specs, check_vma=False
    )
```

```python
import functools
import math

import jax
import jax.numpy as jnp
from jax import lax
from jax.experimental import pallas as pl
from jax.experimental.pallas import tpu as pltpu
from jax.sharding import PartitionSpec as P

LANES = 128
CODES = 32700.0
VMEM_LIMIT = 56 * 1024 * 1024


def unit_rows(rows):
    return 48 if rows % 48 == 0 else rows


def encode(values):
    top = functools.reduce(jnp.maximum, values)
    top = jnp.max(top, axis=0, keepdims=True)
    exponent = jnp.ceil(jnp.log2(jnp.maximum(top, 1e-30)))
    factor = jnp.exp2(-exponent) * CODES
    codes = [(v * factor + 0.5).astype(jnp.int32).astype(jnp.int16) for v in values]
    row = jnp.broadcast_to(exponent, (16, exponent.shape[1]))
    return codes, row.astype(jnp.int32).astype(jnp.int16)


def decode(codes, row):
    exponent = row.astype(jnp.int32).astype(jnp.float32)[0:1]
    scale = jnp.exp2(exponent) * (1.0 / CODES)
    return [c.astype(jnp.int32).astype(jnp.float32) * scale for c in codes]


def over(front, back):
    clear = 1.0 - front[3]
    return [f + clear * b for f, b in zip(front, back)]


def lookup(table, index):
    numbers = lax.GatherDimensionNumbers(
        offset_dims=(), collapsed_slice_dims=(1,), start_index_map=(1,),
        operand_batching_dims=(0,), start_indices_batching_dims=(0,),
    )
    return lax.gather(
        table, index[..., None], numbers, slice_sizes=(1, 1), mode=lax.GatherScatterMode.PROMISE_IN_BOUNDS
    )


def choose(bins, whole):
    place = whole.astype(jnp.bfloat16)
    one, zero = jnp.ones_like(place), jnp.zeros_like(place)
    return jnp.concatenate([jnp.where(place == k, one, zero) for k in range(bins)], axis=0)


def padded_rows(unit):
    return -(-unit // 16) * 16


def each_strip(width, body):
    strips = width // LANES
    together = 3 if strips % 3 == 0 else 1

    def step(c, carry):
        for k in range(together):
            body(pl.multiple_of((c * together + k) * LANES, LANES))
        return carry

    lax.fori_loop(0, strips // together, step, 0)


def render_kernel(ctl, light, table, slope, row_band, column_band, main, above, below, before, after, send, keep, cells, image, stage, ends, *, groups, units, unit, block, rows, offset, total):
    i = pl.program_id(0)
    half = (groups // 2) * units
    rest = lax.rem(i, half)
    sending = i < half
    parity = jnp.where(sending, 1 - ctl[0], ctl[0])
    group = 2 * (rest // units) + parity
    start = group * rows + offset + lax.rem(rest, units) * unit
    layers = main.shape[0]
    width = main.shape[2]
    tall = padded_rows(unit)
    aligned = block == unit
    inner = slice(LANES, LANES + width)

    @pl.when(i == 0)
    def _():
        cells[:, :, 0:LANES] = jnp.zeros((layers, tall + 32, LANES), jnp.bfloat16)
        cells[:, :, LANES + width:] = jnp.zeros((layers, tall + 32, LANES), jnp.bfloat16)

    def load_layer(layer, carry):
        up = above[layer].astype(jnp.float32)
        down = below[layer].astype(jnp.float32)
        up = jnp.where(start > 0, up, 0.0)
        down = jnp.where(start + unit < total, down, 0.0)
        if aligned:
            cells[layer, 0:16, inner] = up.astype(jnp.bfloat16)
            cells[layer, 16:16 + unit, inner] = main[layer]
            cells[layer, 16 + unit:32 + unit, inner] = down.astype(jnp.bfloat16)
        else:
            shift = pl.multiple_of(lax.rem(start, block), 8)
            stage[0:block, :] = main[layer].astype(jnp.float32)
            body = stage[pl.ds(shift, unit), :]
            up = jnp.where(lax.rem(start, 16) == 0, up[8:16], up[0:8])
            down = jnp.where(lax.rem(start + unit, 16) == 0, down[0:8], down[8:16])
            stage[0:8, :] = jnp.zeros((8, width), jnp.float32)
            stage[8:16, :] = up
            stage[16:16 + unit, :] = body
            stage[16 + unit:24 + unit, :] = down
            stage[24 + unit:tall + 32, :] = jnp.zeros((tall + 8 - unit, width), jnp.float32)
            cells[layer, :, inner] = stage[0:tall + 32, :].astype(jnp.bfloat16)
        return carry

    lax.fori_loop(0, layers, load_layer, 0)
    if not aligned:
        ends[0, 0:unit, :] = before[0].astype(jnp.float32)
        ends[1, 0:unit, :] = after[0].astype(jnp.float32)

    lx, ly, lz = light[0], light[1], light[2]
    step = 16
    bins = table.shape[1] // step
    slopes = [jnp.broadcast_to(slope[k:k + 1, :], (step, LANES)) for k in range(4)]

    def strip(c, carry):
        at = pl.multiple_of(c * LANES, LANES)
        cols = pl.ds(at, LANES)
        shifted = pl.ds(pl.multiple_of(at + LANES, LANES), LANES)
        window = pl.ds(at, 3 * LANES)
        spans = [slice(r, r + step) for r in range(0, tall, step)]
        inside = [slice(16 + r, 16 + r + step) for r in range(0, tall, step)]
        if aligned:
            low = [before[0, s, cols].astype(jnp.float32) for s in spans]
            far = [after[0, s, cols].astype(jnp.float32) for s in spans]
        else:
            low = [ends[0, s, cols] for s in spans]
            far = [ends[1, s, cols] for s in spans]
        here = [cells[0, s, shifted].astype(jnp.float32) for s in inside]
        clear = [None] * len(spans)
        colour = [None] * len(spans)
        for first in range(0, layers, 2):
            pair = range(first, min(first + 2, layers))
            slope_y = [jnp.dot(row_band[...], cells[l, :, shifted], preferred_element_type=jnp.float32) for l in pair]
            slope_z = [jnp.dot(cells[l, 16:16 + tall, window], column_band[...], preferred_element_type=jnp.float32) for l in pair]
            for n, s in enumerate(spans):
                parts, picks, shades, tilts = [], [], [], []
                for m, layer in enumerate(pair):
                    if layer + 1 < layers:
                        high = cells[layer + 1, inside[n], shifted].astype(jnp.float32)
                    else:
                        high = far[n]
                    position = jnp.clip(here[n] * 2.5 + 7.5, 0.0, 15.0)
                    index = position.astype(jnp.int32)
                    whole = index.astype(jnp.float32)
                    parts.append(position - whole)
                    tilts.append([lookup(slopes[k], index) for k in range(4)])
                    picks.append(choose(bins, whole))
                    gx = high - low[n]
                    gy = slope_y[m][s]
                    gz = slope_z[m][s]
                    facing = jnp.abs(gx * lx + gy * ly + gz * lz)
                    square = gx * gx + gy * gy + gz * gz
                    shades.append(0.045 + facing * lax.rsqrt(jnp.maximum(square, 4.0)))
                    low[n], here[n] = here[n], high
                pick = jnp.concatenate(picks, axis=1) if len(picks) > 1 else picks[0]
                found = jnp.dot(table[...], pick, preferred_element_type=jnp.float32)
                for m, layer in enumerate(pair):
                    lanes = slice(m * LANES, (m + 1) * LANES)
                    tf = [
                        found[k * step:(k + 1) * step, lanes]
                        + found[(4 + k) * step:(5 + k) * step, lanes]
                        + parts[m] * tilts[m][k]
                        for k in range(4)
                    ]
                    shade = shades[m]
                    if layer == 0:
                        colour[n] = [tf[k] * shade for k in range(3)]
                        clear[n] = 1.0 - tf[3]
                    else:
                        seen = shade * clear[n]
                        colour[n] = [colour[n][k] + tf[k] * seen for k in range(3)]
                        clear[n] = clear[n] - clear[n] * tf[3]
        for n, s in enumerate(spans):
            for k in range(3):
                image[k, s, cols] = colour[n][k]
            image[3, s, cols] = 1.0 - clear[n]
        return carry

    lax.fori_loop(0, width // LANES, strip, 0)

    @pl.when(sending)
    def _():
        def put(at):
            cols = pl.ds(at, LANES)
            put_codes(send, [image[k, 0:unit, cols] for k in range(4)], cols, unit)

        each_strip(width, put)

    @pl.when(jnp.logical_not(sending))
    def _():
        keep[0] = image[:, 0:unit, :]


def put_codes(send, values, cols, unit):
    codes, row = encode(values)
    for k in range(4):
        send[0, k * unit:(k + 1) * unit, cols] = codes[k]
    send[0, 4 * unit:4 * unit + 16, cols] = row


def get_unit(ctl, mine, got, cols, unit):
    theirs = decode(
        [got[0, k * unit:(k + 1) * unit, cols] for k in range(4)],
        got[0, 4 * unit:4 * unit + 16, cols],
    )
    ours = [mine[0, k, :, cols] for k in range(4)]
    behind = ctl[1] == 1
    front = [jnp.where(behind, t, o) for t, o in zip(theirs, ours)]
    back = [jnp.where(behind, o, t) for t, o in zip(theirs, ours)]
    return over(front, back)


def merge_kernel(ctl, mine, got, send, keep, *, groups, units, unit):
    i = pl.program_id(0)
    width = mine.shape[3]
    sending = i < (groups // 2) * units

    @pl.when(sending)
    def _():
        def put(at):
            cols = pl.ds(at, LANES)
            put_codes(send, get_unit(ctl, mine, got, cols, unit), cols, unit)

        each_strip(width, put)

    @pl.when(jnp.logical_not(sending))
    def _():
        def put(at):
            cols = pl.ds(at, LANES)
            merged = get_unit(ctl, mine, got, cols, unit)
            for k in range(4):
                keep[0, k, :, cols] = merged[k]

        each_strip(width, put)


def last_merge_kernel(ctl, mine, got, send, image, *, unit, blocks):
    width = mine.shape[3]

    def put(at):
        cols = pl.ds(at, LANES)
        merged = get_unit(ctl, mine, got, cols, unit)
        for k in range(4):
            image[k, :, cols] = merged[k]

    each_strip(width, put)
    part = width // blocks
    for b in range(blocks):
        wide = jnp.concatenate([image[k, :, b * part:(b + 1) * part] for k in range(4)], axis=1)
        codes, row = encode([wide])
        send[b, 0, 0:unit, :] = codes[0]
        send[b, 0, unit:unit + 16, :] = row


def compose_kernel(got, *refs, unit, blocks):
    out = refs[-1]
    part = out.shape[2]
    total = None
    for b in range(blocks):
        wide = decode([got[b, 0, 0:unit, :]], got[b, 0, unit:unit + 16, :])[0]
        layer = [wide[:, k * part:(k + 1) * part] for k in range(4)]
        total = layer if total is None else over(total, layer)
    for k in range(4):
        out[k] = total[k]


def params():
    return pltpu.CompilerParams(vmem_limit_bytes=VMEM_LIMIT, dimension_semantics=("arbitrary",))


def unit_index(groups, units, bit):
    half = (groups // 2) * units

    def index(i, ctl):
        rest = lax.rem(i, half)
        parity = jnp.where(i < half, 1 - ctl[bit], ctl[bit])
        return (2 * (rest // units) + parity) * units + lax.rem(rest, units)

    return index


def split_outputs(groups, units, unit, width):
    half = (groups // 2) * units
    shapes = [
        jax.ShapeDtypeStruct((half, 4 * unit + 16, width), jnp.int16),
        jax.ShapeDtypeStruct((half, 4, unit, width), jnp.float32),
    ]
    specs = [
        pl.BlockSpec((1, 4 * unit + 16, width), lambda i, ctl: (jnp.minimum(i, half - 1), 0, 0)),
        pl.BlockSpec((1, 4, unit, width), lambda i, ctl: (jnp.maximum(i - half, 0), 0, 0, 0)),
    ]
    return shapes, specs


def band(shape, dim, offset):
    place = lax.broadcasted_iota(jnp.int32, shape, dim) - lax.broadcasted_iota(jnp.int32, shape, 1 - dim) - offset
    return jnp.where(place == 1, 1.0, jnp.where(place == -1, -1.0, 0.0)).astype(jnp.bfloat16)


def render(ctl, light, table, slope, field, before, after, *, groups, units, unit, rows, offset):
    layers, total, width = field.shape
    block = math.lcm(unit, 16)
    tall = padded_rows(unit)
    row_band = band((tall, tall + 32), 1, 16)
    column_band = band((3 * LANES, LANES), 0, LANES)
    half = (groups // 2) * units
    index = unit_index(groups, units, 0)

    def start(i, ctl):
        unit_at = index(i, ctl)
        return (unit_at // units) * rows + offset + lax.rem(unit_at, units) * unit

    def main_at(i, ctl):
        return (0, start(i, ctl) // block, 0)

    def above_at(i, ctl):
        return (0, jnp.maximum(start(i, ctl) - 1, 0) // 16, 0)

    def below_at(i, ctl):
        return (0, jnp.minimum(start(i, ctl) + unit, total - 1) // 16, 0)

    shapes, specs = split_outputs(groups, units, unit, width)
    kernel = functools.partial(
        render_kernel, groups=groups, units=units, unit=unit, block=block, rows=rows, offset=offset, total=total
    )
    cells = layers * 2 * half * unit * width
    return pl.pallas_call(
        kernel,
        grid_spec=pltpu.PrefetchScalarGridSpec(
            num_scalar_prefetch=1,
            grid=(2 * half,),
            in_specs=[
                pl.BlockSpec(memory_space=pltpu.SMEM),
                pl.BlockSpec(table.shape, lambda i, ctl: (0, 0)),
                pl.BlockSpec(slope.shape, lambda i, ctl: (0, 0)),
                pl.BlockSpec((tall, tall + 32), lambda i, ctl: (0, 0)),
                pl.BlockSpec((3 * LANES, LANES), lambda i, ctl: (0, 0)),
                pl.BlockSpec((layers, block, width), main_at),
                pl.BlockSpec((layers, 16, width), above_at),
                pl.BlockSpec((layers, 16, width), below_at),
                pl.BlockSpec((1, unit, width), lambda i, ctl: (index(i, ctl), 0, 0)),
                pl.BlockSpec((1, unit, width), lambda i, ctl: (index(i, ctl), 0, 0)),
            ],
            out_specs=specs,
            scratch_shapes=[
                pltpu.VMEM((layers, tall + 32, width + 2 * LANES), jnp.bfloat16),
                pltpu.VMEM((4, tall, width), jnp.float32),
                pltpu.VMEM((max(block, tall + 32), width) if block != unit else (8, LANES), jnp.float32),
                pltpu.VMEM((2, tall, width) if block != unit else (1, 8, LANES), jnp.float32),
            ],
        ),
        out_shape=shapes,
        compiler_params=params(),
        cost_estimate=pl.CostEstimate(flops=16384 * cells, bytes_accessed=6 * cells, transcendentals=cells),
        name="render",
    )(ctl, light, table, slope, row_band, column_band, field, field, field, before, after)


def merge(ctl, mine, got, *, groups, units, unit):
    width = mine.shape[3]
    half = (groups // 2) * units
    index = unit_index(groups, units, 0)
    shapes, specs = split_outputs(groups, units, unit, width)
    cells = 4 * 2 * half * unit * width
    return pl.pallas_call(
        functools.partial(merge_kernel, groups=groups, units=units, unit=unit),
        grid_spec=pltpu.PrefetchScalarGridSpec(
            num_scalar_prefetch=1,
            grid=(2 * half,),
            in_specs=[
                pl.BlockSpec((1, 4, unit, width), lambda i, ctl: (index(i, ctl), 0, 0, 0)),
                pl.BlockSpec((1, 4 * unit + 16, width), lambda i, ctl: (index(i, ctl), 0, 0)),
            ],
            out_specs=specs,
        ),
        out_shape=shapes,
        compiler_params=params(),
        cost_estimate=pl.CostEstimate(flops=32768 * cells, bytes_accessed=cells, transcendentals=0),
        name="merge",
    )(ctl, mine, got)


def last_merge(ctl, mine, got, *, units, unit, blocks):
    width = mine.shape[3]
    cells = 4 * units * unit * width
    return pl.pallas_call(
        functools.partial(last_merge_kernel, unit=unit, blocks=blocks),
        grid_spec=pltpu.PrefetchScalarGridSpec(
            num_scalar_prefetch=1,
            grid=(units,),
            in_specs=[
                pl.BlockSpec((1, 4, unit, width), lambda i, ctl: (i, 0, 0, 0)),
                pl.BlockSpec((1, 4 * unit + 16, width), lambda i, ctl: (i, 0, 0)),
            ],
            out_specs=pl.BlockSpec((blocks, 1, unit + 16, 4 * width // blocks), lambda i, ctl: (0, i, 0, 0)),
            scratch_shapes=[pltpu.VMEM((4, unit, width), jnp.float32)],
        ),
        out_shape=jax.ShapeDtypeStruct((blocks, units, unit + 16, 4 * width // blocks), jnp.int16),
        compiler_params=params(),
        cost_estimate=pl.CostEstimate(flops=32768 * cells, bytes_accessed=cells, transcendentals=0),
        name="last_merge",
    )(ctl, mine, got)


def compose(got, so_far, *, unit, first, rows):
    blocks, units = got.shape[:2]
    part = got.shape[3] // 4
    cells = 4 * units * unit * part * blocks
    operands = [got]
    in_specs = [pl.BlockSpec((blocks, 1, unit + 16, 4 * part), lambda i: (0, i, 0, 0))]
    if so_far is not None:
        operands.append(so_far)
        in_specs.append(pl.BlockSpec(memory_space=pl.ANY))
    return pl.pallas_call(
        functools.partial(compose_kernel, unit=unit, blocks=blocks),
        grid=(units,),
        in_specs=in_specs,
        out_specs=pl.BlockSpec((4, unit, part), lambda i: (0, first + i, 0)),
        out_shape=jax.ShapeDtypeStruct((4, rows, part), jnp.float32),
        input_output_aliases={1: 0} if so_far is not None else {},
        compiler_params=params(),
        cost_estimate=pl.CostEstimate(flops=32768 * cells, bytes_accessed=cells, transcendentals=0),
        name="compose",
    )(*operands)


def chunk_units(units):
    return [1] * units


def per_device(field, transfer, bin_order, light_angles):
    tiles = lax.axis_size("tile")
    blocks = lax.axis_size("depth")
    devices = tiles * blocks
    layers, total, width = field.shape
    rows = total // tiles
    unit = unit_rows(rows)
    levels = tiles.bit_length() - 1

    table = jnp.take(transfer, bin_order, axis=1)
    table = table * jnp.array([[1.0], [1.0], [1.0], [0.01]], jnp.float32)
    bins = table.shape[1]
    slope = jnp.concatenate([table[:, 1:] - table[:, :-1], jnp.zeros_like(table[:, :1])], axis=1)
    slope = jnp.pad(slope, ((0, 4), (0, LANES - bins)))
    coarse = lax.reduce_precision(table, exponent_bits=8, mantissa_bits=7)
    table = jnp.concatenate([coarse, table - coarse], axis=0)
    spread = jnp.eye(16, dtype=jnp.float32)
    table = (table[:, None, :, None] * spread[None, :, None, :]).reshape(8 * 16, bins * 16).astype(jnp.bfloat16)
    azimuth, polar = light_angles[0], light_angles[1]
    light = 0.105 * jnp.stack(
        [jnp.cos(azimuth) * jnp.sin(polar), jnp.sin(azimuth) * jnp.sin(polar), jnp.cos(polar)]
    )

    tile = lax.axis_index("tile")
    bits = [((tile >> b) & 1).astype(jnp.int32) for b in range(levels)]
    controls = [jnp.stack([bits[min(b, levels - 1)], bits[max(b - 1, 0)]]) for b in range(levels + 1)]
    up = [(i, i + 1) for i in range(devices - 1)]
    down = [(j, i) for i, j in up]
    both = ("depth", "tile")
    front = field[0].reshape(tiles, rows, width)
    back = field[layers - 1].reshape(tiles, rows, width)

    sizes = chunk_units(rows // unit)
    count = len(sizes)
    starts = [sum(sizes[:n]) * unit for n in range(count)]
    halos = []
    for n, units in enumerate(sizes):
        def cut(layer):
            part = layer[:, starts[n]:starts[n] + units * unit]
            return part.reshape(tiles * units, unit, width)

        ends = (cut(back), cut(front))
        if n > 0:
            ends, _ = lax.optimization_barrier((ends, halos[n - 1]))
        halos.append((lax.ppermute(ends[0], both, up), lax.ppermute(ends[1], both, down)))

    def exchange(send, level):
        return lax.ppermute(send, "tile", [(i, i ^ (1 << level)) for i in range(tiles)])

    chain = []
    waits = []

    def after_last(control):
        if chain:
            control, _, _ = lax.optimization_barrier((control, chain[-1], list(waits)))
            waits.clear()
        return control

    state = [None] * count

    def start_chunk(n):
        before, after = halos[n]
        send, keep = render(
            after_last(controls[0]), light, table, slope, field, before, after,
            groups=tiles, units=sizes[n], unit=unit, rows=rows, offset=starts[n],
        )
        chain.append(send)
        state[n] = (keep, exchange(send, 0))

    def merge_chunk(n, level):
        keep, got = state[n]
        send, keep = merge(
            after_last(controls[level]), keep, got, groups=tiles >> level, units=sizes[n], unit=unit
        )
        chain.append(send)
        state[n] = (keep, exchange(send, level))

    def block_chunk(n):
        keep, got = state[n]
        send = last_merge(after_last(controls[levels]), keep, got, units=sizes[n], unit=unit, blocks=blocks)
        chain.append(send)
        state[n] = lax.all_to_all(send, "depth", split_axis=0, concat_axis=0, tiled=True)

    def turn(step):
        n, level = step
        return (level + 1.5 if n == count - 1 else level, n)

    last = count - 1
    for n, level in sorted([(n, level) for n in range(count) for level in range(levels + 1)], key=turn):
        if n == 0 and level == 1 and count > 1:
            waits.extend(halos[last])
        if n == 0 and level == 2:
            waits.extend(state[k][1] for k in range(last))
        if level == 0:
            start_chunk(n)
        elif level < levels:
            merge_chunk(n, level)
        else:
            block_chunk(n)
    final = None
    for n in range(count):
        final = compose(state[n], final, unit=unit, first=starts[n] // unit, rows=rows)
    return final


def solution(mesh):
    in_specs = (P(("depth", "tile"), None, None), P(), P(), P())
    out_specs = P(None, "tile", "depth")
    return jax.shard_map(
        per_device, mesh=mesh, in_specs=in_specs, out_specs=out_specs, check_vma=False
    )
```

```python
import functools
import math

import jax
import jax.numpy as jnp
from jax import lax
from jax.experimental import pallas as pl
from jax.experimental.pallas import tpu as pltpu
from jax.sharding import PartitionSpec as P

LANES = 128
HALF = LANES // 2
CODES = 32700.0
VMEM_LIMIT = 56 * 1024 * 1024


def unit_rows(rows):
    return 48 if rows % 48 == 0 else rows


def encode(values):
    top = functools.reduce(jnp.maximum, values)
    top = jnp.max(top, axis=0, keepdims=True)
    exponent = jnp.ceil(jnp.log2(jnp.maximum(top, 1e-30)))
    factor = jnp.exp2(-exponent) * CODES
    codes = [(v * factor + 0.5).astype(jnp.int32).astype(jnp.int16) for v in values]
    row = jnp.broadcast_to(exponent, (16, exponent.shape[1]))
    return codes, row.astype(jnp.int32).astype(jnp.int16)


def decode(codes, row):
    exponent = row.astype(jnp.int32).astype(jnp.float32)[0:1]
    scale = jnp.exp2(exponent) * (1.0 / CODES)
    return [c.astype(jnp.int32).astype(jnp.float32) * scale for c in codes]


def over(front, back):
    clear = 1.0 - front[3]
    return [f + clear * b for f, b in zip(front, back)]


def lookup(table, index):
    numbers = lax.GatherDimensionNumbers(
        offset_dims=(), collapsed_slice_dims=(1,), start_index_map=(1,),
        operand_batching_dims=(0,), start_indices_batching_dims=(0,),
    )
    return lax.gather(
        table, index[..., None], numbers, slice_sizes=(1, 1), mode=lax.GatherScatterMode.PROMISE_IN_BOUNDS
    )


def choose(bins, whole):
    place = whole.astype(jnp.bfloat16)
    one, zero = jnp.ones_like(place), jnp.zeros_like(place)
    return jnp.concatenate([jnp.where(place == k, one, zero) for k in range(bins)], axis=0)


def padded_rows(unit):
    return -(-unit // 16) * 16


def each_strip(width, body):
    strips = width // LANES
    together = 3 if strips % 3 == 0 else 1

    def step(c, carry):
        for k in range(together):
            body(pl.multiple_of((c * together + k) * LANES, LANES))
        return carry

    lax.fori_loop(0, strips // together, step, 0)


def render_kernel(ctl, light, table, slope, row_band, column_band, main, above, below, before, after, send, keep, cells, halves, image, stage, ends, *, groups, units, unit, block, rows, offset, total):
    i = pl.program_id(0)
    half = (groups // 2) * units
    rest = lax.rem(i, half)
    sending = i < half
    parity = jnp.where(sending, 1 - ctl[0], ctl[0])
    group = 2 * (rest // units) + parity
    start = group * rows + offset + lax.rem(rest, units) * unit
    layers = main.shape[0]
    width = main.shape[2]
    tall = padded_rows(unit)
    aligned = block == unit
    inner = slice(HALF, HALF + width)

    @pl.when(i == 0)
    def _():
        halves[:, :, 0:LANES] = jnp.zeros((layers, tall, LANES), jnp.bfloat16)
        halves[:, :, width:] = jnp.zeros((layers, tall, LANES), jnp.bfloat16)

    def load_layer(layer, carry):
        up = above[layer].astype(jnp.float32)
        down = below[layer].astype(jnp.float32)
        up = jnp.where(start > 0, up, 0.0)
        down = jnp.where(start + unit < total, down, 0.0)
        if aligned:
            cells[layer, 0:16, :] = up.astype(jnp.bfloat16)
            cells[layer, 16:16 + unit, :] = main[layer]
            cells[layer, 16 + unit:32 + unit, :] = down.astype(jnp.bfloat16)
        else:
            shift = pl.multiple_of(lax.rem(start, block), 8)
            stage[0:block, :] = main[layer].astype(jnp.float32)
            body = stage[pl.ds(shift, unit), :]
            up = jnp.where(lax.rem(start, 16) == 0, up[8:16], up[0:8])
            down = jnp.where(lax.rem(start + unit, 16) == 0, down[0:8], down[8:16])
            stage[0:8, :] = jnp.zeros((8, width), jnp.float32)
            stage[8:16, :] = up
            stage[16:16 + unit, :] = body
            stage[16 + unit:24 + unit, :] = down
            stage[24 + unit:tall + 32, :] = jnp.zeros((tall + 8 - unit, width), jnp.float32)
            cells[layer, :, :] = stage[0:tall + 32, :].astype(jnp.bfloat16)
        halves[layer, :, inner] = cells[layer, 16:16 + tall, :]
        return carry

    lax.fori_loop(0, layers, load_layer, 0)
    if not aligned:
        ends[0, 0:unit, :] = before[0].astype(jnp.float32)
        ends[1, 0:unit, :] = after[0].astype(jnp.float32)

    lx, ly, lz = light[0], light[1], light[2]
    step = 16
    bins = table.shape[1] // step
    slopes = [jnp.broadcast_to(slope[k:k + 1, :], (step, LANES)) for k in range(4)]

    def strip(c, carry):
        at = pl.multiple_of(c * LANES, LANES)
        cols = pl.ds(at, LANES)
        window = pl.ds(at, 2 * LANES)
        spans = [slice(r, r + step) for r in range(0, tall, step)]
        inside = [slice(16 + r, 16 + r + step) for r in range(0, tall, step)]
        if aligned:
            low = [before[0, s, cols].astype(jnp.float32) for s in spans]
            far = [after[0, s, cols].astype(jnp.float32) for s in spans]
        else:
            low = [ends[0, s, cols] for s in spans]
            far = [ends[1, s, cols] for s in spans]
        here = [cells[0, s, cols].astype(jnp.float32) for s in inside]
        clear = [None] * len(spans)
        colour = [None] * len(spans)
        for first in range(0, layers, 2):
            pair = range(first, min(first + 2, layers))
            count = len(pair)
            both = jnp.concatenate([cells[l, :, cols] for l in pair], axis=1) if count > 1 else cells[first, :, cols]
            slope_y = jnp.dot(row_band[...], both, preferred_element_type=jnp.float32)
            wide = halves[first:first + count, :, window].reshape(count * tall, 2 * LANES)
            slope_z = jnp.dot(wide, column_band[...], preferred_element_type=jnp.float32)
            for n, s in enumerate(spans):
                parts, picks, shades, tilts = [], [], [], []
                for m, layer in enumerate(pair):
                    if layer + 1 < layers:
                        high = cells[layer + 1, inside[n], cols].astype(jnp.float32)
                    else:
                        high = far[n]
                    position = jnp.clip(here[n] * 2.5 + 7.5, 0.0, 15.0)
                    index = position.astype(jnp.int32)
                    whole = index.astype(jnp.float32)
                    parts.append(position - whole)
                    tilts.append([lookup(slopes[k], index) for k in range(4)])
                    picks.append(choose(bins, whole))
                    gx = high - low[n]
                    gy = slope_y[s, m * LANES:(m + 1) * LANES]
                    gz = slope_z[m * tall + s.start:m * tall + s.stop]
                    facing = jnp.abs(gx * lx + gy * ly + gz * lz)
                    square = gx * gx + gy * gy + gz * gz
                    shades.append(0.045 + facing * lax.rsqrt(jnp.maximum(square, 4.0)))
                    low[n], here[n] = here[n], high
                pick = jnp.concatenate(picks, axis=1) if len(picks) > 1 else picks[0]
                found = jnp.dot(table[...], pick, preferred_element_type=jnp.float32)
                for m, layer in enumerate(pair):
                    lanes = slice(m * LANES, (m + 1) * LANES)
                    tf = [
                        found[k * step:(k + 1) * step, lanes]
                        + found[(4 + k) * step:(5 + k) * step, lanes]
                        + parts[m] * tilts[m][k]
                        for k in range(4)
                    ]
                    shade = shades[m]
                    if layer == 0:
                        colour[n] = [tf[k] * shade for k in range(3)]
                        clear[n] = 1.0 - tf[3]
                    else:
                        seen = shade * clear[n]
                        colour[n] = [colour[n][k] + tf[k] * seen for k in range(3)]
                        clear[n] = clear[n] - clear[n] * tf[3]
        for n, s in enumerate(spans):
            for k in range(3):
                image[k, s, cols] = colour[n][k]
            image[3, s, cols] = 1.0 - clear[n]
        return carry

    lax.fori_loop(0, width // LANES, strip, 0)

    @pl.when(sending)
    def _():
        def put(at):
            cols = pl.ds(at, LANES)
            put_codes(send, [image[k, 0:unit, cols] for k in range(4)], cols, unit)

        each_strip(width, put)

    @pl.when(jnp.logical_not(sending))
    def _():
        keep[0] = image[:, 0:unit, :]


def put_codes(send, values, cols, unit):
    codes, row = encode(values)
    for k in range(4):
        send[0, k * unit:(k + 1) * unit, cols] = codes[k]
    send[0, 4 * unit:4 * unit + 16, cols] = row


def get_unit(ctl, mine, got, cols, unit):
    theirs = decode(
        [got[0, k * unit:(k + 1) * unit, cols] for k in range(4)],
        got[0, 4 * unit:4 * unit + 16, cols],
    )
    ours = [mine[0, k, :, cols] for k in range(4)]
    behind = ctl[1] == 1
    front = [jnp.where(behind, t, o) for t, o in zip(theirs, ours)]
    back = [jnp.where(behind, o, t) for t, o in zip(theirs, ours)]
    return over(front, back)


def merge_kernel(ctl, mine, got, *sends, units, unit):
    turn = pl.program_id(0) // units
    width = mine.shape[3]
    for k, send in enumerate(sends):
        @pl.when(turn == k)
        def _(send=send):
            def put(at):
                cols = pl.ds(at, LANES)
                put_codes(send, get_unit(ctl, mine, got, cols, unit), cols, unit)

            each_strip(width, put)


def gather_kernel(ctl, *refs, unit, blocks):
    parts, send, image = refs[:-2], refs[-2], refs[-1]
    width = image.shape[2]
    for me in range(len(parts)):
        @pl.when(ctl[0] == me)
        def _(me=me):
            def put(at):
                cols = pl.ds(at, LANES)
                total = None
                for j in range(len(parts)):
                    got = parts[me ^ j]
                    part = decode(
                        [got[0, k * unit:(k + 1) * unit, cols] for k in range(4)],
                        got[0, 4 * unit:4 * unit + 16, cols],
                    )
                    total = part if total is None else over(total, part)
                for k in range(4):
                    image[k, :, cols] = total[k]

            each_strip(width, put)

    part = width // blocks
    for b in range(blocks):
        wide = jnp.concatenate([image[k, :, b * part:(b + 1) * part] for k in range(4)], axis=1)
        codes, row = encode([wide])
        send[b, 0, 0:unit, :] = codes[0]
        send[b, 0, unit:unit + 16, :] = row


def compose_kernel(got, *refs, unit, blocks):
    out = refs[-1]
    part = out.shape[2]
    total = None
    for b in range(blocks):
        wide = decode([got[b, 0, 0:unit, :]], got[b, 0, unit:unit + 16, :])[0]
        layer = [wide[:, k * part:(k + 1) * part] for k in range(4)]
        total = layer if total is None else over(total, layer)
    for k in range(4):
        out[k] = total[k]


def params():
    return pltpu.CompilerParams(vmem_limit_bytes=VMEM_LIMIT, dimension_semantics=("arbitrary",))


def unit_index(groups, units, bit):
    half = (groups // 2) * units

    def index(i, ctl):
        rest = lax.rem(i, half)
        parity = jnp.where(i < half, 1 - ctl[bit], ctl[bit])
        return (2 * (rest // units) + parity) * units + lax.rem(rest, units)

    return index


def split_outputs(groups, units, unit, width):
    half = (groups // 2) * units
    shapes = [
        jax.ShapeDtypeStruct((half, 4 * unit + 16, width), jnp.int16),
        jax.ShapeDtypeStruct((half, 4, unit, width), jnp.float32),
    ]
    specs = [
        pl.BlockSpec((1, 4 * unit + 16, width), lambda i, ctl: (jnp.minimum(i, half - 1), 0, 0)),
        pl.BlockSpec((1, 4, unit, width), lambda i, ctl: (jnp.maximum(i - half, 0), 0, 0, 0)),
    ]
    return shapes, specs


def band(shape, dim, offset):
    place = lax.broadcasted_iota(jnp.int32, shape, dim) - lax.broadcasted_iota(jnp.int32, shape, 1 - dim) - offset
    return jnp.where(place == 1, 1.0, jnp.where(place == -1, -1.0, 0.0)).astype(jnp.bfloat16)


def render(ctl, light, table, slope, field, before, after, *, groups, units, unit, rows, offset):
    layers, total, width = field.shape
    block = math.lcm(unit, 16)
    tall = padded_rows(unit)
    row_band = band((tall, tall + 32), 1, 16)
    column_band = band((2 * LANES, LANES), 0, HALF)
    half = (groups // 2) * units
    index = unit_index(groups, units, 0)

    def start(i, ctl):
        unit_at = index(i, ctl)
        return (unit_at // units) * rows + offset + lax.rem(unit_at, units) * unit

    def main_at(i, ctl):
        return (0, start(i, ctl) // block, 0)

    def above_at(i, ctl):
        return (0, jnp.maximum(start(i, ctl) - 1, 0) // 16, 0)

    def below_at(i, ctl):
        return (0, jnp.minimum(start(i, ctl) + unit, total - 1) // 16, 0)

    shapes, specs = split_outputs(groups, units, unit, width)
    kernel = functools.partial(
        render_kernel, groups=groups, units=units, unit=unit, block=block, rows=rows, offset=offset, total=total
    )
    cells = layers * 2 * half * unit * width
    return pl.pallas_call(
        kernel,
        grid_spec=pltpu.PrefetchScalarGridSpec(
            num_scalar_prefetch=1,
            grid=(2 * half,),
            in_specs=[
                pl.BlockSpec(memory_space=pltpu.SMEM),
                pl.BlockSpec(table.shape, lambda i, ctl: (0, 0)),
                pl.BlockSpec(slope.shape, lambda i, ctl: (0, 0)),
                pl.BlockSpec((tall, tall + 32), lambda i, ctl: (0, 0)),
                pl.BlockSpec((2 * LANES, LANES), lambda i, ctl: (0, 0)),
                pl.BlockSpec((layers, block, width), main_at),
                pl.BlockSpec((layers, 16, width), above_at),
                pl.BlockSpec((layers, 16, width), below_at),
                pl.BlockSpec((1, unit, width), lambda i, ctl: (index(i, ctl), 0, 0)),
                pl.BlockSpec((1, unit, width), lambda i, ctl: (index(i, ctl), 0, 0)),
            ],
            out_specs=specs,
            scratch_shapes=[
                pltpu.VMEM((layers, tall + 32, width), jnp.bfloat16),
                pltpu.VMEM((layers, tall, width + LANES), jnp.bfloat16),
                pltpu.VMEM((4, tall, width), jnp.float32),
                pltpu.VMEM((max(block, tall + 32), width) if block != unit else (8, LANES), jnp.float32),
                pltpu.VMEM((2, tall, width) if block != unit else (1, 8, LANES), jnp.float32),
            ],
        ),
        out_shape=shapes,
        compiler_params=params(),
        cost_estimate=pl.CostEstimate(flops=16384 * cells, bytes_accessed=6 * cells, transcendentals=cells),
        name="render",
    )(ctl, light, table, slope, row_band, column_band, field, field, field, before, after)


def merge(ctl, mine, got, *, places, units, unit):
    width = mine.shape[3]
    cells = 4 * places * units * unit * width

    def index(i, ctl):
        return (ctl[0] ^ (i // units)) * units + lax.rem(i, units)

    def spec(k):
        return pl.BlockSpec(
            (1, 4 * unit + 16, width), lambda i, ctl: (jnp.clip(i - k * units, 0, units - 1), 0, 0)
        )

    return pl.pallas_call(
        functools.partial(merge_kernel, units=units, unit=unit),
        grid_spec=pltpu.PrefetchScalarGridSpec(
            num_scalar_prefetch=1,
            grid=(places * units,),
            in_specs=[
                pl.BlockSpec((1, 4, unit, width), lambda i, ctl: (index(i, ctl), 0, 0, 0)),
                pl.BlockSpec((1, 4 * unit + 16, width), lambda i, ctl: (index(i, ctl), 0, 0)),
            ],
            out_specs=[spec(k) for k in range(places)],
        ),
        out_shape=[jax.ShapeDtypeStruct((units, 4 * unit + 16, width), jnp.int16)] * places,
        compiler_params=params(),
        cost_estimate=pl.CostEstimate(flops=32768 * cells, bytes_accessed=cells, transcendentals=0),
        name="merge",
    )(ctl, mine, got)


def gather_parts(ctl, parts, *, units, unit, blocks):
    width = parts[0].shape[2]
    cells = 4 * units * unit * width
    return pl.pallas_call(
        functools.partial(gather_kernel, unit=unit, blocks=blocks),
        grid_spec=pltpu.PrefetchScalarGridSpec(
            num_scalar_prefetch=1,
            grid=(units,),
            in_specs=[pl.BlockSpec((1, 4 * unit + 16, width), lambda i, ctl: (i, 0, 0))] * len(parts),
            out_specs=pl.BlockSpec((blocks, 1, unit + 16, 4 * width // blocks), lambda i, ctl: (0, i, 0, 0)),
            scratch_shapes=[pltpu.VMEM((4, unit, width), jnp.float32)],
        ),
        out_shape=jax.ShapeDtypeStruct((blocks, units, unit + 16, 4 * width // blocks), jnp.int16),
        compiler_params=params(),
        cost_estimate=pl.CostEstimate(flops=131072 * cells, bytes_accessed=cells, transcendentals=0),
        name="gather_parts",
    )(ctl, *parts)


def compose(got, so_far, *, unit, first, rows):
    blocks, units = got.shape[:2]
    part = got.shape[3] // 4
    cells = 4 * units * unit * part * blocks
    operands = [got]
    in_specs = [pl.BlockSpec((blocks, 1, unit + 16, 4 * part), lambda i: (0, i, 0, 0))]
    if so_far is not None:
        operands.append(so_far)
        in_specs.append(pl.BlockSpec(memory_space=pl.ANY))
    return pl.pallas_call(
        functools.partial(compose_kernel, unit=unit, blocks=blocks),
        grid=(units,),
        in_specs=in_specs,
        out_specs=pl.BlockSpec((4, unit, part), lambda i: (0, first + i, 0)),
        out_shape=jax.ShapeDtypeStruct((4, rows, part), jnp.float32),
        input_output_aliases={1: 0} if so_far is not None else {},
        compiler_params=params(),
        cost_estimate=pl.CostEstimate(flops=32768 * cells, bytes_accessed=cells, transcendentals=0),
        name="compose",
    )(*operands)


def chunk_units(units):
    return [1] * units


def per_device(field, transfer, bin_order, light_angles):
    tiles = lax.axis_size("tile")
    blocks = lax.axis_size("depth")
    devices = tiles * blocks
    layers, total, width = field.shape
    rows = total // tiles
    unit = unit_rows(rows)
    places = tiles // 2

    table = jnp.take(transfer, bin_order, axis=1)
    table = table * jnp.array([[1.0], [1.0], [1.0], [0.01]], jnp.float32)
    bins = table.shape[1]
    slope = jnp.concatenate([table[:, 1:] - table[:, :-1], jnp.zeros_like(table[:, :1])], axis=1)
    slope = jnp.pad(slope, ((0, 4), (0, LANES - bins)))
    coarse = lax.reduce_precision(table, exponent_bits=8, mantissa_bits=7)
    table = jnp.concatenate([coarse, table - coarse], axis=0)
    spread = jnp.eye(16, dtype=jnp.float32)
    table = (table[:, None, :, None] * spread[None, :, None, :]).reshape(8 * 16, bins * 16).astype(jnp.bfloat16)
    azimuth, polar = light_angles[0], light_angles[1]
    light = 0.105 * jnp.stack(
        [jnp.cos(azimuth) * jnp.sin(polar), jnp.sin(azimuth) * jnp.sin(polar), jnp.cos(polar)]
    )

    tile = lax.axis_index("tile")
    core, place = (tile & 1).astype(jnp.int32), (tile >> 1).astype(jnp.int32)
    render_control = jnp.stack([core, core])
    merge_control = jnp.stack([place, core])
    up = [(i, i + 1) for i in range(devices - 1)]
    down = [(j, i) for i, j in up]
    both = ("depth", "tile")

    sizes = chunk_units(rows // unit)
    count = len(sizes)
    starts = [sum(sizes[:n]) * unit for n in range(count)]
    halos = []
    for n, units in enumerate(sizes):
        def cut(layer):
            part = field.reshape(layers, tiles, rows, width)[layer:layer + 1, :, starts[n]:starts[n] + units * unit]
            return part.reshape(tiles * units, unit, width)

        ends = (cut(layers - 1), cut(0))
        if n > 0:
            ends, _ = lax.optimization_barrier((ends, halos[n - 1]))
        halos.append((lax.ppermute(ends[0], both, up), lax.ppermute(ends[1], both, down)))

    def exchange(send, distance):
        return lax.ppermute(send, "tile", [(i, i ^ distance) for i in range(tiles)])

    chain = []
    waits = []

    def after_last(control):
        if chain:
            control, _, _ = lax.optimization_barrier((control, chain[-1], list(waits)))
            waits.clear()
        return control

    state = [None] * count

    def start_chunk(n):
        before, after = halos[n]
        send, keep = render(
            after_last(render_control), light, table, slope, field, before, after,
            groups=tiles, units=sizes[n], unit=unit, rows=rows, offset=starts[n],
        )
        chain.append(send)
        state[n] = (keep, exchange(send, 1))

    def merge_chunk(n):
        keep, got = state[n]
        sends = merge(after_last(merge_control), keep, got, places=places, units=sizes[n], unit=unit)
        chain.append(sends[-1])
        state[n] = [sends[0]] + [exchange(sends[k], 2 * k) for k in range(1, places)]

    def block_chunk(n):
        send = gather_parts(after_last(merge_control), state[n], units=sizes[n], unit=unit, blocks=blocks)
        chain.append(send)
        state[n] = lax.all_to_all(send, "depth", split_axis=0, concat_axis=0, tiled=True)

    last = count - 1
    steps = [(n, level) for n in range(count) for level in range(3)]
    for n, level in sorted(steps, key=lambda step: (step[1] + 1.5 * (step[0] == last), step[0])):
        if n == 0 and level == 1 and count > 1:
            waits.extend(halos[last])
        if n == 0 and level == 2:
            waits.extend(part for k in range(last) for part in state[k])
        (start_chunk, merge_chunk, block_chunk)[level](n)
    final = None
    for n in range(count):
        final = compose(state[n], final, unit=unit, first=starts[n] // unit, rows=rows)
    return final


def solution(mesh):
    in_specs = (P(("depth", "tile"), None, None), P(), P(), P())
    out_specs = P(None, "tile", "depth")
    return jax.shard_map(
        per_device, mesh=mesh, in_specs=in_specs, out_specs=out_specs, check_vma=False
    )
```

```python
import functools
import math

import jax
import jax.numpy as jnp
from jax import lax
from jax.experimental import pallas as pl
from jax.experimental.pallas import tpu as pltpu
from jax.sharding import PartitionSpec as P

LANES = 128
CODES = 32700.0
VMEM_LIMIT = 56 * 1024 * 1024


def unit_rows(rows):
    return 48 if rows % 48 == 0 else rows


def encode(values):
    top = functools.reduce(jnp.maximum, values)
    top = jnp.max(top, axis=0, keepdims=True)
    exponent = jnp.ceil(jnp.log2(jnp.maximum(top, 1e-30)))
    factor = jnp.exp2(-exponent) * CODES
    codes = [(v * factor + 0.5).astype(jnp.int32).astype(jnp.int16) for v in values]
    row = jnp.broadcast_to(exponent, (16, exponent.shape[1]))
    return codes, row.astype(jnp.int32).astype(jnp.int16)


def decode(codes, row):
    exponent = row.astype(jnp.int32).astype(jnp.float32)[0:1]
    scale = jnp.exp2(exponent) * (1.0 / CODES)
    return [c.astype(jnp.int32).astype(jnp.float32) * scale for c in codes]


def over(front, back):
    clear = 1.0 - front[3]
    return [f + clear * b for f, b in zip(front, back)]


def lookup(table, index):
    numbers = lax.GatherDimensionNumbers(
        offset_dims=(), collapsed_slice_dims=(1,), start_index_map=(1,),
        operand_batching_dims=(0,), start_indices_batching_dims=(0,),
    )
    return lax.gather(
        table, index[..., None], numbers, slice_sizes=(1, 1), mode=lax.GatherScatterMode.PROMISE_IN_BOUNDS
    )


def choose(bins, whole):
    place = whole.astype(jnp.bfloat16)
    one, zero = jnp.ones_like(place), jnp.zeros_like(place)
    return jnp.concatenate([jnp.where(place == k, one, zero) for k in range(bins)], axis=0)


def padded_rows(unit):
    return -(-unit // 16) * 16


def each_strip(width, body):
    strips = width // LANES
    together = 3 if strips % 3 == 0 else 1

    def step(c, carry):
        for k in range(together):
            body(pl.multiple_of((c * together + k) * LANES, LANES))
        return carry

    lax.fori_loop(0, strips // together, step, 0)


def render_kernel(ctl, light, table, slope, row_bands, column_bands, main, above, below, before, after, send, keep, cells, slopes_y, slopes_z, image, stage, ends, *, groups, units, unit, block, rows, offset, total):
    i = pl.program_id(0)
    half = (groups // 2) * units
    rest = lax.rem(i, half)
    sending = i < half
    parity = jnp.where(sending, 1 - ctl[0], ctl[0])
    group = 2 * (rest // units) + parity
    start = group * rows + offset + lax.rem(rest, units) * unit
    layers = main.shape[0]
    width = main.shape[2]
    tall = padded_rows(unit)
    aligned = block == unit

    def load_layer(layer, carry):
        shift = pl.multiple_of(lax.rem(start, block), 8)
        stage[0:block, :] = main[layer].astype(jnp.float32)
        body = stage[pl.ds(shift, unit), :]
        up = above[layer].astype(jnp.float32)
        down = below[layer].astype(jnp.float32)
        up = jnp.where(lax.rem(start, 16) == 0, up[8:16], up[0:8])
        down = jnp.where(lax.rem(start + unit, 16) == 0, down[0:8], down[8:16])
        stage[0:8, :] = jnp.zeros((8, width), jnp.float32)
        stage[8:16, :] = up
        stage[16:16 + unit, :] = body
        stage[16 + unit:24 + unit, :] = down
        stage[24 + unit:tall + 32, :] = jnp.zeros((tall + 8 - unit, width), jnp.float32)
        cells[layer, :, :] = stage[0:tall + 32, :].astype(jnp.bfloat16)
        return carry

    if not aligned:
        lax.fori_loop(0, layers, load_layer, 0)
        ends[0, 0:unit, :] = before[0].astype(jnp.float32)
        ends[1, 0:unit, :] = after[0].astype(jnp.float32)

    def own(first, count, s, cols):
        if aligned:
            return main[first:first + count, s, cols]
        return cells[first:first + count, 16 + s.start:16 + s.stop, cols]

    def tower(layer, cols):
        if aligned:
            return jnp.concatenate([above[layer, :, cols], main[layer, :, cols], below[layer, :, cols]], axis=0)
        return cells[layer, :, cols]

    def end(which, s, cols):
        if aligned:
            return (before, after)[which][0, s, cols].astype(jnp.float32)
        return ends[which, s, cols]

    lx, ly, lz = light[0], light[1], light[2]
    step = 16
    bins = table.shape[1] // step
    tilts_of = [jnp.broadcast_to(slope[k:k + 1, :], (step, LANES)) for k in range(4)]
    row_kind = jnp.where(start == 0, 1, 0) + jnp.where(start + unit == total, 2, 0)

    def strip(c, carry):
        at = pl.multiple_of(c * LANES, LANES)
        cols = pl.ds(at, LANES)
        window = pl.ds(pl.multiple_of(jnp.clip(at - LANES, 0, width - 3 * LANES), LANES), 3 * LANES)
        column_kind = jnp.where(at == 0, 0, jnp.where(at == width - LANES, 2, 1))
        for first in range(0, layers, 2):
            count = min(2, layers - first)
            towers = [tower(first + m, cols) for m in range(count)]
            both = jnp.concatenate(towers, axis=1) if count > 1 else towers[0]
            found = jnp.dot(row_bands[row_kind], both, preferred_element_type=jnp.float32)
            wide = own(first, count, slice(0, tall), window).reshape(count * tall, 3 * LANES)
            across = jnp.dot(wide, column_bands[column_kind], preferred_element_type=jnp.float32)
            for m in range(count):
                slopes_y[first + m] = found[:, m * LANES:(m + 1) * LANES]
                slopes_z[first + m] = across[m * tall:(m + 1) * tall]

        for r in range(0, tall, step):
            s = slice(r, r + step)
            low = end(0, s, cols)
            here = own(0, 1, s, cols)[0].astype(jnp.float32)
            clear, colour = None, None
            for first in range(0, layers, 2):
                pair = range(first, min(first + 2, layers))
                parts, picks, shades, tilts = [], [], [], []
                for layer in pair:
                    if layer + 1 < layers:
                        high = own(layer + 1, 1, s, cols)[0].astype(jnp.float32)
                    else:
                        high = end(1, s, cols)
                    position = jnp.clip(here * 2.5 + 7.5, 0.0, 15.0)
                    index = position.astype(jnp.int32)
                    whole = index.astype(jnp.float32)
                    parts.append(position - whole)
                    tilts.append([lookup(tilts_of[k], index) for k in range(4)])
                    picks.append(choose(bins, whole))
                    gx = high - low
                    gy = slopes_y[layer, s, :]
                    gz = slopes_z[layer, s, :]
                    facing = jnp.abs(gx * lx + gy * ly + gz * lz)
                    square = gx * gx + gy * gy + gz * gz
                    shades.append(0.045 + facing * lax.rsqrt(jnp.maximum(square, 4.0)))
                    low, here = here, high
                pick = jnp.concatenate(picks, axis=1) if len(picks) > 1 else picks[0]
                found = jnp.dot(table[...], pick, preferred_element_type=jnp.float32)
                for m, layer in enumerate(pair):
                    lanes = slice(m * LANES, (m + 1) * LANES)
                    tf = [
                        found[k * step:(k + 1) * step, lanes]
                        + found[(4 + k) * step:(5 + k) * step, lanes]
                        + parts[m] * tilts[m][k]
                        for k in range(4)
                    ]
                    if layer == 0:
                        colour = [tf[k] * shades[m] for k in range(3)]
                        clear = 1.0 - tf[3]
                    else:
                        seen = shades[m] * clear
                        colour = [colour[k] + tf[k] * seen for k in range(3)]
                        clear = clear - clear * tf[3]
            for k in range(3):
                image[k, s, cols] = colour[k]
            image[3, s, cols] = 1.0 - clear
        return carry

    lax.fori_loop(0, width // LANES, strip, 0)

    @pl.when(sending)
    def _():
        send[0] = image[:, 0:unit, :]

    @pl.when(jnp.logical_not(sending))
    def _():
        keep[0] = image[:, 0:unit, :]


def put_codes(send, values, cols, unit):
    codes, row = encode(values)
    for k in range(4):
        send[0, k * unit:(k + 1) * unit, cols] = codes[k]
    send[0, 4 * unit:4 * unit + 16, cols] = row


def get_unit(ctl, mine, got, cols):
    theirs = [got[0, k, :, cols] for k in range(4)]
    ours = [mine[0, k, :, cols] for k in range(4)]
    behind = ctl[1] == 1
    front = [jnp.where(behind, t, o) for t, o in zip(theirs, ours)]
    back = [jnp.where(behind, o, t) for t, o in zip(theirs, ours)]
    return over(front, back)


def merge_kernel(ctl, mine, got, *sends, units, unit):
    turn = pl.program_id(0) // units
    width = mine.shape[3]
    for k, send in enumerate(sends):
        @pl.when(turn == k)
        def _(send=send):
            def put(at):
                cols = pl.ds(at, LANES)
                put_codes(send, get_unit(ctl, mine, got, cols), cols, unit)

            each_strip(width, put)


def gather_kernel(ctl, *refs, unit, blocks):
    parts, send, image = refs[:-2], refs[-2], refs[-1]
    width = image.shape[2]
    for me in range(len(parts)):
        @pl.when(ctl[0] == me)
        def _(me=me):
            def put(at):
                cols = pl.ds(at, LANES)
                total = None
                for j in range(len(parts)):
                    got = parts[me ^ j]
                    part = decode(
                        [got[0, k * unit:(k + 1) * unit, cols] for k in range(4)],
                        got[0, 4 * unit:4 * unit + 16, cols],
                    )
                    total = part if total is None else over(total, part)
                for k in range(4):
                    image[k, :, cols] = total[k]

            each_strip(width, put)

    part = width // blocks
    for b in range(blocks):
        wide = jnp.concatenate([image[k, :, b * part:(b + 1) * part] for k in range(4)], axis=1)
        codes, row = encode([wide])
        send[b, 0, 0:unit, :] = codes[0]
        send[b, 0, unit:unit + 16, :] = row


def compose_kernel(got, *refs, unit, blocks):
    out = refs[-1]
    part = out.shape[2]
    total = None
    for b in range(blocks):
        wide = decode([got[b, 0, 0:unit, :]], got[b, 0, unit:unit + 16, :])[0]
        layer = [wide[:, k * part:(k + 1) * part] for k in range(4)]
        total = layer if total is None else over(total, layer)
    for k in range(4):
        out[k] = total[k]


def params():
    return pltpu.CompilerParams(vmem_limit_bytes=VMEM_LIMIT, dimension_semantics=("arbitrary",))


def unit_index(groups, units, bit):
    half = (groups // 2) * units

    def index(i, ctl):
        rest = lax.rem(i, half)
        parity = jnp.where(i < half, 1 - ctl[bit], ctl[bit])
        return (2 * (rest // units) + parity) * units + lax.rem(rest, units)

    return index


def split_outputs(groups, units, unit, width):
    half = (groups // 2) * units
    shapes = [
        jax.ShapeDtypeStruct((half, 4, unit, width), jnp.float32),
        jax.ShapeDtypeStruct((half, 4, unit, width), jnp.float32),
    ]
    specs = [
        pl.BlockSpec((1, 4, unit, width), lambda i, ctl: (jnp.minimum(i, half - 1), 0, 0, 0)),
        pl.BlockSpec((1, 4, unit, width), lambda i, ctl: (jnp.maximum(i - half, 0), 0, 0, 0)),
    ]
    return shapes, specs


def band(shape, dim, offset):
    place = lax.broadcasted_iota(jnp.int32, shape, dim) - lax.broadcasted_iota(jnp.int32, shape, 1 - dim) - offset
    return jnp.where(place == 1, 1.0, jnp.where(place == -1, -1.0, 0.0)).astype(jnp.bfloat16)


def render(ctl, light, table, slope, field, before, after, *, groups, units, unit, rows, offset):
    layers, total, width = field.shape
    block = math.lcm(unit, 16)
    tall = padded_rows(unit)
    row_band = band((tall, tall + 32), 1, 16)
    place = lax.broadcasted_iota(jnp.int32, (tall, tall + 32), 1)
    top, bottom = place >= 16, place < 16 + unit
    row_bands = jnp.stack([
        jnp.where(jnp.logical_and(jnp.logical_or(top, kind % 2 == 0), jnp.logical_or(bottom, kind < 2)), row_band, 0)
        for kind in range(4)
    ])
    column_bands = jnp.stack([band((3 * LANES, LANES), 0, k * LANES) for k in range(3)])
    half = (groups // 2) * units
    index = unit_index(groups, units, 0)

    def start(i, ctl):
        unit_at = index(i, ctl)
        return (unit_at // units) * rows + offset + lax.rem(unit_at, units) * unit

    def main_at(i, ctl):
        return (0, start(i, ctl) // block, 0)

    def above_at(i, ctl):
        return (0, jnp.maximum(start(i, ctl) - 1, 0) // 16, 0)

    def below_at(i, ctl):
        return (0, jnp.minimum(start(i, ctl) + unit, total - 1) // 16, 0)

    shapes, specs = split_outputs(groups, units, unit, width)
    kernel = functools.partial(
        render_kernel, groups=groups, units=units, unit=unit, block=block, rows=rows, offset=offset, total=total
    )
    cells = layers * 2 * half * unit * width
    return pl.pallas_call(
        kernel,
        grid_spec=pltpu.PrefetchScalarGridSpec(
            num_scalar_prefetch=1,
            grid=(2 * half,),
            in_specs=[
                pl.BlockSpec(memory_space=pltpu.SMEM),
                pl.BlockSpec(table.shape, lambda i, ctl: (0, 0)),
                pl.BlockSpec(slope.shape, lambda i, ctl: (0, 0)),
                pl.BlockSpec((4, tall, tall + 32), lambda i, ctl: (0, 0, 0)),
                pl.BlockSpec((3, 3 * LANES, LANES), lambda i, ctl: (0, 0, 0)),
                pl.BlockSpec((layers, block, width), main_at),
                pl.BlockSpec((layers, 16, width), above_at),
                pl.BlockSpec((layers, 16, width), below_at),
                pl.BlockSpec((1, unit, width), lambda i, ctl: (index(i, ctl), 0, 0)),
                pl.BlockSpec((1, unit, width), lambda i, ctl: (index(i, ctl), 0, 0)),
            ],
            out_specs=specs,
            scratch_shapes=[
                pltpu.VMEM((layers, tall + 32, width) if block != unit else (1, 16, LANES), jnp.bfloat16),
                pltpu.VMEM((layers, tall, LANES), jnp.float32),
                pltpu.VMEM((layers, tall, LANES), jnp.float32),
                pltpu.VMEM((4, tall, width), jnp.float32),
                pltpu.VMEM((max(block, tall + 32), width) if block != unit else (8, LANES), jnp.float32),
                pltpu.VMEM((2, tall, width) if block != unit else (1, 8, LANES), jnp.float32),
            ],
        ),
        out_shape=shapes,
        compiler_params=params(),
        cost_estimate=pl.CostEstimate(flops=16384 * cells, bytes_accessed=6 * cells, transcendentals=cells),
        name="render",
    )(ctl, light, table, slope, row_bands, column_bands, field, field, field, before, after)


def merge(ctl, mine, got, *, places, units, unit):
    width = mine.shape[3]
    cells = 4 * places * units * unit * width

    def index(i, ctl):
        return (ctl[0] ^ (i // units)) * units + lax.rem(i, units)

    def spec(k):
        return pl.BlockSpec(
            (1, 4 * unit + 16, width), lambda i, ctl: (jnp.clip(i - k * units, 0, units - 1), 0, 0)
        )

    return pl.pallas_call(
        functools.partial(merge_kernel, units=units, unit=unit),
        grid_spec=pltpu.PrefetchScalarGridSpec(
            num_scalar_prefetch=1,
            grid=(places * units,),
            in_specs=[
                pl.BlockSpec((1, 4, unit, width), lambda i, ctl: (index(i, ctl), 0, 0, 0)),
                pl.BlockSpec((1, 4, unit, width), lambda i, ctl: (index(i, ctl), 0, 0, 0)),
            ],
            out_specs=[spec(k) for k in range(places)],
        ),
        out_shape=[jax.ShapeDtypeStruct((units, 4 * unit + 16, width), jnp.int16)] * places,
        compiler_params=params(),
        cost_estimate=pl.CostEstimate(flops=32768 * cells, bytes_accessed=cells, transcendentals=0),
        name="merge",
    )(ctl, mine, got)


def gather_parts(ctl, parts, *, units, unit, blocks):
    width = parts[0].shape[2]
    cells = 4 * units * unit * width
    return pl.pallas_call(
        functools.partial(gather_kernel, unit=unit, blocks=blocks),
        grid_spec=pltpu.PrefetchScalarGridSpec(
            num_scalar_prefetch=1,
            grid=(units,),
            in_specs=[pl.BlockSpec((1, 4 * unit + 16, width), lambda i, ctl: (i, 0, 0))] * len(parts),
            out_specs=pl.BlockSpec((blocks, 1, unit + 16, 4 * width // blocks), lambda i, ctl: (0, i, 0, 0)),
            scratch_shapes=[pltpu.VMEM((4, unit, width), jnp.float32)],
        ),
        out_shape=jax.ShapeDtypeStruct((blocks, units, unit + 16, 4 * width // blocks), jnp.int16),
        compiler_params=params(),
        cost_estimate=pl.CostEstimate(flops=131072 * cells, bytes_accessed=cells, transcendentals=0),
        name="gather_parts",
    )(ctl, *parts)


def compose(got, so_far, *, unit, first, rows):
    blocks, units = got.shape[:2]
    part = got.shape[3] // 4
    cells = 4 * units * unit * part * blocks
    operands = [got]
    in_specs = [pl.BlockSpec((blocks, 1, unit + 16, 4 * part), lambda i: (0, i, 0, 0))]
    if so_far is not None:
        operands.append(so_far)
        in_specs.append(pl.BlockSpec(memory_space=pl.ANY))
    return pl.pallas_call(
        functools.partial(compose_kernel, unit=unit, blocks=blocks),
        grid=(units,),
        in_specs=in_specs,
        out_specs=pl.BlockSpec((4, unit, part), lambda i: (0, first + i, 0)),
        out_shape=jax.ShapeDtypeStruct((4, rows, part), jnp.float32),
        input_output_aliases={1: 0} if so_far is not None else {},
        compiler_params=params(),
        cost_estimate=pl.CostEstimate(flops=32768 * cells, bytes_accessed=cells, transcendentals=0),
        name="compose",
    )(*operands)


def chunk_units(units):
    return [1] * units


def per_device(field, transfer, bin_order, light_angles):
    tiles = lax.axis_size("tile")
    blocks = lax.axis_size("depth")
    devices = tiles * blocks
    layers, total, width = field.shape
    rows = total // tiles
    unit = unit_rows(rows)
    places = tiles // 2

    table = jnp.take(transfer, bin_order, axis=1)
    table = table * jnp.array([[1.0], [1.0], [1.0], [0.01]], jnp.float32)
    bins = table.shape[1]
    slope = jnp.concatenate([table[:, 1:] - table[:, :-1], jnp.zeros_like(table[:, :1])], axis=1)
    slope = jnp.pad(slope, ((0, 4), (0, LANES - bins)))
    coarse = lax.reduce_precision(table, exponent_bits=8, mantissa_bits=7)
    table = jnp.concatenate([coarse, table - coarse], axis=0)
    spread = jnp.eye(16, dtype=jnp.float32)
    table = (table[:, None, :, None] * spread[None, :, None, :]).reshape(8 * 16, bins * 16).astype(jnp.bfloat16)
    azimuth, polar = light_angles[0], light_angles[1]
    light = 0.105 * jnp.stack(
        [jnp.cos(azimuth) * jnp.sin(polar), jnp.sin(azimuth) * jnp.sin(polar), jnp.cos(polar)]
    )

    tile = lax.axis_index("tile")
    core, place = (tile & 1).astype(jnp.int32), (tile >> 1).astype(jnp.int32)
    render_control = jnp.stack([core, core])
    merge_control = jnp.stack([place, core])
    up = [(i, i + 1) for i in range(devices - 1)]
    down = [(j, i) for i, j in up]
    both = ("depth", "tile")

    sizes = chunk_units(rows // unit)
    count = len(sizes)
    starts = [sum(sizes[:n]) * unit for n in range(count)]
    halos = []
    for n, units in enumerate(sizes):
        def cut(layer):
            part = field.reshape(layers, tiles, rows, width)[layer:layer + 1, :, starts[n]:starts[n] + units * unit]
            return part.reshape(tiles * units, unit, width)

        ends = (cut(layers - 1), cut(0))
        if n > 0:
            ends, _ = lax.optimization_barrier((ends, halos[n - 1]))
        halos.append((lax.ppermute(ends[0], both, up), lax.ppermute(ends[1], both, down)))

    def exchange(send, distance):
        return lax.ppermute(send, "tile", [(i, i ^ distance) for i in range(tiles)])

    chain = []
    waits = []

    def after_last(control):
        if chain:
            control, _, _ = lax.optimization_barrier((control, chain[-1], list(waits)))
            waits.clear()
        return control

    state = [None] * count

    def start_chunk(n):
        before, after = halos[n]
        send, keep = render(
            after_last(render_control), light, table, slope, field, before, after,
            groups=tiles, units=sizes[n], unit=unit, rows=rows, offset=starts[n],
        )
        chain.append(send)
        state[n] = (keep, exchange(send, 1))

    def merge_chunk(n):
        keep, got = state[n]
        sends = merge(after_last(merge_control), keep, got, places=places, units=sizes[n], unit=unit)
        chain.append(sends[-1])
        state[n] = [sends[0]] + [exchange(sends[k], 2 * k) for k in range(1, places)]

    def block_chunk(n):
        send = gather_parts(after_last(merge_control), state[n], units=sizes[n], unit=unit, blocks=blocks)
        chain.append(send)
        state[n] = lax.all_to_all(send, "depth", split_axis=0, concat_axis=0, tiled=True)

    last = count - 1
    steps = [(n, level) for n in range(count) for level in range(3)]
    for n, level in sorted(steps, key=lambda step: (step[1] + 1.5 * (step[0] == last), step[0])):
        if n == 0 and level == 1 and count > 1:
            waits.extend(halos[last])
        if n == 0 and level == 2:
            waits.extend(part for k in range(last) for part in state[k])
        (start_chunk, merge_chunk, block_chunk)[level](n)
    final = None
    for n in range(count):
        final = compose(state[n], final, unit=unit, first=starts[n] // unit, rows=rows)
    return final


def solution(mesh):
    in_specs = (P(("depth", "tile"), None, None), P(), P(), P())
    out_specs = P(None, "tile", "depth")
    return jax.shard_map(
        per_device, mesh=mesh, in_specs=in_specs, out_specs=out_specs, check_vma=False
    )
```

```python
import functools
import math

import jax
import jax.numpy as jnp
from jax import lax
from jax.experimental import pallas as pl
from jax.experimental.pallas import tpu as pltpu
from jax.sharding import PartitionSpec as P

LANES = 128
CODES = 32700.0
VMEM_LIMIT = 56 * 1024 * 1024


def unit_rows(rows):
    return 48 if rows % 48 == 0 else rows


def encode(values):
    top = functools.reduce(jnp.maximum, values)
    top = jnp.max(top, axis=0, keepdims=True)
    exponent = jnp.ceil(jnp.log2(jnp.maximum(top, 1e-30)))
    factor = jnp.exp2(-exponent) * CODES
    codes = [(v * factor + 0.5).astype(jnp.int32).astype(jnp.int16) for v in values]
    row = jnp.broadcast_to(exponent, (16, exponent.shape[1]))
    return codes, row.astype(jnp.int32).astype(jnp.int16)


def decode(codes, row):
    exponent = row.astype(jnp.int32).astype(jnp.float32)[0:1]
    scale = jnp.exp2(exponent) * (1.0 / CODES)
    return [c.astype(jnp.int32).astype(jnp.float32) * scale for c in codes]


def over(front, back):
    clear = 1.0 - front[3]
    return [f + clear * b for f, b in zip(front, back)]


def lookup(table, index):
    numbers = lax.GatherDimensionNumbers(
        offset_dims=(), collapsed_slice_dims=(1,), start_index_map=(1,),
        operand_batching_dims=(0,), start_indices_batching_dims=(0,),
    )
    return lax.gather(
        table, index[..., None], numbers, slice_sizes=(1, 1), mode=lax.GatherScatterMode.PROMISE_IN_BOUNDS
    )


def padded_rows(unit):
    return -(-unit // 16) * 16


def each_strip(width, body):
    strips = width // LANES
    together = 3 if strips % 3 == 0 else 1

    def step(c, carry):
        for k in range(together):
            body(pl.multiple_of((c * together + k) * LANES, LANES))
        return carry

    lax.fori_loop(0, strips // together, step, 0)


def render_kernel(ctl, light, table, row_bands, column_bands, main, above, below, before, after, send, keep, cells, slopes_y, slopes_z, image, stage, ends, *, groups, units, unit, block, rows, offset, total):
    i = pl.program_id(0)
    half = (groups // 2) * units
    rest = lax.rem(i, half)
    sending = i < half
    parity = jnp.where(sending, 1 - ctl[0], ctl[0])
    group = 2 * (rest // units) + parity
    start = group * rows + offset + lax.rem(rest, units) * unit
    layers = main.shape[0]
    width = main.shape[2]
    tall = padded_rows(unit)
    aligned = block == unit

    def load_layer(layer, carry):
        shift = pl.multiple_of(lax.rem(start, block), 8)
        stage[0:block, :] = main[layer].astype(jnp.float32)
        body = stage[pl.ds(shift, unit), :]
        up = above[layer].astype(jnp.float32)
        down = below[layer].astype(jnp.float32)
        up = jnp.where(lax.rem(start, 16) == 0, up[8:16], up[0:8])
        down = jnp.where(lax.rem(start + unit, 16) == 0, down[0:8], down[8:16])
        stage[0:8, :] = jnp.zeros((8, width), jnp.float32)
        stage[8:16, :] = up
        stage[16:16 + unit, :] = body
        stage[16 + unit:24 + unit, :] = down
        stage[24 + unit:tall + 32, :] = jnp.zeros((tall + 8 - unit, width), jnp.float32)
        cells[layer, :, :] = stage[0:tall + 32, :].astype(jnp.bfloat16)
        return carry

    if not aligned:
        lax.fori_loop(0, layers, load_layer, 0)
        ends[0, 0:unit, :] = before[0].astype(jnp.float32)
        ends[1, 0:unit, :] = after[0].astype(jnp.float32)

    def own(first, count, s, cols):
        if aligned:
            return main[first:first + count, s, cols]
        return cells[first:first + count, 16 + s.start:16 + s.stop, cols]

    def tower(layer, cols):
        if aligned:
            return jnp.concatenate([above[layer, :, cols], main[layer, :, cols], below[layer, :, cols]], axis=0)
        return cells[layer, :, cols]

    def end(which, s, cols):
        if aligned:
            return (before, after)[which][0, s, cols].astype(jnp.float32)
        return ends[which, s, cols]

    lx, ly, lz = light[0], light[1], light[2]
    step = 16
    tables = [jnp.broadcast_to(table[k:k + 1, :], (step, LANES)) for k in range(8)]
    row_kind = jnp.where(start == 0, 1, 0) + jnp.where(start + unit == total, 2, 0)

    def strip(c, carry):
        at = pl.multiple_of(c * LANES, LANES)
        cols = pl.ds(at, LANES)
        window = pl.ds(pl.multiple_of(jnp.clip(at - LANES, 0, width - 3 * LANES), LANES), 3 * LANES)
        column_kind = jnp.where(at == 0, 0, jnp.where(at == width - LANES, 2, 1))
        for first in range(0, layers, 2):
            count = min(2, layers - first)
            towers = [tower(first + m, cols) for m in range(count)]
            both = jnp.concatenate(towers, axis=1) if count > 1 else towers[0]
            found = jnp.dot(row_bands[row_kind], both, preferred_element_type=jnp.float32)
            wide = own(first, count, slice(0, tall), window).reshape(count * tall, 3 * LANES)
            across = jnp.dot(wide, column_bands[column_kind], preferred_element_type=jnp.float32)
            for m in range(count):
                slopes_y[first + m] = found[:, m * LANES:(m + 1) * LANES]
                slopes_z[first + m] = across[m * tall:(m + 1) * tall]

        for r in range(0, tall, step):
            s = slice(r, r + step)
            low = end(0, s, cols)
            here = own(0, 1, s, cols)[0].astype(jnp.float32)
            clear, colour = None, None
            for layer in range(layers):
                high = own(layer + 1, 1, s, cols)[0].astype(jnp.float32) if layer + 1 < layers else end(1, s, cols)
                position = jnp.clip(here * 2.5 + 7.5, 0.0, 15.0)
                index = position.astype(jnp.int32)
                part = position - index.astype(jnp.float32)
                tf = [lookup(tables[k], index) + part * lookup(tables[4 + k], index) for k in range(4)]
                gx = high - low
                gy = slopes_y[layer, s, :]
                gz = slopes_z[layer, s, :]
                facing = jnp.abs(gx * lx + gy * ly + gz * lz)
                square = gx * gx + gy * gy + gz * gz
                shade = 0.045 + facing * lax.rsqrt(jnp.maximum(square, 4.0))
                low, here = here, high
                if layer == 0:
                    colour = [tf[k] * shade for k in range(3)]
                    clear = 1.0 - tf[3]
                else:
                    seen = shade * clear
                    colour = [colour[k] + tf[k] * seen for k in range(3)]
                    clear = clear - clear * tf[3]
            for k in range(3):
                image[k, s, cols] = colour[k]
            image[3, s, cols] = 1.0 - clear
        return carry

    lax.fori_loop(0, width // LANES, strip, 0)

    @pl.when(sending)
    def _():
        send[0] = image[:, 0:unit, :]

    @pl.when(jnp.logical_not(sending))
    def _():
        keep[0] = image[:, 0:unit, :]


def merge_pair(ctl, mine, got, cols):
    theirs = [got[0, k, :, cols] for k in range(4)]
    ours = [mine[0, k, :, cols] for k in range(4)]
    behind = ctl[1] == 1
    front = [jnp.where(behind, t, o) for t, o in zip(theirs, ours)]
    back = [jnp.where(behind, o, t) for t, o in zip(theirs, ours)]
    return over(front, back)


def merge_kernel(ctl, *refs, members, places, unit):
    inputs, sends = refs[:2 * members], refs[2 * members:2 * members + places]
    image, tops = refs[2 * members + places:]
    turn = pl.program_id(0)
    width = image.shape[2]

    for n in range(members):
        @pl.when(lax.rem(turn, members) == n)
        def _(n=n):
            def put(at):
                cols = pl.ds(at, LANES)
                merged = merge_pair(ctl, inputs[2 * n], inputs[2 * n + 1], cols)
                for k in range(4):
                    image[k, :, cols] = merged[k]
                top = functools.reduce(jnp.maximum, merged)
                tops[0:8, cols] = jnp.max(top.reshape(unit // 8, 8, LANES), axis=0)

            each_strip(width, put)

    top = jnp.max(tops[0:8, :], axis=0, keepdims=True)
    exponent = jnp.ceil(jnp.log2(jnp.maximum(top, 1e-30)))
    tops[0:8, :] = jnp.broadcast_to(jnp.exp2(-exponent) * CODES, (8, width))
    row = jnp.broadcast_to(exponent, (16, width)).astype(jnp.int32).astype(jnp.int16)

    for k, send in enumerate(sends):
        @pl.when(turn // members == k)
        def _(send=send):
            def put(at):
                cols = pl.ds(at, LANES)
                factor = tops[0:1, cols]
                for k in range(4):
                    codes = (image[k, :, cols] * factor + 0.5).astype(jnp.int32).astype(jnp.int16)
                    send[0, k * unit:(k + 1) * unit, cols] = codes

            each_strip(width, put)
            send[0, 4 * unit:4 * unit + 16, :] = row


def gather_kernel(ctl, *refs, unit, blocks):
    parts, send, image = refs[:-2], refs[-2], refs[-1]
    width = image.shape[2]
    for me in range(len(parts)):
        @pl.when(ctl[0] == me)
        def _(me=me):
            def put(at):
                cols = pl.ds(at, LANES)
                total = None
                for j in range(len(parts)):
                    got = parts[me ^ j]
                    part = decode(
                        [got[0, k * unit:(k + 1) * unit, cols] for k in range(4)],
                        got[0, 4 * unit:4 * unit + 16, cols],
                    )
                    total = part if total is None else over(total, part)
                for k in range(4):
                    image[k, :, cols] = total[k]

            each_strip(width, put)

    part = width // blocks
    for b in range(blocks):
        wide = jnp.concatenate([image[k, :, b * part:(b + 1) * part] for k in range(4)], axis=1)
        codes, row = encode([wide])
        send[b, 0, 0:unit, :] = codes[0]
        send[b, 0, unit:unit + 16, :] = row


def compose_kernel(got, *refs, unit, blocks):
    out = refs[-1]
    part = out.shape[2]
    total = None
    for b in range(blocks):
        wide = decode([got[b, 0, 0:unit, :]], got[b, 0, unit:unit + 16, :])[0]
        layer = [wide[:, k * part:(k + 1) * part] for k in range(4)]
        total = layer if total is None else over(total, layer)
    for k in range(4):
        out[k] = total[k]


def params():
    return pltpu.CompilerParams(vmem_limit_bytes=VMEM_LIMIT, dimension_semantics=("arbitrary",))


def unit_index(groups, units, bit):
    half = (groups // 2) * units

    def index(i, ctl):
        rest = lax.rem(i, half)
        parity = jnp.where(i < half, 1 - ctl[bit], ctl[bit])
        return (2 * (rest // units) + parity) * units + lax.rem(rest, units)

    return index


def split_outputs(groups, units, unit, width):
    half = (groups // 2) * units
    shapes = [
        jax.ShapeDtypeStruct((half, 4, unit, width), jnp.float32),
        jax.ShapeDtypeStruct((half, 4, unit, width), jnp.float32),
    ]
    specs = [
        pl.BlockSpec((1, 4, unit, width), lambda i, ctl: (jnp.minimum(i, half - 1), 0, 0, 0)),
        pl.BlockSpec((1, 4, unit, width), lambda i, ctl: (jnp.maximum(i - half, 0), 0, 0, 0)),
    ]
    return shapes, specs


def band(shape, dim, offset):
    place = lax.broadcasted_iota(jnp.int32, shape, dim) - lax.broadcasted_iota(jnp.int32, shape, 1 - dim) - offset
    return jnp.where(place == 1, 1.0, jnp.where(place == -1, -1.0, 0.0)).astype(jnp.bfloat16)


def render(ctl, light, table, field, before, after, *, groups, units, unit, rows, offset, halo_at):
    layers, total, width = field.shape
    block = math.lcm(unit, 16)
    tall = padded_rows(unit)
    row_band = band((tall, tall + 32), 1, 16)
    place = lax.broadcasted_iota(jnp.int32, (tall, tall + 32), 1)
    top, bottom = place >= 16, place < 16 + unit
    row_bands = jnp.stack([
        jnp.where(jnp.logical_and(jnp.logical_or(top, kind % 2 == 0), jnp.logical_or(bottom, kind < 2)), row_band, 0)
        for kind in range(4)
    ])
    column_bands = jnp.stack([band((3 * LANES, LANES), 0, k * LANES) for k in range(3)])
    half = (groups // 2) * units
    index = unit_index(groups, units, 0)

    def start(i, ctl):
        unit_at = index(i, ctl)
        return (unit_at // units) * rows + offset + lax.rem(unit_at, units) * unit

    def main_at(i, ctl):
        return (0, start(i, ctl) // block, 0)

    def above_at(i, ctl):
        return (0, jnp.maximum(start(i, ctl) - 1, 0) // 16, 0)

    def below_at(i, ctl):
        return (0, jnp.minimum(start(i, ctl) + unit, total - 1) // 16, 0)

    shapes, specs = split_outputs(groups, units, unit, width)
    kernel = functools.partial(
        render_kernel, groups=groups, units=units, unit=unit, block=block, rows=rows, offset=offset, total=total
    )
    cells = layers * 2 * half * unit * width
    return pl.pallas_call(
        kernel,
        grid_spec=pltpu.PrefetchScalarGridSpec(
            num_scalar_prefetch=1,
            grid=(2 * half,),
            in_specs=[
                pl.BlockSpec(memory_space=pltpu.SMEM),
                pl.BlockSpec(table.shape, lambda i, ctl: (0, 0)),
                pl.BlockSpec((4, tall, tall + 32), lambda i, ctl: (0, 0, 0)),
                pl.BlockSpec((3, 3 * LANES, LANES), lambda i, ctl: (0, 0, 0)),
                pl.BlockSpec((layers, block, width), main_at),
                pl.BlockSpec((layers, 16, width), above_at),
                pl.BlockSpec((layers, 16, width), below_at),
                pl.BlockSpec((1, unit, width), lambda i, ctl: (index(i, ctl), halo_at, 0)),
                pl.BlockSpec((1, unit, width), lambda i, ctl: (index(i, ctl), halo_at, 0)),
            ],
            out_specs=specs,
            scratch_shapes=[
                pltpu.VMEM((layers, tall + 32, width) if block != unit else (1, 16, LANES), jnp.bfloat16),
                pltpu.VMEM((layers, tall, LANES), jnp.float32),
                pltpu.VMEM((layers, tall, LANES), jnp.float32),
                pltpu.VMEM((4, tall, width), jnp.float32),
                pltpu.VMEM((max(block, tall + 32), width) if block != unit else (8, LANES), jnp.float32),
                pltpu.VMEM((2, tall, width) if block != unit else (1, 8, LANES), jnp.float32),
            ],
        ),
        out_shape=shapes,
        compiler_params=params(),
        cost_estimate=pl.CostEstimate(flops=16384 * cells, bytes_accessed=6 * cells, transcendentals=cells),
        name="render",
    )(ctl, light, table, row_bands, column_bands, field, field, field, before, after)


def merge(ctl, pairs, *, places, unit):
    members = len(pairs)
    width = pairs[0][0].shape[3]
    cells = 4 * places * members * unit * width

    def spec(k):
        return pl.BlockSpec(
            (1, 4 * unit + 16, width), lambda i, ctl: (jnp.clip(i - k * members, 0, members - 1), 0, 0)
        )

    return pl.pallas_call(
        functools.partial(merge_kernel, members=members, places=places, unit=unit),
        grid_spec=pltpu.PrefetchScalarGridSpec(
            num_scalar_prefetch=1,
            grid=(places * members,),
            in_specs=[pl.BlockSpec((1, 4, unit, width), lambda i, ctl: (ctl[0] ^ (i // members), 0, 0, 0))]
            * (2 * members),
            out_specs=[spec(k) for k in range(places)],
            scratch_shapes=[pltpu.VMEM((4, unit, width), jnp.float32), pltpu.VMEM((8, width), jnp.float32)],
        ),
        out_shape=[jax.ShapeDtypeStruct((members, 4 * unit + 16, width), jnp.int16)] * places,
        compiler_params=params(),
        cost_estimate=pl.CostEstimate(flops=32768 * cells, bytes_accessed=cells, transcendentals=0),
        name="merge",
    )(ctl, *[array for pair in pairs for array in pair])


def gather_parts(ctl, parts, *, units, unit, blocks):
    width = parts[0].shape[2]
    cells = 4 * units * unit * width
    return pl.pallas_call(
        functools.partial(gather_kernel, unit=unit, blocks=blocks),
        grid_spec=pltpu.PrefetchScalarGridSpec(
            num_scalar_prefetch=1,
            grid=(units,),
            in_specs=[pl.BlockSpec((1, 4 * unit + 16, width), lambda i, ctl: (i, 0, 0))] * len(parts),
            out_specs=pl.BlockSpec((blocks, 1, unit + 16, 4 * width // blocks), lambda i, ctl: (0, i, 0, 0)),
            scratch_shapes=[pltpu.VMEM((4, unit, width), jnp.float32)],
        ),
        out_shape=jax.ShapeDtypeStruct((blocks, units, unit + 16, 4 * width // blocks), jnp.int16),
        compiler_params=params(),
        cost_estimate=pl.CostEstimate(flops=131072 * cells, bytes_accessed=cells, transcendentals=0),
        name="gather_parts",
    )(ctl, *parts)


def compose(got, so_far, *, unit, first, rows):
    blocks, units = got.shape[:2]
    part = got.shape[3] // 4
    cells = 4 * units * unit * part * blocks
    operands = [got]
    in_specs = [pl.BlockSpec((blocks, 1, unit + 16, 4 * part), lambda i: (0, i, 0, 0))]
    if so_far is not None:
        operands.append(so_far)
        in_specs.append(pl.BlockSpec(memory_space=pl.ANY))
    return pl.pallas_call(
        functools.partial(compose_kernel, unit=unit, blocks=blocks),
        grid=(units,),
        in_specs=in_specs,
        out_specs=pl.BlockSpec((4, unit, part), lambda i: (0, first + i, 0)),
        out_shape=jax.ShapeDtypeStruct((4, rows, part), jnp.float32),
        input_output_aliases={1: 0} if so_far is not None else {},
        compiler_params=params(),
        cost_estimate=pl.CostEstimate(flops=32768 * cells, bytes_accessed=cells, transcendentals=0),
        name="compose",
    )(*operands)


def per_device(field, transfer, bin_order, light_angles):
    tiles = lax.axis_size("tile")
    blocks = lax.axis_size("depth")
    devices = tiles * blocks
    layers, total, width = field.shape
    rows = total // tiles
    unit = unit_rows(rows)
    places = tiles // 2

    table = jnp.take(transfer, bin_order, axis=1)
    table = table * jnp.array([[1.0], [1.0], [1.0], [0.01]], jnp.float32)
    bins = table.shape[1]
    slope = jnp.concatenate([table[:, 1:] - table[:, :-1], jnp.zeros_like(table[:, :1])], axis=1)
    table = jnp.pad(jnp.concatenate([table, slope], axis=0), ((0, 0), (0, LANES - bins)))
    azimuth, polar = light_angles[0], light_angles[1]
    light = 0.105 * jnp.stack(
        [jnp.cos(azimuth) * jnp.sin(polar), jnp.sin(azimuth) * jnp.sin(polar), jnp.cos(polar)]
    )

    tile = lax.axis_index("tile")
    core, place = (tile & 1).astype(jnp.int32), (tile >> 1).astype(jnp.int32)
    render_control = jnp.stack([core, core])
    merge_control = jnp.stack([place, core])
    up = [(i, i + 1) for i in range(devices - 1)]
    down = [(j, i) for i, j in up]
    both = ("depth", "tile")

    count = rows // unit
    starts = [n * unit for n in range(count)]

    def cut(layer, first, stop):
        part = field.reshape(layers, tiles, rows, width)[layer:layer + 1, :, first * unit:stop * unit]
        return part.reshape(tiles, (stop - first) * unit, width)

    halos = []
    for first, stop in [(0, 1), (1, count)][:count]:
        ends = (cut(layers - 1, first, stop), cut(0, first, stop))
        if halos:
            ends, _ = lax.optimization_barrier((ends, halos[0][:2]))
        pair = (lax.ppermute(ends[0], both, up), lax.ppermute(ends[1], both, down))
        halos += [pair + (n - first,) for n in range(first, stop)]

    def exchange(send, distance):
        return lax.ppermute(send, "tile", [(i, i ^ distance) for i in range(tiles)])

    chain = []
    waits = []

    def after_last(control):
        if chain:
            control, _, _ = lax.optimization_barrier((control, chain[-1], list(waits)))
            waits.clear()
        return control

    state = [None] * count

    def start_chunk(n):
        before, after, at = halos[n]
        send, keep = render(
            after_last(render_control), light, table, field, before, after,
            groups=tiles, units=1, unit=unit, rows=rows, offset=starts[n], halo_at=at,
        )
        chain.append(send)
        state[n] = (keep, exchange(send, 1))

    def merge_group(members):
        sends = merge(after_last(merge_control), [state[n] for n in members], places=places, unit=unit)
        chain.append(sends[-1])
        return [sends[0]] + [exchange(sends[k], 2 * k) for k in range(1, places)]

    def block_group(members, parts):
        send = gather_parts(after_last(merge_control), parts, units=len(members), unit=unit, blocks=blocks)
        chain.append(send)
        return lax.all_to_all(send, "depth", split_axis=0, concat_axis=0, tiled=True)

    early, late = list(range(count - 1)), [count - 1]
    results = []
    if early:
        for n in early:
            start_chunk(n)
        early_parts = merge_group(early)
        start_chunk(count - 1)
        waits.extend(early_parts)
        results.append(block_group(early, early_parts))
    else:
        start_chunk(count - 1)
    results.append(block_group(late, merge_group(late)))
    final = None
    done = 0
    for result in results:
        final = compose(result, final, unit=unit, first=done, rows=rows)
        done += result.shape[1]
    return final


def solution(mesh):
    in_specs = (P(("depth", "tile"), None, None), P(), P(), P())
    out_specs = P(None, "tile", "depth")
    return jax.shard_map(
        per_device, mesh=mesh, in_specs=in_specs, out_specs=out_specs, check_vma=False
    )
```

```python
import functools
import math

import jax
import jax.numpy as jnp
from jax import lax
from jax.experimental import pallas as pl
from jax.experimental.pallas import tpu as pltpu
from jax.sharding import PartitionSpec as P

LANES = 128
CODES = 32700.0
ON_MATRIX = 6
VMEM_LIMIT = 56 * 1024 * 1024


def unit_rows(rows):
    return 48 if rows % 48 == 0 else rows


def exponent_of(top):
    return jnp.ceil(jnp.log2(jnp.maximum(top, 1e-30)))


def pack(low, high, factor):
    low = (low * factor + 0.5).astype(jnp.int32)
    high = (high * factor + 0.5).astype(jnp.int32)
    return low | (high << 16)


def unpack(word, scale):
    return (word & 0xFFFF).astype(jnp.float32) * scale, (word >> 16).astype(jnp.float32) * scale


def scale_of(row):
    return jnp.exp2(row.astype(jnp.float32)) * (1.0 / CODES)


def over(front, back):
    clear = 1.0 - front[3]
    return [f + clear * b for f, b in zip(front, back)]


def lookup(table, index):
    numbers = lax.GatherDimensionNumbers(
        offset_dims=(), collapsed_slice_dims=(1,), start_index_map=(1,),
        operand_batching_dims=(0,), start_indices_batching_dims=(0,),
    )
    return lax.gather(
        table, index[..., None], numbers, slice_sizes=(1, 1), mode=lax.GatherScatterMode.PROMISE_IN_BOUNDS
    )


def choose(bins, whole):
    place = whole.astype(jnp.bfloat16)
    one, zero = jnp.ones_like(place), jnp.zeros_like(place)
    return jnp.concatenate([jnp.where(place == k, one, zero) for k in range(bins)], axis=0)


def padded_rows(unit):
    return -(-unit // 16) * 16


def each_strip(width, body):
    strips = width // LANES
    together = 3 if strips % 3 == 0 else 1

    def step(c, carry):
        for k in range(together):
            body(pl.multiple_of((c * together + k) * LANES, LANES))
        return carry

    lax.fori_loop(0, strips // together, step, 0)


def render_kernel(ctl, light, table, slope, row_bands, column_bands, main, above, below, before, after, send, keep, cells, slopes_y, slopes_z, image, stage, ends, *, groups, units, unit, block, rows, offset, total):
    i = pl.program_id(0)
    half = (groups // 2) * units
    rest = lax.rem(i, half)
    sending = i < half
    parity = jnp.where(sending, 1 - ctl[0], ctl[0])
    group = 2 * (rest // units) + parity
    start = group * rows + offset + lax.rem(rest, units) * unit
    layers = main.shape[0]
    width = main.shape[2]
    tall = padded_rows(unit)
    aligned = block == unit

    def load_layer(layer, carry):
        shift = pl.multiple_of(lax.rem(start, block), 8)
        stage[0:block, :] = main[layer].astype(jnp.float32)
        body = stage[pl.ds(shift, unit), :]
        up = above[layer].astype(jnp.float32)
        down = below[layer].astype(jnp.float32)
        up = jnp.where(lax.rem(start, 16) == 0, up[8:16], up[0:8])
        down = jnp.where(lax.rem(start + unit, 16) == 0, down[0:8], down[8:16])
        stage[0:8, :] = jnp.zeros((8, width), jnp.float32)
        stage[8:16, :] = up
        stage[16:16 + unit, :] = body
        stage[16 + unit:24 + unit, :] = down
        stage[24 + unit:tall + 32, :] = jnp.zeros((tall + 8 - unit, width), jnp.float32)
        cells[layer, :, :] = stage[0:tall + 32, :].astype(jnp.bfloat16)
        return carry

    if not aligned:
        lax.fori_loop(0, layers, load_layer, 0)
        ends[0, 0:unit, :] = before[0].astype(jnp.float32)
        ends[1, 0:unit, :] = after[0].astype(jnp.float32)

    def own(first, count, s, cols):
        if aligned:
            return main[first:first + count, s, cols]
        return cells[first:first + count, 16 + s.start:16 + s.stop, cols]

    def tower(layer, cols):
        if aligned:
            return jnp.concatenate([above[layer, :, cols], main[layer, :, cols], below[layer, :, cols]], axis=0)
        return cells[layer, :, cols]

    def end(which, s, cols):
        if aligned:
            return (before, after)[which][0, s, cols].astype(jnp.float32)
        return ends[which, s, cols]

    lx, ly, lz = light[0], light[1], light[2]
    step = 16
    bins = table.shape[1] // step
    rows_found = table.shape[0] // (2 * step)
    tilts_of = [jnp.broadcast_to(slope[k:k + 1, :], (step, LANES)) for k in range(rows_found - 4, 4)]
    row_kind = jnp.where(start == 0, 1, 0) + jnp.where(start + unit == total, 2, 0)

    def strip(c, carry):
        at = pl.multiple_of(c * LANES, LANES)
        cols = pl.ds(at, LANES)
        window = pl.ds(pl.multiple_of(jnp.clip(at - LANES, 0, width - 3 * LANES), LANES), 3 * LANES)
        column_kind = jnp.where(at == 0, 0, jnp.where(at == width - LANES, 2, 1))
        for first in range(0, layers, 2):
            count = min(2, layers - first)
            towers = [tower(first + m, cols) for m in range(count)]
            both = jnp.concatenate(towers, axis=1) if count > 1 else towers[0]
            found = jnp.dot(row_bands[row_kind], both, preferred_element_type=jnp.float32)
            wide = own(first, count, slice(0, tall), window).reshape(count * tall, 3 * LANES)
            across = jnp.dot(wide, column_bands[column_kind], preferred_element_type=jnp.float32)
            for m in range(count):
                slopes_y[first + m] = found[:, m * LANES:(m + 1) * LANES]
                slopes_z[first + m] = across[m * tall:(m + 1) * tall]

        for r in range(0, tall, step):
            s = slice(r, r + step)
            low = end(0, s, cols)
            here = own(0, 1, s, cols)[0].astype(jnp.float32)
            clear, colour = None, None
            for first in range(0, layers, 2):
                pair = range(first, min(first + 2, layers))
                parts, picks, shades, tilts = [], [], [], []
                for layer in pair:
                    if layer + 1 < layers:
                        high = own(layer + 1, 1, s, cols)[0].astype(jnp.float32)
                    else:
                        high = end(1, s, cols)
                    position = jnp.clip(here * 2.5 + 7.5, 0.0, 15.0)
                    index = position.astype(jnp.int32)
                    whole = index.astype(jnp.float32)
                    parts.append(position - whole)
                    tilts.append([lookup(tilt, index) for tilt in tilts_of])
                    picks.append(choose(bins, whole))
                    gx = high - low
                    gy = slopes_y[layer, s, :]
                    gz = slopes_z[layer, s, :]
                    facing = jnp.abs(gx * lx + gy * ly + gz * lz)
                    square = gx * gx + gy * gy + gz * gz
                    shades.append(0.045 + facing * lax.rsqrt(jnp.maximum(square, 4.0)))
                    low, here = here, high
                pick = jnp.concatenate(picks, axis=1) if len(picks) > 1 else picks[0]
                found = jnp.dot(table[...], pick, preferred_element_type=jnp.float32)
                for m, layer in enumerate(pair):
                    lanes = slice(m * LANES, (m + 1) * LANES)
                    half_rows = rows_found * step
                    looked = [
                        found[k * step:(k + 1) * step, lanes]
                        + found[half_rows + k * step:half_rows + (k + 1) * step, lanes]
                        for k in range(rows_found)
                    ] + tilts[m]
                    tf = [looked[k] + parts[m] * looked[4 + k] for k in range(4)]
                    if layer == 0:
                        colour = [tf[k] * shades[m] for k in range(3)]
                        clear = 1.0 - tf[3]
                    else:
                        seen = shades[m] * clear
                        colour = [colour[k] + tf[k] * seen for k in range(3)]
                        clear = clear - clear * tf[3]
            for k in range(3):
                image[k, s, cols] = colour[k]
            image[3, s, cols] = 1.0 - clear
        return carry

    lax.fori_loop(0, width // LANES, strip, 0)

    @pl.when(sending)
    def _():
        send[0] = image[:, 0:unit, :]

    @pl.when(jnp.logical_not(sending))
    def _():
        keep[0] = image[:, 0:unit, :]


def merge_pair(ctl, mine, got, cols):
    theirs = [got[0, k, :, cols] for k in range(4)]
    ours = [mine[0, k, :, cols] for k in range(4)]
    behind = ctl[1] == 1
    front = [jnp.where(behind, t, o) for t, o in zip(theirs, ours)]
    back = [jnp.where(behind, o, t) for t, o in zip(theirs, ours)]
    return over(front, back)


def merge_kernel(ctl, *refs, members, places, unit):
    inputs, sends = refs[:2 * members], refs[2 * members:2 * members + places]
    image, tops = refs[2 * members + places:]
    turn = pl.program_id(0)
    width = image.shape[2]

    for n in range(members):
        @pl.when(lax.rem(turn, members) == n)
        def _(n=n):
            def put(at):
                cols = pl.ds(at, LANES)
                merged = merge_pair(ctl, inputs[2 * n], inputs[2 * n + 1], cols)
                for k in range(4):
                    image[k, :, cols] = merged[k]
                top = functools.reduce(jnp.maximum, merged)
                tops[0:8, cols] = jnp.max(top.reshape(unit // 8, 8, LANES), axis=0)

            each_strip(width, put)

    exponent = exponent_of(jnp.max(tops[0:8, :], axis=0, keepdims=True))
    tops[0:8, :] = jnp.broadcast_to(jnp.exp2(-exponent) * CODES, (8, width))
    row = jnp.broadcast_to(exponent, (8, width)).astype(jnp.int32)

    for k, send in enumerate(sends):
        @pl.when(turn // members == k)
        def _(send=send):
            def put(at):
                cols = pl.ds(at, LANES)
                factor = tops[0:1, cols]
                for k in range(2):
                    send[0, k * unit:(k + 1) * unit, cols] = pack(image[2 * k, :, cols], image[2 * k + 1, :, cols], factor)

            each_strip(width, put)
            send[0, 2 * unit:2 * unit + 8, :] = row


def gather_kernel(ctl, *refs, unit, blocks):
    parts, send, image = refs[:-2], refs[-2], refs[-1]
    width = image.shape[2]
    for me in range(len(parts)):
        @pl.when(ctl[0] == me)
        def _(me=me):
            def put(at):
                cols = pl.ds(at, LANES)
                total = None
                for j in range(len(parts)):
                    got = parts[me ^ j]
                    scale = scale_of(got[0, 2 * unit:2 * unit + 1, cols])
                    part = []
                    for k in range(2):
                        part += unpack(got[0, k * unit:(k + 1) * unit, cols], scale)
                    total = part if total is None else over(total, part)
                for k in range(4):
                    image[k, :, cols] = total[k]

            each_strip(width, put)

    part = width // blocks
    half = unit // 2
    for b in range(blocks):
        wide = jnp.concatenate([image[k, :, b * part:(b + 1) * part] for k in range(4)], axis=1)
        exponent = exponent_of(jnp.max(wide, axis=0, keepdims=True))
        factor = jnp.exp2(-exponent) * CODES
        send[b, 0, 8:8 + half, :] = pack(wide[:half], wide[half:], factor)
        send[b, 0, 0:8, :] = jnp.broadcast_to(exponent, (8, 4 * part)).astype(jnp.int32)


def compose_kernel(got, *refs, unit, blocks):
    out = refs[-1]
    part = out.shape[2]
    half = unit // 2
    total = None
    for b in range(blocks):
        scale = scale_of(got[b, 0, 0:1, :])
        wide = jnp.concatenate(unpack(got[b, 0, 8:8 + half, :], scale), axis=0)
        layer = [wide[:, k * part:(k + 1) * part] for k in range(4)]
        total = layer if total is None else over(total, layer)
    for k in range(4):
        out[k] = total[k]


def params():
    return pltpu.CompilerParams(vmem_limit_bytes=VMEM_LIMIT, dimension_semantics=("arbitrary",))


def unit_index(groups, units, bit):
    half = (groups // 2) * units

    def index(i, ctl):
        rest = lax.rem(i, half)
        parity = jnp.where(i < half, 1 - ctl[bit], ctl[bit])
        return (2 * (rest // units) + parity) * units + lax.rem(rest, units)

    return index


def split_outputs(groups, units, unit, width):
    half = (groups // 2) * units
    shapes = [
        jax.ShapeDtypeStruct((half, 4, unit, width), jnp.float32),
        jax.ShapeDtypeStruct((half, 4, unit, width), jnp.float32),
    ]
    specs = [
        pl.BlockSpec((1, 4, unit, width), lambda i, ctl: (jnp.minimum(i, half - 1), 0, 0, 0)),
        pl.BlockSpec((1, 4, unit, width), lambda i, ctl: (jnp.maximum(i - half, 0), 0, 0, 0)),
    ]
    return shapes, specs


def band(shape, dim, offset):
    place = lax.broadcasted_iota(jnp.int32, shape, dim) - lax.broadcasted_iota(jnp.int32, shape, 1 - dim) - offset
    return jnp.where(place == 1, 1.0, jnp.where(place == -1, -1.0, 0.0)).astype(jnp.bfloat16)


def render(ctl, light, table, slope, field, before, after, *, groups, units, unit, rows, offset, halo_at):
    layers, total, width = field.shape
    block = math.lcm(unit, 16)
    tall = padded_rows(unit)
    row_band = band((tall, tall + 32), 1, 16)
    place = lax.broadcasted_iota(jnp.int32, (tall, tall + 32), 1)
    top, bottom = place >= 16, place < 16 + unit
    row_bands = jnp.stack([
        jnp.where(jnp.logical_and(jnp.logical_or(top, kind % 2 == 0), jnp.logical_or(bottom, kind < 2)), row_band, 0)
        for kind in range(4)
    ])
    column_bands = jnp.stack([band((3 * LANES, LANES), 0, k * LANES) for k in range(3)])
    half = (groups // 2) * units
    index = unit_index(groups, units, 0)

    def start(i, ctl):
        unit_at = index(i, ctl)
        return (unit_at // units) * rows + offset + lax.rem(unit_at, units) * unit

    def main_at(i, ctl):
        return (0, start(i, ctl) // block, 0)

    def above_at(i, ctl):
        return (0, jnp.maximum(start(i, ctl) - 1, 0) // 16, 0)

    def below_at(i, ctl):
        return (0, jnp.minimum(start(i, ctl) + unit, total - 1) // 16, 0)

    shapes, specs = split_outputs(groups, units, unit, width)
    kernel = functools.partial(
        render_kernel, groups=groups, units=units, unit=unit, block=block, rows=rows, offset=offset, total=total
    )
    cells = layers * 2 * half * unit * width
    return pl.pallas_call(
        kernel,
        grid_spec=pltpu.PrefetchScalarGridSpec(
            num_scalar_prefetch=1,
            grid=(2 * half,),
            in_specs=[
                pl.BlockSpec(memory_space=pltpu.SMEM),
                pl.BlockSpec(table.shape, lambda i, ctl: (0, 0)),
                pl.BlockSpec(slope.shape, lambda i, ctl: (0, 0)),
                pl.BlockSpec((4, tall, tall + 32), lambda i, ctl: (0, 0, 0)),
                pl.BlockSpec((3, 3 * LANES, LANES), lambda i, ctl: (0, 0, 0)),
                pl.BlockSpec((layers, block, width), main_at),
                pl.BlockSpec((layers, 16, width), above_at),
                pl.BlockSpec((layers, 16, width), below_at),
                pl.BlockSpec((1, unit, width), lambda i, ctl: (index(i, ctl), halo_at, 0)),
                pl.BlockSpec((1, unit, width), lambda i, ctl: (index(i, ctl), halo_at, 0)),
            ],
            out_specs=specs,
            scratch_shapes=[
                pltpu.VMEM((layers, tall + 32, width) if block != unit else (1, 16, LANES), jnp.bfloat16),
                pltpu.VMEM((layers, tall, LANES), jnp.float32),
                pltpu.VMEM((layers, tall, LANES), jnp.float32),
                pltpu.VMEM((4, tall, width), jnp.float32),
                pltpu.VMEM((max(block, tall + 32), width) if block != unit else (8, LANES), jnp.float32),
                pltpu.VMEM((2, tall, width) if block != unit else (1, 8, LANES), jnp.float32),
            ],
        ),
        out_shape=shapes,
        compiler_params=params(),
        cost_estimate=pl.CostEstimate(flops=16384 * cells, bytes_accessed=6 * cells, transcendentals=cells),
        name="render",
    )(ctl, light, table, slope, row_bands, column_bands, field, field, field, before, after)


def merge(ctl, pairs, *, places, unit):
    members = len(pairs)
    width = pairs[0][0].shape[3]
    cells = 4 * places * members * unit * width

    def spec(k):
        return pl.BlockSpec(
            (1, 2 * unit + 8, width), lambda i, ctl: (jnp.clip(i - k * members, 0, members - 1), 0, 0)
        )

    return pl.pallas_call(
        functools.partial(merge_kernel, members=members, places=places, unit=unit),
        grid_spec=pltpu.PrefetchScalarGridSpec(
            num_scalar_prefetch=1,
            grid=(places * members,),
            in_specs=[pl.BlockSpec((1, 4, unit, width), lambda i, ctl: (ctl[0] ^ (i // members), 0, 0, 0))]
            * (2 * members),
            out_specs=[spec(k) for k in range(places)],
            scratch_shapes=[pltpu.VMEM((4, unit, width), jnp.float32), pltpu.VMEM((8, width), jnp.float32)],
        ),
        out_shape=[jax.ShapeDtypeStruct((members, 2 * unit + 8, width), jnp.int32)] * places,
        compiler_params=params(),
        cost_estimate=pl.CostEstimate(flops=32768 * cells, bytes_accessed=cells, transcendentals=0),
        name="merge",
    )(ctl, *[array for pair in pairs for array in pair])


def gather_parts(ctl, parts, *, units, unit, blocks):
    width = parts[0].shape[2]
    cells = 4 * units * unit * width
    return pl.pallas_call(
        functools.partial(gather_kernel, unit=unit, blocks=blocks),
        grid_spec=pltpu.PrefetchScalarGridSpec(
            num_scalar_prefetch=1,
            grid=(units,),
            in_specs=[pl.BlockSpec((1, 2 * unit + 8, width), lambda i, ctl: (i, 0, 0))] * len(parts),
            out_specs=pl.BlockSpec((blocks, 1, unit // 2 + 8, 4 * width // blocks), lambda i, ctl: (0, i, 0, 0)),
            scratch_shapes=[pltpu.VMEM((4, unit, width), jnp.float32)],
        ),
        out_shape=jax.ShapeDtypeStruct((blocks, units, unit // 2 + 8, 4 * width // blocks), jnp.int32),
        compiler_params=params(),
        cost_estimate=pl.CostEstimate(flops=131072 * cells, bytes_accessed=cells, transcendentals=0),
        name="gather_parts",
    )(ctl, *parts)


def compose(got, so_far, *, unit, first, rows):
    blocks, units = got.shape[:2]
    part = got.shape[3] // 4
    cells = 4 * units * unit * part * blocks
    operands = [got]
    in_specs = [pl.BlockSpec((blocks, 1, unit // 2 + 8, 4 * part), lambda i: (0, i, 0, 0))]
    if so_far is not None:
        operands.append(so_far)
        in_specs.append(pl.BlockSpec(memory_space=pl.ANY))
    return pl.pallas_call(
        functools.partial(compose_kernel, unit=unit, blocks=blocks),
        grid=(units,),
        in_specs=in_specs,
        out_specs=pl.BlockSpec((4, unit, part), lambda i: (0, first + i, 0)),
        out_shape=jax.ShapeDtypeStruct((4, rows, part), jnp.float32),
        input_output_aliases={1: 0} if so_far is not None else {},
        compiler_params=params(),
        cost_estimate=pl.CostEstimate(flops=32768 * cells, bytes_accessed=cells, transcendentals=0),
        name="compose",
    )(*operands)


def per_device(field, transfer, bin_order, light_angles):
    tiles = lax.axis_size("tile")
    blocks = lax.axis_size("depth")
    devices = tiles * blocks
    layers, total, width = field.shape
    rows = total // tiles
    unit = unit_rows(rows)
    places = tiles // 2

    table = jnp.take(transfer, bin_order, axis=1)
    table = table * jnp.array([[1.0], [1.0], [1.0], [0.01]], jnp.float32)
    bins = table.shape[1]
    slope = jnp.concatenate([table[:, 1:] - table[:, :-1], jnp.zeros_like(table[:, :1])], axis=1)
    table = jnp.concatenate([table, slope[:ON_MATRIX - 4]], axis=0)
    slope = jnp.pad(slope, ((0, 4), (0, LANES - bins)))
    coarse = lax.reduce_precision(table, exponent_bits=8, mantissa_bits=7)
    table = jnp.concatenate([coarse, table - coarse], axis=0)
    spread = jnp.eye(16, dtype=jnp.float32)
    table = (table[:, None, :, None] * spread[None, :, None, :]).reshape(2 * ON_MATRIX * 16, bins * 16)
    table = table.astype(jnp.bfloat16)
    azimuth, polar = light_angles[0], light_angles[1]
    light = 0.105 * jnp.stack(
        [jnp.cos(azimuth) * jnp.sin(polar), jnp.sin(azimuth) * jnp.sin(polar), jnp.cos(polar)]
    )

    tile = lax.axis_index("tile")
    core, place = (tile & 1).astype(jnp.int32), (tile >> 1).astype(jnp.int32)
    render_control = jnp.stack([core, core])
    merge_control = jnp.stack([place, core])
    up = [(i, i + 1) for i in range(devices - 1)]
    down = [(j, i) for i, j in up]
    both = ("depth", "tile")

    count = rows // unit
    starts = [n * unit for n in range(count)]

    def cut(layer, first, stop):
        part = field.reshape(layers, tiles, rows, width)[layer:layer + 1, :, first * unit:stop * unit]
        return part.reshape(tiles, (stop - first) * unit, width)

    halos = []
    for first, stop in [(0, 1), (1, count)][:count]:
        ends = (cut(layers - 1, first, stop), cut(0, first, stop))
        if halos:
            ends, _ = lax.optimization_barrier((ends, halos[0][:2]))
        pair = (lax.ppermute(ends[0], both, up), lax.ppermute(ends[1], both, down))
        halos += [pair + (n - first,) for n in range(first, stop)]

    def exchange(send, distance):
        return lax.ppermute(send, "tile", [(i, i ^ distance) for i in range(tiles)])

    chain = []
    waits = []

    def after_last(control):
        if chain:
            control, _, _ = lax.optimization_barrier((control, chain[-1], list(waits)))
            waits.clear()
        return control

    state = [None] * count

    def start_chunk(n):
        before, after, at = halos[n]
        send, keep = render(
            after_last(render_control), light, table, slope, field, before, after,
            groups=tiles, units=1, unit=unit, rows=rows, offset=starts[n], halo_at=at,
        )
        chain.append(send)
        state[n] = (keep, exchange(send, 1))

    def merge_group(members):
        sends = merge(after_last(merge_control), [state[n] for n in members], places=places, unit=unit)
        chain.append(sends[-1])
        return [sends[0]] + [exchange(sends[k], 2 * k) for k in range(1, places)]

    def block_group(members, parts):
        send = gather_parts(after_last(merge_control), parts, units=len(members), unit=unit, blocks=blocks)
        chain.append(send)
        return lax.all_to_all(send, "depth", split_axis=0, concat_axis=0, tiled=True)

    early, late = list(range(count - 1)), [count - 1]
    results = []
    if early:
        for n in early:
            start_chunk(n)
        early_parts = merge_group(early)
        start_chunk(count - 1)
        waits.extend(early_parts)
        results.append(block_group(early, early_parts))
    else:
        start_chunk(count - 1)
    results.append(block_group(late, merge_group(late)))
    final = None
    done = 0
    for result in results:
        final = compose(result, final, unit=unit, first=done, rows=rows)
        done += result.shape[1]
    return final


def solution(mesh):
    in_specs = (P(("depth", "tile"), None, None), P(), P(), P())
    out_specs = P(None, "tile", "depth")
    return jax.shard_map(
        per_device, mesh=mesh, in_specs=in_specs, out_specs=out_specs, check_vma=False
    )
```

```python
import functools
import math

import jax
import jax.numpy as jnp
from jax import lax
from jax.experimental import pallas as pl
from jax.experimental.pallas import tpu as pltpu
from jax.sharding import PartitionSpec as P

LANES = 128
CODES = 32700.0
ON_MATRIX = 4
VMEM_LIMIT = 56 * 1024 * 1024


def unit_rows(rows):
    return 48 if rows % 48 == 0 else rows


def exponent_of(top):
    return jnp.ceil(jnp.log2(jnp.maximum(top, 1e-30)))


def pack(low, high, factor):
    low = (low * factor + 0.5).astype(jnp.int32)
    high = (high * factor + 0.5).astype(jnp.int32)
    return low | (high << 16)


def unpack(word, scale):
    return (word & 0xFFFF).astype(jnp.float32) * scale, (word >> 16).astype(jnp.float32) * scale


def scale_of(row):
    return jnp.exp2(row.astype(jnp.float32)) * (1.0 / CODES)


def over(front, back):
    clear = 1.0 - front[3]
    return [f + clear * b for f, b in zip(front, back)]


def lookup(table, index):
    numbers = lax.GatherDimensionNumbers(
        offset_dims=(), collapsed_slice_dims=(1,), start_index_map=(1,),
        operand_batching_dims=(0,), start_indices_batching_dims=(0,),
    )
    return lax.gather(
        table, index[..., None], numbers, slice_sizes=(1, 1), mode=lax.GatherScatterMode.PROMISE_IN_BOUNDS
    )


def one_hot(x, levels):
    rows = []
    for j in range(levels):
        if j == 0:
            row = 1 - x
        elif j == levels - 1:
            row = x - (levels - 2)
        else:
            row = jnp.minimum(x if j == 1 else x - (j - 1), (j + 1) - x)
        rows.append(jnp.maximum(row, 0))
    return rows


def choose(bins, index, whole):
    high = (index >> 2).astype(jnp.float32)
    low = (whole - 4.0 * high).astype(jnp.bfloat16)
    highs, lows = one_hot(high.astype(jnp.bfloat16), bins // 4), one_hot(low, 4)
    return jnp.concatenate([h * l for h in highs for l in lows], axis=0)


def padded_rows(unit):
    return -(-unit // 16) * 16


def each_strip(width, body):
    strips = width // LANES
    together = 3 if strips % 3 == 0 else 1

    def step(c, carry):
        for k in range(together):
            body(pl.multiple_of((c * together + k) * LANES, LANES))
        return carry

    lax.fori_loop(0, strips // together, step, 0)


def render_kernel(ctl, light, table, slope, row_bands, column_bands, main, above, below, before, after, send, keep, cells, slopes_y, slopes_z, image, stage, ends, *, groups, units, unit, block, rows, offset, total):
    i = pl.program_id(0)
    half = (groups // 2) * units
    rest = lax.rem(i, half)
    sending = i < half
    parity = jnp.where(sending, 1 - ctl[0], ctl[0])
    group = 2 * (rest // units) + parity
    start = group * rows + offset + lax.rem(rest, units) * unit
    layers = main.shape[0]
    width = main.shape[2]
    tall = padded_rows(unit)
    aligned = block == unit

    def load_layer(layer, carry):
        shift = pl.multiple_of(lax.rem(start, block), 8)
        stage[0:block, :] = main[layer].astype(jnp.float32)
        body = stage[pl.ds(shift, unit), :]
        up = above[layer].astype(jnp.float32)
        down = below[layer].astype(jnp.float32)
        up = jnp.where(lax.rem(start, 16) == 0, up[8:16], up[0:8])
        down = jnp.where(lax.rem(start + unit, 16) == 0, down[0:8], down[8:16])
        stage[0:8, :] = jnp.zeros((8, width), jnp.float32)
        stage[8:16, :] = up
        stage[16:16 + unit, :] = body
        stage[16 + unit:24 + unit, :] = down
        stage[24 + unit:tall + 32, :] = jnp.zeros((tall + 8 - unit, width), jnp.float32)
        cells[layer, :, :] = stage[0:tall + 32, :].astype(jnp.bfloat16)
        return carry

    if not aligned:
        lax.fori_loop(0, layers, load_layer, 0)
        ends[0, 0:unit, :] = before[0].astype(jnp.float32)
        ends[1, 0:unit, :] = after[0].astype(jnp.float32)

    def own(first, count, s, cols):
        if aligned:
            return main[first:first + count, s, cols]
        return cells[first:first + count, 16 + s.start:16 + s.stop, cols]

    def tower(layer, cols):
        if aligned:
            return jnp.concatenate([above[layer, :, cols], main[layer, :, cols], below[layer, :, cols]], axis=0)
        return cells[layer, :, cols]

    def end(which, s, cols):
        if aligned:
            return (before, after)[which][0, s, cols].astype(jnp.float32)
        return ends[which, s, cols]

    lx, ly, lz = light[0], light[1], light[2]
    step = 16
    bins = table.shape[1] // step
    rows_found = table.shape[0] // (2 * step)
    tilts_of = [jnp.broadcast_to(slope[k:k + 1, :], (step, LANES)) for k in range(rows_found - 4, 4)]
    row_kind = jnp.where(start == 0, 1, 0) + jnp.where(start + unit == total, 2, 0)

    def strip(c, carry):
        at = pl.multiple_of(c * LANES, LANES)
        cols = pl.ds(at, LANES)
        window = pl.ds(pl.multiple_of(jnp.clip(at - LANES, 0, width - 3 * LANES), LANES), 3 * LANES)
        column_kind = jnp.where(at == 0, 0, jnp.where(at == width - LANES, 2, 1))
        for first in range(0, layers, 2):
            count = min(2, layers - first)
            towers = [tower(first + m, cols) for m in range(count)]
            both = jnp.concatenate(towers, axis=1) if count > 1 else towers[0]
            found = jnp.dot(row_bands[row_kind], both, preferred_element_type=jnp.float32)
            wide = own(first, count, slice(0, tall), window).reshape(count * tall, 3 * LANES)
            across = jnp.dot(wide, column_bands[column_kind], preferred_element_type=jnp.float32)
            for m in range(count):
                slopes_y[first + m] = found[:, m * LANES:(m + 1) * LANES]
                slopes_z[first + m] = across[m * tall:(m + 1) * tall]

        for r in range(0, tall, step):
            s = slice(r, r + step)
            low = end(0, s, cols)
            here = own(0, 1, s, cols)[0].astype(jnp.float32)
            clear, colour = None, None
            for first in range(0, layers, 2):
                pair = range(first, min(first + 2, layers))
                parts, picks, shades, tilts = [], [], [], []
                for layer in pair:
                    if layer + 1 < layers:
                        high = own(layer + 1, 1, s, cols)[0].astype(jnp.float32)
                    else:
                        high = end(1, s, cols)
                    position = jnp.clip(here * 2.5 + 7.5, 0.0, 15.0)
                    index = position.astype(jnp.int32)
                    whole = index.astype(jnp.float32)
                    parts.append(position - whole)
                    tilts.append([lookup(tilt, index) for tilt in tilts_of])
                    picks.append(choose(bins, index, whole))
                    gx = high - low
                    gy = slopes_y[layer, s, :]
                    gz = slopes_z[layer, s, :]
                    facing = jnp.abs(gx * lx + gy * ly + gz * lz)
                    square = gx * gx + gy * gy + gz * gz
                    shades.append(0.045 + facing * lax.rsqrt(jnp.maximum(square, 4.0)))
                    low, here = here, high
                pick = jnp.concatenate(picks, axis=1) if len(picks) > 1 else picks[0]
                found = jnp.dot(table[...], pick, preferred_element_type=jnp.float32)
                for m, layer in enumerate(pair):
                    lanes = slice(m * LANES, (m + 1) * LANES)
                    half_rows = rows_found * step
                    looked = [
                        found[k * step:(k + 1) * step, lanes]
                        + found[half_rows + k * step:half_rows + (k + 1) * step, lanes]
                        for k in range(rows_found)
                    ] + tilts[m]
                    tf = [looked[k] + parts[m] * looked[4 + k] for k in range(4)]
                    if layer == 0:
                        colour = [tf[k] * shades[m] for k in range(3)]
                        clear = 1.0 - tf[3]
                    else:
                        seen = shades[m] * clear
                        colour = [colour[k] + tf[k] * seen for k in range(3)]
                        clear = clear - clear * tf[3]
            for k in range(3):
                image[k, s, cols] = colour[k]
            image[3, s, cols] = 1.0 - clear
        return carry

    lax.fori_loop(0, width // LANES, strip, 0)

    @pl.when(sending)
    def _():
        send[0] = image[:, 0:unit, :]

    @pl.when(jnp.logical_not(sending))
    def _():
        keep[0] = image[:, 0:unit, :]


def merge_pair(ctl, mine, got, cols):
    theirs = [got[0, k, :, cols] for k in range(4)]
    ours = [mine[0, k, :, cols] for k in range(4)]
    behind = ctl[1] == 1
    front = [jnp.where(behind, t, o) for t, o in zip(theirs, ours)]
    back = [jnp.where(behind, o, t) for t, o in zip(theirs, ours)]
    return over(front, back)


def merge_kernel(ctl, *refs, members, places, unit):
    inputs, sends = refs[:2 * members], refs[2 * members:2 * members + places]
    image, tops = refs[2 * members + places:]
    turn = pl.program_id(0)
    width = image.shape[2]

    for n in range(members):
        @pl.when(lax.rem(turn, members) == n)
        def _(n=n):
            def put(at):
                cols = pl.ds(at, LANES)
                merged = merge_pair(ctl, inputs[2 * n], inputs[2 * n + 1], cols)
                for k in range(4):
                    image[k, :, cols] = merged[k]
                top = functools.reduce(jnp.maximum, merged)
                tops[0:8, cols] = jnp.max(top.reshape(unit // 8, 8, LANES), axis=0)

            each_strip(width, put)

    exponent = exponent_of(jnp.max(tops[0:8, :], axis=0, keepdims=True))
    tops[0:8, :] = jnp.broadcast_to(jnp.exp2(-exponent) * CODES, (8, width))
    row = jnp.broadcast_to(exponent, (8, width)).astype(jnp.int32)

    for k, send in enumerate(sends):
        @pl.when(turn // members == k)
        def _(send=send):
            def put(at):
                cols = pl.ds(at, LANES)
                factor = tops[0:1, cols]
                for k in range(2):
                    send[0, k * unit:(k + 1) * unit, cols] = pack(image[2 * k, :, cols], image[2 * k + 1, :, cols], factor)

            each_strip(width, put)
            send[0, 2 * unit:2 * unit + 8, :] = row


def gather_kernel(ctl, *refs, unit, blocks):
    parts, send, image = refs[:-2], refs[-2], refs[-1]
    width = image.shape[2]
    for me in range(len(parts)):
        @pl.when(ctl[0] == me)
        def _(me=me):
            def put(at):
                cols = pl.ds(at, LANES)
                total = None
                for j in range(len(parts)):
                    got = parts[me ^ j]
                    scale = scale_of(got[0, 2 * unit:2 * unit + 1, cols])
                    part = []
                    for k in range(2):
                        part += unpack(got[0, k * unit:(k + 1) * unit, cols], scale)
                    total = part if total is None else over(total, part)
                for k in range(4):
                    image[k, :, cols] = total[k]

            each_strip(width, put)

    part = width // blocks
    half = unit // 2
    for b in range(blocks):
        wide = jnp.concatenate([image[k, :, b * part:(b + 1) * part] for k in range(4)], axis=1)
        exponent = exponent_of(jnp.max(wide, axis=0, keepdims=True))
        factor = jnp.exp2(-exponent) * CODES
        send[b, 0, 8:8 + half, :] = pack(wide[:half], wide[half:], factor)
        send[b, 0, 0:8, :] = jnp.broadcast_to(exponent, (8, 4 * part)).astype(jnp.int32)


def compose_kernel(got, *refs, unit, blocks):
    out = refs[-1]
    part = out.shape[2]
    half = unit // 2
    total = None
    for b in range(blocks):
        scale = scale_of(got[b, 0, 0:1, :])
        wide = jnp.concatenate(unpack(got[b, 0, 8:8 + half, :], scale), axis=0)
        layer = [wide[:, k * part:(k + 1) * part] for k in range(4)]
        total = layer if total is None else over(total, layer)
    for k in range(4):
        out[k] = total[k]


def params():
    return pltpu.CompilerParams(vmem_limit_bytes=VMEM_LIMIT, dimension_semantics=("arbitrary",))


def unit_index(groups, units, bit):
    half = (groups // 2) * units

    def index(i, ctl):
        rest = lax.rem(i, half)
        parity = jnp.where(i < half, 1 - ctl[bit], ctl[bit])
        return (2 * (rest // units) + parity) * units + lax.rem(rest, units)

    return index


def split_outputs(groups, units, unit, width):
    half = (groups // 2) * units
    shapes = [
        jax.ShapeDtypeStruct((half, 4, unit, width), jnp.float32),
        jax.ShapeDtypeStruct((half, 4, unit, width), jnp.float32),
    ]
    specs = [
        pl.BlockSpec((1, 4, unit, width), lambda i, ctl: (jnp.minimum(i, half - 1), 0, 0, 0)),
        pl.BlockSpec((1, 4, unit, width), lambda i, ctl: (jnp.maximum(i - half, 0), 0, 0, 0)),
    ]
    return shapes, specs


def band(shape, dim, offset):
    place = lax.broadcasted_iota(jnp.int32, shape, dim) - lax.broadcasted_iota(jnp.int32, shape, 1 - dim) - offset
    return jnp.where(place == 1, 1.0, jnp.where(place == -1, -1.0, 0.0)).astype(jnp.bfloat16)


def render(ctl, light, table, slope, field, before, after, *, groups, units, unit, rows, offset, halo_at):
    layers, total, width = field.shape
    block = math.lcm(unit, 16)
    tall = padded_rows(unit)
    row_band = band((tall, tall + 32), 1, 16)
    place = lax.broadcasted_iota(jnp.int32, (tall, tall + 32), 1)
    top, bottom = place >= 16, place < 16 + unit
    row_bands = jnp.stack([
        jnp.where(jnp.logical_and(jnp.logical_or(top, kind % 2 == 0), jnp.logical_or(bottom, kind < 2)), row_band, 0)
        for kind in range(4)
    ])
    column_bands = jnp.stack([band((3 * LANES, LANES), 0, k * LANES) for k in range(3)])
    half = (groups // 2) * units
    index = unit_index(groups, units, 0)

    def start(i, ctl):
        unit_at = index(i, ctl)
        return (unit_at // units) * rows + offset + lax.rem(unit_at, units) * unit

    def main_at(i, ctl):
        return (0, start(i, ctl) // block, 0)

    def above_at(i, ctl):
        return (0, jnp.maximum(start(i, ctl) - 1, 0) // 16, 0)

    def below_at(i, ctl):
        return (0, jnp.minimum(start(i, ctl) + unit, total - 1) // 16, 0)

    shapes, specs = split_outputs(groups, units, unit, width)
    kernel = functools.partial(
        render_kernel, groups=groups, units=units, unit=unit, block=block, rows=rows, offset=offset, total=total
    )
    cells = layers * 2 * half * unit * width
    return pl.pallas_call(
        kernel,
        grid_spec=pltpu.PrefetchScalarGridSpec(
            num_scalar_prefetch=1,
            grid=(2 * half,),
            in_specs=[
                pl.BlockSpec(memory_space=pltpu.SMEM),
                pl.BlockSpec(table.shape, lambda i, ctl: (0, 0)),
                pl.BlockSpec(slope.shape, lambda i, ctl: (0, 0)),
                pl.BlockSpec((4, tall, tall + 32), lambda i, ctl: (0, 0, 0)),
                pl.BlockSpec((3, 3 * LANES, LANES), lambda i, ctl: (0, 0, 0)),
                pl.BlockSpec((layers, block, width), main_at),
                pl.BlockSpec((layers, 16, width), above_at),
                pl.BlockSpec((layers, 16, width), below_at),
                pl.BlockSpec((1, unit, width), lambda i, ctl: (index(i, ctl), halo_at, 0)),
                pl.BlockSpec((1, unit, width), lambda i, ctl: (index(i, ctl), halo_at, 0)),
            ],
            out_specs=specs,
            scratch_shapes=[
                pltpu.VMEM((layers, tall + 32, width) if block != unit else (1, 16, LANES), jnp.bfloat16),
                pltpu.VMEM((layers, tall, LANES), jnp.float32),
                pltpu.VMEM((layers, tall, LANES), jnp.float32),
                pltpu.VMEM((4, tall, width), jnp.float32),
                pltpu.VMEM((max(block, tall + 32), width) if block != unit else (8, LANES), jnp.float32),
                pltpu.VMEM((2, tall, width) if block != unit else (1, 8, LANES), jnp.float32),
            ],
        ),
        out_shape=shapes,
        compiler_params=params(),
        cost_estimate=pl.CostEstimate(flops=16384 * cells, bytes_accessed=6 * cells, transcendentals=cells),
        name="render",
    )(ctl, light, table, slope, row_bands, column_bands, field, field, field, before, after)


def merge(ctl, pairs, *, places, unit):
    members = len(pairs)
    width = pairs[0][0].shape[3]
    cells = 4 * places * members * unit * width

    def spec(k):
        return pl.BlockSpec(
            (1, 2 * unit + 8, width), lambda i, ctl: (jnp.clip(i - k * members, 0, members - 1), 0, 0)
        )

    return pl.pallas_call(
        functools.partial(merge_kernel, members=members, places=places, unit=unit),
        grid_spec=pltpu.PrefetchScalarGridSpec(
            num_scalar_prefetch=1,
            grid=(places * members,),
            in_specs=[pl.BlockSpec((1, 4, unit, width), lambda i, ctl: (ctl[0] ^ (i // members), 0, 0, 0))]
            * (2 * members),
            out_specs=[spec(k) for k in range(places)],
            scratch_shapes=[pltpu.VMEM((4, unit, width), jnp.float32), pltpu.VMEM((8, width), jnp.float32)],
        ),
        out_shape=[jax.ShapeDtypeStruct((members, 2 * unit + 8, width), jnp.int32)] * places,
        compiler_params=params(),
        cost_estimate=pl.CostEstimate(flops=32768 * cells, bytes_accessed=cells, transcendentals=0),
        name="merge",
    )(ctl, *[array for pair in pairs for array in pair])


def gather_parts(ctl, parts, *, units, unit, blocks):
    width = parts[0].shape[2]
    cells = 4 * units * unit * width
    return pl.pallas_call(
        functools.partial(gather_kernel, unit=unit, blocks=blocks),
        grid_spec=pltpu.PrefetchScalarGridSpec(
            num_scalar_prefetch=1,
            grid=(units,),
            in_specs=[pl.BlockSpec((1, 2 * unit + 8, width), lambda i, ctl: (i, 0, 0))] * len(parts),
            out_specs=pl.BlockSpec((blocks, 1, unit // 2 + 8, 4 * width // blocks), lambda i, ctl: (0, i, 0, 0)),
            scratch_shapes=[pltpu.VMEM((4, unit, width), jnp.float32)],
        ),
        out_shape=jax.ShapeDtypeStruct((blocks, units, unit // 2 + 8, 4 * width // blocks), jnp.int32),
        compiler_params=params(),
        cost_estimate=pl.CostEstimate(flops=131072 * cells, bytes_accessed=cells, transcendentals=0),
        name="gather_parts",
    )(ctl, *parts)


def compose(got, so_far, *, unit, first, rows):
    blocks, units = got.shape[:2]
    part = got.shape[3] // 4
    cells = 4 * units * unit * part * blocks
    operands = [got]
    in_specs = [pl.BlockSpec((blocks, 1, unit // 2 + 8, 4 * part), lambda i: (0, i, 0, 0))]
    if so_far is not None:
        operands.append(so_far)
        in_specs.append(pl.BlockSpec(memory_space=pl.ANY))
    return pl.pallas_call(
        functools.partial(compose_kernel, unit=unit, blocks=blocks),
        grid=(units,),
        in_specs=in_specs,
        out_specs=pl.BlockSpec((4, unit, part), lambda i: (0, first + i, 0)),
        out_shape=jax.ShapeDtypeStruct((4, rows, part), jnp.float32),
        input_output_aliases={1: 0} if so_far is not None else {},
        compiler_params=params(),
        cost_estimate=pl.CostEstimate(flops=32768 * cells, bytes_accessed=cells, transcendentals=0),
        name="compose",
    )(*operands)


def per_device(field, transfer, bin_order, light_angles):
    tiles = lax.axis_size("tile")
    blocks = lax.axis_size("depth")
    devices = tiles * blocks
    layers, total, width = field.shape
    rows = total // tiles
    unit = unit_rows(rows)
    places = tiles // 2

    table = jnp.take(transfer, bin_order, axis=1)
    table = table * jnp.array([[1.0], [1.0], [1.0], [0.01]], jnp.float32)
    bins = table.shape[1]
    slope = jnp.concatenate([table[:, 1:] - table[:, :-1], jnp.zeros_like(table[:, :1])], axis=1)
    table = jnp.concatenate([table, slope[:ON_MATRIX - 4]], axis=0)
    slope = jnp.pad(slope, ((0, 4), (0, LANES - bins)))
    coarse = lax.reduce_precision(table, exponent_bits=8, mantissa_bits=7)
    table = jnp.concatenate([coarse, table - coarse], axis=0)
    spread = jnp.eye(16, dtype=jnp.float32)
    table = (table[:, None, :, None] * spread[None, :, None, :]).reshape(2 * ON_MATRIX * 16, bins * 16)
    table = table.astype(jnp.bfloat16)
    azimuth, polar = light_angles[0], light_angles[1]
    light = 0.105 * jnp.stack(
        [jnp.cos(azimuth) * jnp.sin(polar), jnp.sin(azimuth) * jnp.sin(polar), jnp.cos(polar)]
    )

    tile = lax.axis_index("tile")
    core, place = (tile & 1).astype(jnp.int32), (tile >> 1).astype(jnp.int32)
    render_control = jnp.stack([core, core])
    merge_control = jnp.stack([place, core])
    up = [(i, i + 1) for i in range(devices - 1)]
    down = [(j, i) for i, j in up]
    both = ("depth", "tile")

    count = rows // unit
    starts = [n * unit for n in range(count)]

    def cut(layer, first, stop):
        part = field.reshape(layers, tiles, rows, width)[layer:layer + 1, :, first * unit:stop * unit]
        return part.reshape(tiles, (stop - first) * unit, width)

    halos = []
    for first, stop in [(0, 1), (1, count)][:count]:
        ends = (cut(layers - 1, first, stop), cut(0, first, stop))
        if halos:
            ends, _ = lax.optimization_barrier((ends, halos[0][:2]))
        pair = (lax.ppermute(ends[0], both, up), lax.ppermute(ends[1], both, down))
        halos += [pair + (n - first,) for n in range(first, stop)]

    def exchange(send, distance):
        return lax.ppermute(send, "tile", [(i, i ^ distance) for i in range(tiles)])

    chain = []
    waits = []

    def after_last(control):
        if chain:
            control, _, _ = lax.optimization_barrier((control, chain[-1], list(waits)))
            waits.clear()
        return control

    state = [None] * count

    def start_chunk(n):
        before, after, at = halos[n]
        send, keep = render(
            after_last(render_control), light, table, slope, field, before, after,
            groups=tiles, units=1, unit=unit, rows=rows, offset=starts[n], halo_at=at,
        )
        chain.append(send)
        state[n] = (keep, exchange(send, 1))

    def merge_group(members):
        sends = merge(after_last(merge_control), [state[n] for n in members], places=places, unit=unit)
        chain.append(sends[-1])
        return [sends[0]] + [exchange(sends[k], 2 * k) for k in range(1, places)]

    def block_group(members, parts):
        send = gather_parts(after_last(merge_control), parts, units=len(members), unit=unit, blocks=blocks)
        chain.append(send)
        return lax.all_to_all(send, "depth", split_axis=0, concat_axis=0, tiled=True)

    early, late = list(range(count - 1)), [count - 1]
    results = []
    if early:
        for n in early:
            start_chunk(n)
        early_parts = merge_group(early)
        start_chunk(count - 1)
        waits.extend(early_parts)
        results.append(block_group(early, early_parts))
    else:
        start_chunk(count - 1)
    results.append(block_group(late, merge_group(late)))
    final = None
    done = 0
    for result in results:
        final = compose(result, final, unit=unit, first=done, rows=rows)
        done += result.shape[1]
    return final


def solution(mesh):
    in_specs = (P(("depth", "tile"), None, None), P(), P(), P())
    out_specs = P(None, "tile", "depth")
    return jax.shard_map(
        per_device, mesh=mesh, in_specs=in_specs, out_specs=out_specs, check_vma=False
    )
```

```python
import functools
import math

import jax
import jax.numpy as jnp
from jax import lax
from jax.experimental import pallas as pl
from jax.experimental.pallas import tpu as pltpu
from jax.sharding import PartitionSpec as P

LANES = 128
CODES = 32700.0
ON_MATRIX = 4
VMEM_LIMIT = 56 * 1024 * 1024


def unit_rows(rows):
    return 48 if rows % 48 == 0 else rows


def exponent_of(top):
    return jnp.ceil(jnp.log2(jnp.maximum(top, 1e-30)))


def pack(low, high, factor):
    low = (low * factor + 0.5).astype(jnp.int32)
    high = (high * factor + 0.5).astype(jnp.int32)
    return low | (high << 16)


def unpack(word, scale):
    return (word & 0xFFFF).astype(jnp.float32) * scale, (word >> 16).astype(jnp.float32) * scale


def scale_of(row):
    return jnp.exp2(row.astype(jnp.float32)) * (1.0 / CODES)


def over(front, back):
    clear = 1.0 - front[3]
    return [f + clear * b for f, b in zip(front, back)]


def lookup(table, index):
    numbers = lax.GatherDimensionNumbers(
        offset_dims=(), collapsed_slice_dims=(1,), start_index_map=(1,),
        operand_batching_dims=(0,), start_indices_batching_dims=(0,),
    )
    return lax.gather(
        table, index[..., None], numbers, slice_sizes=(1, 1), mode=lax.GatherScatterMode.PROMISE_IN_BOUNDS
    )


def choose(bins, whole):
    place = whole.astype(jnp.bfloat16)
    one, zero = jnp.ones_like(place), jnp.zeros_like(place)
    return jnp.concatenate([jnp.where(place == k, one, zero) for k in range(bins)], axis=0)


def padded_rows(unit):
    return -(-unit // 16) * 16


def each_strip(width, body):
    strips = width // LANES
    together = 3 if strips % 3 == 0 else 1

    def step(c, carry):
        for k in range(together):
            body(pl.multiple_of((c * together + k) * LANES, LANES))
        return carry

    lax.fori_loop(0, strips // together, step, 0)


def render_kernel(ctl, light, table, slope, row_bands, column_bands, main, above, below, before, after, send, keep, cells, slopes_y, slopes_z, image, stage, ends, *, groups, units, unit, block, rows, offset, total):
    i = pl.program_id(0)
    half = (groups // 2) * units
    rest = lax.rem(i, half)
    sending = i < half
    parity = jnp.where(sending, 1 - ctl[0], ctl[0])
    group = 2 * (rest // units) + parity
    start = group * rows + offset + lax.rem(rest, units) * unit
    layers = main.shape[0]
    width = main.shape[2]
    tall = padded_rows(unit)
    aligned = block == unit

    def load_layer(layer, carry):
        shift = pl.multiple_of(lax.rem(start, block), 8)
        stage[0:block, :] = main[layer].astype(jnp.float32)
        body = stage[pl.ds(shift, unit), :]
        up = above[layer].astype(jnp.float32)
        down = below[layer].astype(jnp.float32)
        up = jnp.where(lax.rem(start, 16) == 0, up[8:16], up[0:8])
        down = jnp.where(lax.rem(start + unit, 16) == 0, down[0:8], down[8:16])
        stage[0:8, :] = jnp.zeros((8, width), jnp.float32)
        stage[8:16, :] = up
        stage[16:16 + unit, :] = body
        stage[16 + unit:24 + unit, :] = down
        stage[24 + unit:tall + 32, :] = jnp.zeros((tall + 8 - unit, width), jnp.float32)
        cells[layer, :, :] = stage[0:tall + 32, :].astype(jnp.bfloat16)
        return carry

    if not aligned:
        lax.fori_loop(0, layers, load_layer, 0)
        ends[0, 0:unit, :] = before[0].astype(jnp.float32)
        ends[1, 0:unit, :] = after[0].astype(jnp.float32)

    def own(first, count, s, cols):
        if aligned:
            return main[first:first + count, s, cols]
        return cells[first:first + count, 16 + s.start:16 + s.stop, cols]

    def tower(layer, cols):
        if aligned:
            return jnp.concatenate([above[layer, :, cols], main[layer, :, cols], below[layer, :, cols]], axis=0)
        return cells[layer, :, cols]

    def end(which, s, cols):
        if aligned:
            return (before, after)[which][0, s, cols].astype(jnp.float32)
        return ends[which, s, cols]

    lx, ly, lz = light[0], light[1], light[2]
    step = 16
    bins = table.shape[1] // (2 * step)
    rows_found = table.shape[0] // step
    tilts_of = [jnp.broadcast_to(slope[k:k + 1, :], (step, LANES)) for k in range(rows_found - 4, 4)]
    row_kind = jnp.where(start == 0, 1, 0) + jnp.where(start + unit == total, 2, 0)

    def strip(c, carry):
        at = pl.multiple_of(c * LANES, LANES)
        cols = pl.ds(at, LANES)
        window = pl.ds(pl.multiple_of(jnp.clip(at - LANES, 0, width - 3 * LANES), LANES), 3 * LANES)
        column_kind = jnp.where(at == 0, 0, jnp.where(at == width - LANES, 2, 1))
        for first in range(0, layers, 2):
            count = min(2, layers - first)
            towers = [tower(first + m, cols) for m in range(count)]
            both = jnp.concatenate(towers, axis=1) if count > 1 else towers[0]
            found = jnp.dot(row_bands[row_kind], both, preferred_element_type=jnp.float32)
            wide = own(first, count, slice(0, tall), window).reshape(count * tall, 3 * LANES)
            across = jnp.dot(wide, column_bands[column_kind], preferred_element_type=jnp.float32)
            for m in range(count):
                slopes_y[first + m] = found[:, m * LANES:(m + 1) * LANES]
                slopes_z[first + m] = across[m * tall:(m + 1) * tall]

        for r in range(0, tall, step):
            s = slice(r, r + step)
            low = end(0, s, cols)
            here = own(0, 1, s, cols)[0].astype(jnp.float32)
            clear, colour = None, None
            for first in range(0, layers, 2):
                pair = range(first, min(first + 2, layers))
                parts, picks, shades, tilts = [], [], [], []
                for layer in pair:
                    if layer + 1 < layers:
                        high = own(layer + 1, 1, s, cols)[0].astype(jnp.float32)
                    else:
                        high = end(1, s, cols)
                    position = jnp.clip(here * 2.5 + 7.5, 0.0, 15.0)
                    index = position.astype(jnp.int32)
                    whole = index.astype(jnp.float32)
                    parts.append(position - whole)
                    tilts.append([lookup(tilt, index) for tilt in tilts_of])
                    picks.append(choose(bins, whole))
                    gx = high - low
                    gy = slopes_y[layer, s, :]
                    gz = slopes_z[layer, s, :]
                    facing = jnp.abs(gx * lx + gy * ly + gz * lz)
                    square = gx * gx + gy * gy + gz * gz
                    shades.append(0.045 + facing * lax.rsqrt(jnp.maximum(square, 4.0)))
                    low, here = here, high
                pick = jnp.concatenate(picks, axis=1) if len(picks) > 1 else picks[0]
                found = jnp.dot(table[...], jnp.concatenate([pick, pick], axis=0), preferred_element_type=jnp.float32)
                for m, layer in enumerate(pair):
                    lanes = slice(m * LANES, (m + 1) * LANES)
                    looked = [found[k * step:(k + 1) * step, lanes] for k in range(rows_found)] + tilts[m]
                    tf = [looked[k] + parts[m] * looked[4 + k] for k in range(4)]
                    if layer == 0:
                        colour = [tf[k] * shades[m] for k in range(3)]
                        clear = 1.0 - tf[3]
                    else:
                        seen = shades[m] * clear
                        colour = [colour[k] + tf[k] * seen for k in range(3)]
                        clear = clear - clear * tf[3]
            for k in range(3):
                image[k, s, cols] = colour[k]
            image[3, s, cols] = 1.0 - clear
        return carry

    lax.fori_loop(0, width // LANES, strip, 0)

    @pl.when(sending)
    def _():
        send[0] = image[:, 0:unit, :]

    @pl.when(jnp.logical_not(sending))
    def _():
        keep[0] = image[:, 0:unit, :]


def merge_pair(ctl, mine, got, cols):
    theirs = [got[0, k, :, cols] for k in range(4)]
    ours = [mine[0, k, :, cols] for k in range(4)]
    behind = ctl[1] == 1
    front = [jnp.where(behind, t, o) for t, o in zip(theirs, ours)]
    back = [jnp.where(behind, o, t) for t, o in zip(theirs, ours)]
    return over(front, back)


def merge_kernel(ctl, *refs, members, places, unit):
    inputs, sends = refs[:2 * members], refs[2 * members:2 * members + places]
    image, tops = refs[2 * members + places:]
    turn = pl.program_id(0)
    width = image.shape[2]

    for n in range(members):
        @pl.when(lax.rem(turn, members) == n)
        def _(n=n):
            def put(at):
                cols = pl.ds(at, LANES)
                merged = merge_pair(ctl, inputs[2 * n], inputs[2 * n + 1], cols)
                for k in range(4):
                    image[k, :, cols] = merged[k]
                top = functools.reduce(jnp.maximum, merged)
                tops[0:8, cols] = jnp.max(top.reshape(unit // 8, 8, LANES), axis=0)

            each_strip(width, put)

    exponent = exponent_of(jnp.max(tops[0:8, :], axis=0, keepdims=True))
    tops[0:8, :] = jnp.broadcast_to(jnp.exp2(-exponent) * CODES, (8, width))
    row = jnp.broadcast_to(exponent, (8, width)).astype(jnp.int32)

    for k, send in enumerate(sends):
        @pl.when(turn // members == k)
        def _(send=send):
            def put(at):
                cols = pl.ds(at, LANES)
                factor = tops[0:1, cols]
                for k in range(2):
                    send[0, k * unit:(k + 1) * unit, cols] = pack(image[2 * k, :, cols], image[2 * k + 1, :, cols], factor)

            each_strip(width, put)
            send[0, 2 * unit:2 * unit + 8, :] = row


def gather_kernel(ctl, *refs, unit, blocks):
    parts, send, image = refs[:-2], refs[-2], refs[-1]
    width = image.shape[2]
    for me in range(len(parts)):
        @pl.when(ctl[0] == me)
        def _(me=me):
            def put(at):
                cols = pl.ds(at, LANES)
                total = None
                for j in range(len(parts)):
                    got = parts[me ^ j]
                    scale = scale_of(got[0, 2 * unit:2 * unit + 1, cols])
                    part = []
                    for k in range(2):
                        part += unpack(got[0, k * unit:(k + 1) * unit, cols], scale)
                    total = part if total is None else over(total, part)
                for k in range(4):
                    image[k, :, cols] = total[k]

            each_strip(width, put)

    part = width // blocks
    half = unit // 2
    for b in range(blocks):
        wide = jnp.concatenate([image[k, :, b * part:(b + 1) * part] for k in range(4)], axis=1)
        exponent = exponent_of(jnp.max(wide, axis=0, keepdims=True))
        factor = jnp.exp2(-exponent) * CODES
        send[b, 0, 8:8 + half, :] = pack(wide[:half], wide[half:], factor)
        send[b, 0, 0:8, :] = jnp.broadcast_to(exponent, (8, 4 * part)).astype(jnp.int32)


def compose_kernel(got, *refs, unit, blocks):
    out = refs[-1]
    part = out.shape[2]
    half = unit // 2
    total = None
    for b in range(blocks):
        scale = scale_of(got[b, 0, 0:1, :])
        wide = jnp.concatenate(unpack(got[b, 0, 8:8 + half, :], scale), axis=0)
        layer = [wide[:, k * part:(k + 1) * part] for k in range(4)]
        total = layer if total is None else over(total, layer)
    for k in range(4):
        out[k] = total[k]


def params():
    return pltpu.CompilerParams(vmem_limit_bytes=VMEM_LIMIT, dimension_semantics=("arbitrary",))


def unit_index(groups, units, bit):
    half = (groups // 2) * units

    def index(i, ctl):
        rest = lax.rem(i, half)
        parity = jnp.where(i < half, 1 - ctl[bit], ctl[bit])
        return (2 * (rest // units) + parity) * units + lax.rem(rest, units)

    return index


def split_outputs(groups, units, unit, width):
    half = (groups // 2) * units
    shapes = [
        jax.ShapeDtypeStruct((half, 4, unit, width), jnp.float32),
        jax.ShapeDtypeStruct((half, 4, unit, width), jnp.float32),
    ]
    specs = [
        pl.BlockSpec((1, 4, unit, width), lambda i, ctl: (jnp.minimum(i, half - 1), 0, 0, 0)),
        pl.BlockSpec((1, 4, unit, width), lambda i, ctl: (jnp.maximum(i - half, 0), 0, 0, 0)),
    ]
    return shapes, specs


def band(shape, dim, offset):
    place = lax.broadcasted_iota(jnp.int32, shape, dim) - lax.broadcasted_iota(jnp.int32, shape, 1 - dim) - offset
    return jnp.where(place == 1, 1.0, jnp.where(place == -1, -1.0, 0.0)).astype(jnp.bfloat16)


def render(ctl, light, table, slope, field, before, after, *, groups, units, unit, rows, offset, halo_at):
    layers, total, width = field.shape
    block = math.lcm(unit, 16)
    tall = padded_rows(unit)
    row_band = band((tall, tall + 32), 1, 16)
    place = lax.broadcasted_iota(jnp.int32, (tall, tall + 32), 1)
    top, bottom = place >= 16, place < 16 + unit
    row_bands = jnp.stack([
        jnp.where(jnp.logical_and(jnp.logical_or(top, kind % 2 == 0), jnp.logical_or(bottom, kind < 2)), row_band, 0)
        for kind in range(4)
    ])
    column_bands = jnp.stack([band((3 * LANES, LANES), 0, k * LANES) for k in range(3)])
    half = (groups // 2) * units
    index = unit_index(groups, units, 0)

    def start(i, ctl):
        unit_at = index(i, ctl)
        return (unit_at // units) * rows + offset + lax.rem(unit_at, units) * unit

    def main_at(i, ctl):
        return (0, start(i, ctl) // block, 0)

    def above_at(i, ctl):
        return (0, jnp.maximum(start(i, ctl) - 1, 0) // 16, 0)

    def below_at(i, ctl):
        return (0, jnp.minimum(start(i, ctl) + unit, total - 1) // 16, 0)

    shapes, specs = split_outputs(groups, units, unit, width)
    kernel = functools.partial(
        render_kernel, groups=groups, units=units, unit=unit, block=block, rows=rows, offset=offset, total=total
    )
    cells = layers * 2 * half * unit * width
    return pl.pallas_call(
        kernel,
        grid_spec=pltpu.PrefetchScalarGridSpec(
            num_scalar_prefetch=1,
            grid=(2 * half,),
            in_specs=[
                pl.BlockSpec(memory_space=pltpu.SMEM),
                pl.BlockSpec(table.shape, lambda i, ctl: (0, 0)),
                pl.BlockSpec(slope.shape, lambda i, ctl: (0, 0)),
                pl.BlockSpec((4, tall, tall + 32), lambda i, ctl: (0, 0, 0)),
                pl.BlockSpec((3, 3 * LANES, LANES), lambda i, ctl: (0, 0, 0)),
                pl.BlockSpec((layers, block, width), main_at),
                pl.BlockSpec((layers, 16, width), above_at),
                pl.BlockSpec((layers, 16, width), below_at),
                pl.BlockSpec((1, unit, width), lambda i, ctl: (index(i, ctl), halo_at, 0)),
                pl.BlockSpec((1, unit, width), lambda i, ctl: (index(i, ctl), halo_at, 0)),
            ],
            out_specs=specs,
            scratch_shapes=[
                pltpu.VMEM((layers, tall + 32, width) if block != unit else (1, 16, LANES), jnp.bfloat16),
                pltpu.VMEM((layers, tall, LANES), jnp.float32),
                pltpu.VMEM((layers, tall, LANES), jnp.float32),
                pltpu.VMEM((4, tall, width), jnp.float32),
                pltpu.VMEM((max(block, tall + 32), width) if block != unit else (8, LANES), jnp.float32),
                pltpu.VMEM((2, tall, width) if block != unit else (1, 8, LANES), jnp.float32),
            ],
        ),
        out_shape=shapes,
        compiler_params=params(),
        cost_estimate=pl.CostEstimate(flops=16384 * cells, bytes_accessed=6 * cells, transcendentals=cells),
        name="render",
    )(ctl, light, table, slope, row_bands, column_bands, field, field, field, before, after)


def merge(ctl, pairs, *, places, unit):
    members = len(pairs)
    width = pairs[0][0].shape[3]
    cells = 4 * places * members * unit * width

    def spec(k):
        return pl.BlockSpec(
            (1, 2 * unit + 8, width), lambda i, ctl: (jnp.clip(i - k * members, 0, members - 1), 0, 0)
        )

    return pl.pallas_call(
        functools.partial(merge_kernel, members=members, places=places, unit=unit),
        grid_spec=pltpu.PrefetchScalarGridSpec(
            num_scalar_prefetch=1,
            grid=(places * members,),
            in_specs=[pl.BlockSpec((1, 4, unit, width), lambda i, ctl: (ctl[0] ^ (i // members), 0, 0, 0))]
            * (2 * members),
            out_specs=[spec(k) for k in range(places)],
            scratch_shapes=[pltpu.VMEM((4, unit, width), jnp.float32), pltpu.VMEM((8, width), jnp.float32)],
        ),
        out_shape=[jax.ShapeDtypeStruct((members, 2 * unit + 8, width), jnp.int32)] * places,
        compiler_params=params(),
        cost_estimate=pl.CostEstimate(flops=32768 * cells, bytes_accessed=cells, transcendentals=0),
        name="merge",
    )(ctl, *[array for pair in pairs for array in pair])


def gather_parts(ctl, parts, *, units, unit, blocks):
    width = parts[0].shape[2]
    cells = 4 * units * unit * width
    return pl.pallas_call(
        functools.partial(gather_kernel, unit=unit, blocks=blocks),
        grid_spec=pltpu.PrefetchScalarGridSpec(
            num_scalar_prefetch=1,
            grid=(units,),
            in_specs=[pl.BlockSpec((1, 2 * unit + 8, width), lambda i, ctl: (i, 0, 0))] * len(parts),
            out_specs=pl.BlockSpec((blocks, 1, unit // 2 + 8, 4 * width // blocks), lambda i, ctl: (0, i, 0, 0)),
            scratch_shapes=[pltpu.VMEM((4, unit, width), jnp.float32)],
        ),
        out_shape=jax.ShapeDtypeStruct((blocks, units, unit // 2 + 8, 4 * width // blocks), jnp.int32),
        compiler_params=params(),
        cost_estimate=pl.CostEstimate(flops=131072 * cells, bytes_accessed=cells, transcendentals=0),
        name="gather_parts",
    )(ctl, *parts)


def compose(got, so_far, *, unit, first, rows):
    blocks, units = got.shape[:2]
    part = got.shape[3] // 4
    cells = 4 * units * unit * part * blocks
    operands = [got]
    in_specs = [pl.BlockSpec((blocks, 1, unit // 2 + 8, 4 * part), lambda i: (0, i, 0, 0))]
    if so_far is not None:
        operands.append(so_far)
        in_specs.append(pl.BlockSpec(memory_space=pl.ANY))
    return pl.pallas_call(
        functools.partial(compose_kernel, unit=unit, blocks=blocks),
        grid=(units,),
        in_specs=in_specs,
        out_specs=pl.BlockSpec((4, unit, part), lambda i: (0, first + i, 0)),
        out_shape=jax.ShapeDtypeStruct((4, rows, part), jnp.float32),
        input_output_aliases={1: 0} if so_far is not None else {},
        compiler_params=params(),
        cost_estimate=pl.CostEstimate(flops=32768 * cells, bytes_accessed=cells, transcendentals=0),
        name="compose",
    )(*operands)


def per_device(field, transfer, bin_order, light_angles):
    tiles = lax.axis_size("tile")
    blocks = lax.axis_size("depth")
    devices = tiles * blocks
    layers, total, width = field.shape
    rows = total // tiles
    unit = unit_rows(rows)
    places = tiles // 2

    table = jnp.take(transfer, bin_order, axis=1)
    table = table * jnp.array([[1.0], [1.0], [1.0], [0.01]], jnp.float32)
    bins = table.shape[1]
    slope = jnp.concatenate([table[:, 1:] - table[:, :-1], jnp.zeros_like(table[:, :1])], axis=1)
    table = jnp.concatenate([table, slope[:ON_MATRIX - 4]], axis=0)
    slope = jnp.pad(slope, ((0, 4), (0, LANES - bins)))
    coarse = lax.reduce_precision(table, exponent_bits=8, mantissa_bits=7)
    table = jnp.concatenate([coarse, table - coarse], axis=1)
    spread = jnp.eye(16, dtype=jnp.float32)
    table = (table[:, None, :, None] * spread[None, :, None, :]).reshape(ON_MATRIX * 16, 2 * bins * 16)
    table = table.astype(jnp.bfloat16)
    azimuth, polar = light_angles[0], light_angles[1]
    light = 0.105 * jnp.stack(
        [jnp.cos(azimuth) * jnp.sin(polar), jnp.sin(azimuth) * jnp.sin(polar), jnp.cos(polar)]
    )

    tile = lax.axis_index("tile")
    core, place = (tile & 1).astype(jnp.int32), (tile >> 1).astype(jnp.int32)
    render_control = jnp.stack([core, core])
    merge_control = jnp.stack([place, core])
    up = [(i, i + 1) for i in range(devices - 1)]
    down = [(j, i) for i, j in up]
    both = ("depth", "tile")

    count = rows // unit
    starts = [n * unit for n in range(count)]

    def cut(layer, first, stop):
        part = field.reshape(layers, tiles, rows, width)[layer:layer + 1, :, first * unit:stop * unit]
        return part.reshape(tiles, (stop - first) * unit, width)

    halos = []
    for first, stop in [(0, 1), (1, count)][:count]:
        ends = (cut(layers - 1, first, stop), cut(0, first, stop))
        if halos:
            ends, _ = lax.optimization_barrier((ends, halos[0][:2]))
        pair = (lax.ppermute(ends[0], both, up), lax.ppermute(ends[1], both, down))
        halos += [pair + (n - first,) for n in range(first, stop)]

    def exchange(send, distance):
        return lax.ppermute(send, "tile", [(i, i ^ distance) for i in range(tiles)])

    chain = []
    waits = []

    def after_last(control):
        if chain:
            control, _, _ = lax.optimization_barrier((control, chain[-1], list(waits)))
            waits.clear()
        return control

    state = [None] * count

    def start_chunk(n):
        before, after, at = halos[n]
        send, keep = render(
            after_last(render_control), light, table, slope, field, before, after,
            groups=tiles, units=1, unit=unit, rows=rows, offset=starts[n], halo_at=at,
        )
        chain.append(send)
        state[n] = (keep, exchange(send, 1))

    def merge_group(members):
        sends = merge(after_last(merge_control), [state[n] for n in members], places=places, unit=unit)
        chain.append(sends[-1])
        return [sends[0]] + [exchange(sends[k], 2 * k) for k in range(1, places)]

    def block_group(members, parts):
        send = gather_parts(after_last(merge_control), parts, units=len(members), unit=unit, blocks=blocks)
        chain.append(send)
        return lax.all_to_all(send, "depth", split_axis=0, concat_axis=0, tiled=True)

    early, late = list(range(count - 1)), [count - 1]
    results = []
    if early:
        for n in early:
            start_chunk(n)
        early_parts = merge_group(early)
        start_chunk(count - 1)
        waits.extend(early_parts)
        results.append(block_group(early, early_parts))
    else:
        start_chunk(count - 1)
    results.append(block_group(late, merge_group(late)))
    final = None
    done = 0
    for result in results:
        final = compose(result, final, unit=unit, first=done, rows=rows)
        done += result.shape[1]
    return final


def solution(mesh):
    in_specs = (P(("depth", "tile"), None, None), P(), P(), P())
    out_specs = P(None, "tile", "depth")
    return jax.shard_map(
        per_device, mesh=mesh, in_specs=in_specs, out_specs=out_specs, check_vma=False
    )
```

```python
import functools
import math

import jax
import jax.numpy as jnp
from jax import lax
from jax.experimental import pallas as pl
from jax.experimental.pallas import tpu as pltpu
from jax.sharding import PartitionSpec as P

LANES = 128
CODES = 32700.0
ON_MATRIX = 4
VMEM_LIMIT = 56 * 1024 * 1024


def unit_rows(rows):
    return 48 if rows % 48 == 0 else rows


def exponent_of(top):
    return jnp.ceil(jnp.log2(jnp.maximum(top, 1e-30)))


def pack(low, high, factor):
    low = (low * factor + 0.5).astype(jnp.int32)
    high = (high * factor + 0.5).astype(jnp.int32)
    return low | (high << 16)


def unpack(word, scale):
    return (word & 0xFFFF).astype(jnp.float32) * scale, (word >> 16).astype(jnp.float32) * scale


def scale_of(row):
    return jnp.exp2(row.astype(jnp.float32)) * (1.0 / CODES)


def over(front, back):
    clear = 1.0 - front[3]
    return [f + clear * b for f, b in zip(front, back)]


def lookup(table, index):
    numbers = lax.GatherDimensionNumbers(
        offset_dims=(), collapsed_slice_dims=(1,), start_index_map=(1,),
        operand_batching_dims=(0,), start_indices_batching_dims=(0,),
    )
    return lax.gather(
        table, index[..., None], numbers, slice_sizes=(1, 1), mode=lax.GatherScatterMode.PROMISE_IN_BOUNDS
    )


def choose(bins, whole):
    place = whole.astype(jnp.bfloat16)
    one, zero = jnp.ones_like(place), jnp.zeros_like(place)
    return jnp.concatenate([jnp.where(place == k, one, zero) for k in range(bins)], axis=0)


def padded_rows(unit):
    return -(-unit // 16) * 16


def each_strip(width, body):
    strips = width // LANES
    together = 3 if strips % 3 == 0 else 1

    def step(c, carry):
        for k in range(together):
            body(pl.multiple_of((c * together + k) * LANES, LANES))
        return carry

    lax.fori_loop(0, strips // together, step, 0)


def render_kernel(ctl, light, table, slope, row_bands, column_bands, main, above, below, before, after, send, keep, cells, slopes_y, slopes_z, image, stage, ends, *, groups, units, unit, block, rows, offset, total):
    i = pl.program_id(0)
    half = (groups // 2) * units
    rest = lax.rem(i, half)
    sending = i < half
    parity = jnp.where(sending, 1 - ctl[0], ctl[0])
    group = 2 * (rest // units) + parity
    start = group * rows + offset + lax.rem(rest, units) * unit
    layers = main.shape[0]
    width = main.shape[2]
    tall = padded_rows(unit)
    aligned = block == unit

    def load_layer(layer, carry):
        shift = pl.multiple_of(lax.rem(start, block), 8)
        stage[0:block, :] = main[layer].astype(jnp.float32)
        body = stage[pl.ds(shift, unit), :]
        up = above[layer].astype(jnp.float32)
        down = below[layer].astype(jnp.float32)
        up = jnp.where(lax.rem(start, 16) == 0, up[8:16], up[0:8])
        down = jnp.where(lax.rem(start + unit, 16) == 0, down[0:8], down[8:16])
        stage[0:8, :] = jnp.zeros((8, width), jnp.float32)
        stage[8:16, :] = up
        stage[16:16 + unit, :] = body
        stage[16 + unit:24 + unit, :] = down
        stage[24 + unit:tall + 32, :] = jnp.zeros((tall + 8 - unit, width), jnp.float32)
        cells[layer, :, :] = stage[0:tall + 32, :].astype(jnp.bfloat16)
        return carry

    if not aligned:
        lax.fori_loop(0, layers, load_layer, 0)
        ends[0, 0:unit, :] = before[0].astype(jnp.float32)
        ends[1, 0:unit, :] = after[0].astype(jnp.float32)

    def own(first, count, s, cols):
        if aligned:
            return main[first:first + count, s, cols]
        return cells[first:first + count, 16 + s.start:16 + s.stop, cols]

    def tower(layer, cols):
        if aligned:
            return jnp.concatenate([above[layer, :, cols], main[layer, :, cols], below[layer, :, cols]], axis=0)
        return cells[layer, :, cols]

    def end(which, s, cols):
        if aligned:
            return (before, after)[which][0, s, cols].astype(jnp.float32)
        return ends[which, s, cols]

    lx, ly, lz = light[0], light[1], light[2]
    step = 16
    bins = table.shape[1] // step
    rows_found = table.shape[0] // (2 * step)
    tilts_of = [jnp.broadcast_to(slope[k:k + 1, :], (step, LANES)) for k in range(rows_found - 4, 4)]
    row_kind = jnp.where(start == 0, 1, 0) + jnp.where(start + unit == total, 2, 0)

    def strip(c, carry):
        at = pl.multiple_of(c * LANES, LANES)
        cols = pl.ds(at, LANES)
        window = pl.ds(pl.multiple_of(jnp.clip(at - LANES, 0, width - 3 * LANES), LANES), 3 * LANES)
        column_kind = jnp.where(at == 0, 0, jnp.where(at == width - LANES, 2, 1))
        wide = own(0, layers, slice(0, tall), window).reshape(layers * tall, 3 * LANES)
        across = jnp.dot(wide, column_bands[column_kind], preferred_element_type=jnp.float32)
        for layer in range(layers):
            slopes_z[layer] = across[layer * tall:(layer + 1) * tall]
        for first in range(0, layers, 2):
            count = min(2, layers - first)
            towers = [tower(first + m, cols) for m in range(count)]
            both = jnp.concatenate(towers, axis=1) if count > 1 else towers[0]
            found = jnp.dot(row_bands[row_kind], both, preferred_element_type=jnp.float32)
            for m in range(count):
                slopes_y[first + m] = found[:, m * LANES:(m + 1) * LANES]

        for r in range(0, tall, step):
            s = slice(r, r + step)
            low = end(0, s, cols)
            here = own(0, 1, s, cols)[0].astype(jnp.float32)
            clear, colour = None, None
            for first in range(0, layers, 2):
                pair = range(first, min(first + 2, layers))
                parts, picks, shades, tilts = [], [], [], []
                for layer in pair:
                    if layer + 1 < layers:
                        high = own(layer + 1, 1, s, cols)[0].astype(jnp.float32)
                    else:
                        high = end(1, s, cols)
                    position = jnp.clip(here * 2.5 + 7.5, 0.0, 15.0)
                    index = position.astype(jnp.int32)
                    whole = index.astype(jnp.float32)
                    parts.append(position - whole)
                    tilts.append([lookup(tilt, index) for tilt in tilts_of])
                    picks.append(choose(bins, whole))
                    gx = high - low
                    gy = slopes_y[layer, s, :]
                    gz = slopes_z[layer, s, :]
                    facing = jnp.abs(gx * lx + gy * ly + gz * lz)
                    square = gx * gx + gy * gy + gz * gz
                    shades.append(0.045 + facing * lax.rsqrt(jnp.maximum(square, 4.0)))
                    low, here = here, high
                pick = jnp.concatenate(picks, axis=1) if len(picks) > 1 else picks[0]
                found = jnp.dot(table[...], pick, preferred_element_type=jnp.float32)
                for m, layer in enumerate(pair):
                    lanes = slice(m * LANES, (m + 1) * LANES)
                    half_rows = rows_found * step
                    looked = [
                        found[k * step:(k + 1) * step, lanes]
                        + found[half_rows + k * step:half_rows + (k + 1) * step, lanes]
                        for k in range(rows_found)
                    ] + tilts[m]
                    tf = [looked[k] + parts[m] * looked[4 + k] for k in range(4)]
                    if layer == 0:
                        colour = [tf[k] * shades[m] for k in range(3)]
                        clear = 1.0 - tf[3]
                    else:
                        seen = shades[m] * clear
                        colour = [colour[k] + tf[k] * seen for k in range(3)]
                        clear = clear - clear * tf[3]
            for k in range(3):
                image[k, s, cols] = colour[k]
            image[3, s, cols] = 1.0 - clear
        return carry

    lax.fori_loop(0, width // LANES, strip, 0)

    @pl.when(sending)
    def _():
        send[0] = image[:, 0:unit, :]

    @pl.when(jnp.logical_not(sending))
    def _():
        keep[0] = image[:, 0:unit, :]


def merge_pair(ctl, mine, got, cols):
    theirs = [got[0, k, :, cols] for k in range(4)]
    ours = [mine[0, k, :, cols] for k in range(4)]
    behind = ctl[1] == 1
    front = [jnp.where(behind, t, o) for t, o in zip(theirs, ours)]
    back = [jnp.where(behind, o, t) for t, o in zip(theirs, ours)]
    return over(front, back)


def merge_kernel(ctl, *refs, members, places, unit):
    inputs, sends = refs[:2 * members], refs[2 * members:2 * members + places]
    image, tops = refs[2 * members + places:]
    turn = pl.program_id(0)
    width = image.shape[2]

    for n in range(members):
        @pl.when(lax.rem(turn, members) == n)
        def _(n=n):
            def put(at):
                cols = pl.ds(at, LANES)
                merged = merge_pair(ctl, inputs[2 * n], inputs[2 * n + 1], cols)
                for k in range(4):
                    image[k, :, cols] = merged[k]
                top = functools.reduce(jnp.maximum, merged)
                tops[0:8, cols] = jnp.max(top.reshape(unit // 8, 8, LANES), axis=0)

            each_strip(width, put)

    exponent = exponent_of(jnp.max(tops[0:8, :], axis=0, keepdims=True))
    tops[0:8, :] = jnp.broadcast_to(jnp.exp2(-exponent) * CODES, (8, width))
    row = jnp.broadcast_to(exponent, (8, width)).astype(jnp.int32)

    for k, send in enumerate(sends):
        @pl.when(turn // members == k)
        def _(send=send):
            def put(at):
                cols = pl.ds(at, LANES)
                factor = tops[0:1, cols]
                for k in range(2):
                    send[0, k * unit:(k + 1) * unit, cols] = pack(image[2 * k, :, cols], image[2 * k + 1, :, cols], factor)

            each_strip(width, put)
            send[0, 2 * unit:2 * unit + 8, :] = row


def gather_kernel(ctl, *refs, unit, blocks):
    parts, send, image = refs[:-2], refs[-2], refs[-1]
    width = image.shape[2]
    for me in range(len(parts)):
        @pl.when(ctl[0] == me)
        def _(me=me):
            def put(at):
                cols = pl.ds(at, LANES)
                total = None
                for j in range(len(parts)):
                    got = parts[me ^ j]
                    scale = scale_of(got[0, 2 * unit:2 * unit + 1, cols])
                    part = []
                    for k in range(2):
                        part += unpack(got[0, k * unit:(k + 1) * unit, cols], scale)
                    total = part if total is None else over(total, part)
                for k in range(4):
                    image[k, :, cols] = total[k]

            each_strip(width, put)

    part = width // blocks
    half = unit // 2
    for b in range(blocks):
        wide = jnp.concatenate([image[k, :, b * part:(b + 1) * part] for k in range(4)], axis=1)
        exponent = exponent_of(jnp.max(wide, axis=0, keepdims=True))
        factor = jnp.exp2(-exponent) * CODES
        send[b, 0, 8:8 + half, :] = pack(wide[:half], wide[half:], factor)
        send[b, 0, 0:8, :] = jnp.broadcast_to(exponent, (8, 4 * part)).astype(jnp.int32)


def compose_kernel(got, *refs, unit, blocks):
    out = refs[-1]
    part = out.shape[2]
    half = unit // 2
    total = None
    for b in range(blocks):
        scale = scale_of(got[b, 0, 0:1, :])
        wide = jnp.concatenate(unpack(got[b, 0, 8:8 + half, :], scale), axis=0)
        layer = [wide[:, k * part:(k + 1) * part] for k in range(4)]
        total = layer if total is None else over(total, layer)
    for k in range(4):
        out[k] = total[k]


def params():
    return pltpu.CompilerParams(vmem_limit_bytes=VMEM_LIMIT, dimension_semantics=("arbitrary",))


def unit_index(groups, units, bit):
    half = (groups // 2) * units

    def index(i, ctl):
        rest = lax.rem(i, half)
        parity = jnp.where(i < half, 1 - ctl[bit], ctl[bit])
        return (2 * (rest // units) + parity) * units + lax.rem(rest, units)

    return index


def split_outputs(groups, units, unit, width):
    half = (groups // 2) * units
    shapes = [
        jax.ShapeDtypeStruct((half, 4, unit, width), jnp.float32),
        jax.ShapeDtypeStruct((half, 4, unit, width), jnp.float32),
    ]
    specs = [
        pl.BlockSpec((1, 4, unit, width), lambda i, ctl: (jnp.minimum(i, half - 1), 0, 0, 0)),
        pl.BlockSpec((1, 4, unit, width), lambda i, ctl: (jnp.maximum(i - half, 0), 0, 0, 0)),
    ]
    return shapes, specs


def band(shape, dim, offset):
    place = lax.broadcasted_iota(jnp.int32, shape, dim) - lax.broadcasted_iota(jnp.int32, shape, 1 - dim) - offset
    return jnp.where(place == 1, 1.0, jnp.where(place == -1, -1.0, 0.0)).astype(jnp.bfloat16)


def render(ctl, light, table, slope, field, before, after, *, groups, units, unit, rows, offset, halo_at):
    layers, total, width = field.shape
    block = math.lcm(unit, 16)
    tall = padded_rows(unit)
    row_band = band((tall, tall + 32), 1, 16)
    place = lax.broadcasted_iota(jnp.int32, (tall, tall + 32), 1)
    top, bottom = place >= 16, place < 16 + unit
    row_bands = jnp.stack([
        jnp.where(jnp.logical_and(jnp.logical_or(top, kind % 2 == 0), jnp.logical_or(bottom, kind < 2)), row_band, 0)
        for kind in range(4)
    ])
    column_bands = jnp.stack([band((3 * LANES, LANES), 0, k * LANES) for k in range(3)])
    half = (groups // 2) * units
    index = unit_index(groups, units, 0)

    def start(i, ctl):
        unit_at = index(i, ctl)
        return (unit_at // units) * rows + offset + lax.rem(unit_at, units) * unit

    def main_at(i, ctl):
        return (0, start(i, ctl) // block, 0)

    def above_at(i, ctl):
        return (0, jnp.maximum(start(i, ctl) - 1, 0) // 16, 0)

    def below_at(i, ctl):
        return (0, jnp.minimum(start(i, ctl) + unit, total - 1) // 16, 0)

    shapes, specs = split_outputs(groups, units, unit, width)
    kernel = functools.partial(
        render_kernel, groups=groups, units=units, unit=unit, block=block, rows=rows, offset=offset, total=total
    )
    cells = layers * 2 * half * unit * width
    return pl.pallas_call(
        kernel,
        grid_spec=pltpu.PrefetchScalarGridSpec(
            num_scalar_prefetch=1,
            grid=(2 * half,),
            in_specs=[
                pl.BlockSpec(memory_space=pltpu.SMEM),
                pl.BlockSpec(table.shape, lambda i, ctl: (0, 0)),
                pl.BlockSpec(slope.shape, lambda i, ctl: (0, 0)),
                pl.BlockSpec((4, tall, tall + 32), lambda i, ctl: (0, 0, 0)),
                pl.BlockSpec((3, 3 * LANES, LANES), lambda i, ctl: (0, 0, 0)),
                pl.BlockSpec((layers, block, width), main_at),
                pl.BlockSpec((layers, 16, width), above_at),
                pl.BlockSpec((layers, 16, width), below_at),
                pl.BlockSpec((1, unit, width), lambda i, ctl: (index(i, ctl), halo_at, 0)),
                pl.BlockSpec((1, unit, width), lambda i, ctl: (index(i, ctl), halo_at, 0)),
            ],
            out_specs=specs,
            scratch_shapes=[
                pltpu.VMEM((layers, tall + 32, width) if block != unit else (1, 16, LANES), jnp.bfloat16),
                pltpu.VMEM((layers, tall, LANES), jnp.float32),
                pltpu.VMEM((layers, tall, LANES), jnp.float32),
                pltpu.VMEM((4, tall, width), jnp.float32),
                pltpu.VMEM((max(block, tall + 32), width) if block != unit else (8, LANES), jnp.float32),
                pltpu.VMEM((2, tall, width) if block != unit else (1, 8, LANES), jnp.float32),
            ],
        ),
        out_shape=shapes,
        compiler_params=params(),
        cost_estimate=pl.CostEstimate(flops=16384 * cells, bytes_accessed=6 * cells, transcendentals=cells),
        name="render",
    )(ctl, light, table, slope, row_bands, column_bands, field, field, field, before, after)


def merge(ctl, pairs, *, places, unit):
    members = len(pairs)
    width = pairs[0][0].shape[3]
    cells = 4 * places * members * unit * width

    def spec(k):
        return pl.BlockSpec(
            (1, 2 * unit + 8, width), lambda i, ctl: (jnp.clip(i - k * members, 0, members - 1), 0, 0)
        )

    return pl.pallas_call(
        functools.partial(merge_kernel, members=members, places=places, unit=unit),
        grid_spec=pltpu.PrefetchScalarGridSpec(
            num_scalar_prefetch=1,
            grid=(places * members,),
            in_specs=[pl.BlockSpec((1, 4, unit, width), lambda i, ctl: (ctl[0] ^ (i // members), 0, 0, 0))]
            * (2 * members),
            out_specs=[spec(k) for k in range(places)],
            scratch_shapes=[pltpu.VMEM((4, unit, width), jnp.float32), pltpu.VMEM((8, width), jnp.float32)],
        ),
        out_shape=[jax.ShapeDtypeStruct((members, 2 * unit + 8, width), jnp.int32)] * places,
        compiler_params=params(),
        cost_estimate=pl.CostEstimate(flops=32768 * cells, bytes_accessed=cells, transcendentals=0),
        name="merge",
    )(ctl, *[array for pair in pairs for array in pair])


def gather_parts(ctl, parts, *, units, unit, blocks):
    width = parts[0].shape[2]
    cells = 4 * units * unit * width
    return pl.pallas_call(
        functools.partial(gather_kernel, unit=unit, blocks=blocks),
        grid_spec=pltpu.PrefetchScalarGridSpec(
            num_scalar_prefetch=1,
            grid=(units,),
            in_specs=[pl.BlockSpec((1, 2 * unit + 8, width), lambda i, ctl: (i, 0, 0))] * len(parts),
            out_specs=pl.BlockSpec((blocks, 1, unit // 2 + 8, 4 * width // blocks), lambda i, ctl: (0, i, 0, 0)),
            scratch_shapes=[pltpu.VMEM((4, unit, width), jnp.float32)],
        ),
        out_shape=jax.ShapeDtypeStruct((blocks, units, unit // 2 + 8, 4 * width // blocks), jnp.int32),
        compiler_params=params(),
        cost_estimate=pl.CostEstimate(flops=131072 * cells, bytes_accessed=cells, transcendentals=0),
        name="gather_parts",
    )(ctl, *parts)


def compose(got, so_far, *, unit, first, rows):
    blocks, units = got.shape[:2]
    part = got.shape[3] // 4
    cells = 4 * units * unit * part * blocks
    operands = [got]
    in_specs = [pl.BlockSpec((blocks, 1, unit // 2 + 8, 4 * part), lambda i: (0, i, 0, 0))]
    if so_far is not None:
        operands.append(so_far)
        in_specs.append(pl.BlockSpec(memory_space=pl.ANY))
    return pl.pallas_call(
        functools.partial(compose_kernel, unit=unit, blocks=blocks),
        grid=(units,),
        in_specs=in_specs,
        out_specs=pl.BlockSpec((4, unit, part), lambda i: (0, first + i, 0)),
        out_shape=jax.ShapeDtypeStruct((4, rows, part), jnp.float32),
        input_output_aliases={1: 0} if so_far is not None else {},
        compiler_params=params(),
        cost_estimate=pl.CostEstimate(flops=32768 * cells, bytes_accessed=cells, transcendentals=0),
        name="compose",
    )(*operands)


def per_device(field, transfer, bin_order, light_angles):
    tiles = lax.axis_size("tile")
    blocks = lax.axis_size("depth")
    devices = tiles * blocks
    layers, total, width = field.shape
    rows = total // tiles
    unit = unit_rows(rows)
    places = tiles // 2

    table = jnp.take(transfer, bin_order, axis=1)
    table = table * jnp.array([[1.0], [1.0], [1.0], [0.01]], jnp.float32)
    bins = table.shape[1]
    slope = jnp.concatenate([table[:, 1:] - table[:, :-1], jnp.zeros_like(table[:, :1])], axis=1)
    table = jnp.concatenate([table, slope[:ON_MATRIX - 4]], axis=0)
    slope = jnp.pad(slope, ((0, 4), (0, LANES - bins)))
    coarse = lax.reduce_precision(table, exponent_bits=8, mantissa_bits=7)
    table = jnp.concatenate([coarse, table - coarse], axis=0)
    spread = jnp.eye(16, dtype=jnp.float32)
    table = (table[:, None, :, None] * spread[None, :, None, :]).reshape(2 * ON_MATRIX * 16, bins * 16)
    table = table.astype(jnp.bfloat16)
    azimuth, polar = light_angles[0], light_angles[1]
    light = 0.105 * jnp.stack(
        [jnp.cos(azimuth) * jnp.sin(polar), jnp.sin(azimuth) * jnp.sin(polar), jnp.cos(polar)]
    )

    tile = lax.axis_index("tile")
    core, place = (tile & 1).astype(jnp.int32), (tile >> 1).astype(jnp.int32)
    render_control = jnp.stack([core, core])
    merge_control = jnp.stack([place, core])
    up = [(i, i + 1) for i in range(devices - 1)]
    down = [(j, i) for i, j in up]
    both = ("depth", "tile")

    count = rows // unit
    starts = [n * unit for n in range(count)]

    def cut(layer, first, stop):
        part = field.reshape(layers, tiles, rows, width)[layer:layer + 1, :, first * unit:stop * unit]
        return part.reshape(tiles, (stop - first) * unit, width)

    halos = []
    for first, stop in [(0, 1), (1, count)][:count]:
        ends = (cut(layers - 1, first, stop), cut(0, first, stop))
        if halos:
            ends, _ = lax.optimization_barrier((ends, halos[0][:2]))
        pair = (lax.ppermute(ends[0], both, up), lax.ppermute(ends[1], both, down))
        halos += [pair + (n - first,) for n in range(first, stop)]

    def exchange(send, distance):
        return lax.ppermute(send, "tile", [(i, i ^ distance) for i in range(tiles)])

    chain = []
    waits = []

    def after_last(control):
        if chain:
            control, _, _ = lax.optimization_barrier((control, chain[-1], list(waits)))
            waits.clear()
        return control

    state = [None] * count

    def start_chunk(n):
        before, after, at = halos[n]
        send, keep = render(
            after_last(render_control), light, table, slope, field, before, after,
            groups=tiles, units=1, unit=unit, rows=rows, offset=starts[n], halo_at=at,
        )
        chain.append(send)
        state[n] = (keep, exchange(send, 1))

    def merge_group(members):
        sends = merge(after_last(merge_control), [state[n] for n in members], places=places, unit=unit)
        chain.append(sends[-1])
        return [sends[0]] + [exchange(sends[k], 2 * k) for k in range(1, places)]

    def block_group(members, parts):
        send = gather_parts(after_last(merge_control), parts, units=len(members), unit=unit, blocks=blocks)
        chain.append(send)
        return lax.all_to_all(send, "depth", split_axis=0, concat_axis=0, tiled=True)

    early, late = list(range(count - 1)), [count - 1]
    results = []
    if early:
        for n in early:
            start_chunk(n)
        early_parts = merge_group(early)
        start_chunk(count - 1)
        waits.extend(early_parts)
        results.append(block_group(early, early_parts))
    else:
        start_chunk(count - 1)
    results.append(block_group(late, merge_group(late)))
    final = None
    done = 0
    for result in results:
        final = compose(result, final, unit=unit, first=done, rows=rows)
        done += result.shape[1]
    return final


def solution(mesh):
    in_specs = (P(("depth", "tile"), None, None), P(), P(), P())
    out_specs = P(None, "tile", "depth")
    return jax.shard_map(
        per_device, mesh=mesh, in_specs=in_specs, out_specs=out_specs, check_vma=False
    )
```

```python
import functools
import math

import jax
import jax.numpy as jnp
from jax import lax
from jax.experimental import pallas as pl
from jax.experimental.pallas import tpu as pltpu
from jax.sharding import PartitionSpec as P

LANES = 128
CODES = 32700.0
ON_MATRIX = 4
VMEM_LIMIT = 56 * 1024 * 1024


def unit_rows(rows):
    return 48 if rows % 48 == 0 else rows


def exponent_of(top):
    return jnp.ceil(jnp.log2(jnp.maximum(top, 1e-30)))


def pack(low, high, factor):
    low = (low * factor + 0.5).astype(jnp.int32)
    high = (high * factor + 0.5).astype(jnp.int32)
    return low | (high << 16)


def unpack(word, scale):
    return (word & 0xFFFF).astype(jnp.float32) * scale, (word >> 16).astype(jnp.float32) * scale


def scale_of(row):
    return jnp.exp2(row.astype(jnp.float32)) * (1.0 / CODES)


def over(front, back):
    clear = 1.0 - front[3]
    return [f + clear * b for f, b in zip(front, back)]


def lookup(table, index):
    numbers = lax.GatherDimensionNumbers(
        offset_dims=(), collapsed_slice_dims=(1,), start_index_map=(1,),
        operand_batching_dims=(0,), start_indices_batching_dims=(0,),
    )
    return lax.gather(
        table, index[..., None], numbers, slice_sizes=(1, 1), mode=lax.GatherScatterMode.PROMISE_IN_BOUNDS
    )


def choose(bins, whole):
    place = whole.astype(jnp.bfloat16)
    one, zero = jnp.ones_like(place), jnp.zeros_like(place)
    return jnp.concatenate([jnp.where(place == k, one, zero) for k in range(bins)], axis=0)


def padded_rows(unit):
    return -(-unit // 16) * 16


def each_strip(width, body):
    strips = width // LANES
    together = 3 if strips % 3 == 0 else 1

    def step(c, carry):
        for k in range(together):
            body(pl.multiple_of((c * together + k) * LANES, LANES))
        return carry

    lax.fori_loop(0, strips // together, step, 0)


def render_kernel(ctl, light, table, slope, row_bands, column_bands, main, above, below, before, after, send, keep, cells, slopes_y, slopes_z, image, stage, ends, *, groups, units, unit, block, rows, offset, total):
    i = pl.program_id(0)
    half = (groups // 2) * units
    rest = lax.rem(i, half)
    sending = i < half
    parity = jnp.where(sending, 1 - ctl[0], ctl[0])
    group = 2 * (rest // units) + parity
    start = group * rows + offset + lax.rem(rest, units) * unit
    layers = main.shape[0]
    width = main.shape[2]
    tall = padded_rows(unit)
    aligned = block == unit

    def load_layer(layer, carry):
        shift = pl.multiple_of(lax.rem(start, block), 8)
        stage[0:block, :] = main[layer].astype(jnp.float32)
        body = stage[pl.ds(shift, unit), :]
        up = above[layer].astype(jnp.float32)
        down = below[layer].astype(jnp.float32)
        up = jnp.where(lax.rem(start, 16) == 0, up[8:16], up[0:8])
        down = jnp.where(lax.rem(start + unit, 16) == 0, down[0:8], down[8:16])
        stage[0:8, :] = jnp.zeros((8, width), jnp.float32)
        stage[8:16, :] = up
        stage[16:16 + unit, :] = body
        stage[16 + unit:24 + unit, :] = down
        stage[24 + unit:tall + 32, :] = jnp.zeros((tall + 8 - unit, width), jnp.float32)
        cells[layer, :, :] = stage[0:tall + 32, :].astype(jnp.bfloat16)
        return carry

    if not aligned:
        lax.fori_loop(0, layers, load_layer, 0)
        ends[0, 0:unit, :] = before[0].astype(jnp.float32)
        ends[1, 0:unit, :] = after[0].astype(jnp.float32)

    def own(first, count, s, cols):
        if aligned:
            return main[first:first + count, s, cols]
        return cells[first:first + count, 16 + s.start:16 + s.stop, cols]

    def tower(layer, cols):
        if aligned:
            return jnp.concatenate([above[layer, :, cols], main[layer, :, cols], below[layer, :, cols]], axis=0)
        return cells[layer, :, cols]

    def end(which, s, cols):
        if aligned:
            return (before, after)[which][0, s, cols].astype(jnp.float32)
        return ends[which, s, cols]

    lx, ly, lz = light[0], light[1], light[2]
    step = 16
    bins = table.shape[1] // step
    rows_found = table.shape[0] // (2 * step)
    tilts_of = [jnp.broadcast_to(slope[k:k + 1, :], (step, LANES)) for k in range(rows_found - 4, 4)]
    row_kind = jnp.where(start == 0, 1, 0) + jnp.where(start + unit == total, 2, 0)

    def strip(c, carry):
        at = pl.multiple_of(c * LANES, LANES)
        cols = pl.ds(at, LANES)
        window = pl.ds(pl.multiple_of(jnp.clip(at - LANES, 0, width - 3 * LANES), LANES), 3 * LANES)
        column_kind = jnp.where(at == 0, 0, jnp.where(at == width - LANES, 2, 1))
        wide = own(0, layers, slice(0, tall), window).reshape(layers * tall, 3 * LANES)
        across = jnp.dot(wide, column_bands[column_kind], preferred_element_type=jnp.float32)
        for layer in range(layers):
            slopes_z[layer] = across[layer * tall:(layer + 1) * tall]
        for first in range(0, layers, 2):
            count = min(2, layers - first)
            towers = [tower(first + m, cols) for m in range(count)]
            both = jnp.concatenate(towers, axis=1) if count > 1 else towers[0]
            found = jnp.dot(row_bands[row_kind], both, preferred_element_type=jnp.float32)
            for m in range(count):
                slopes_y[first + m] = found[:, m * LANES:(m + 1) * LANES]

        for r in range(0, tall, step):
            s = slice(r, r + step)
            low = end(0, s, cols)
            here = own(0, 1, s, cols)[0].astype(jnp.float32)
            clear, colour = None, None
            for first in range(0, layers, 2):
                pair = range(first, min(first + 2, layers))
                parts, picks, shades, tilts = [], [], [], []
                for layer in pair:
                    if layer + 1 < layers:
                        high = own(layer + 1, 1, s, cols)[0].astype(jnp.float32)
                    else:
                        high = end(1, s, cols)
                    position = jnp.clip(here * 2.5 + 7.5, 0.0, 15.0)
                    index = position.astype(jnp.int32)
                    whole = index.astype(jnp.float32)
                    parts.append(position - whole)
                    tilts.append([lookup(tilt, index) for tilt in tilts_of])
                    picks.append(choose(bins, whole))
                    gx = high - low
                    gy = slopes_y[layer, s, :]
                    gz = slopes_z[layer, s, :]
                    facing = jnp.abs(gx * lx + gy * ly + gz * lz)
                    square = gx * gx + gy * gy + gz * gz
                    shades.append(0.045 + facing * lax.rsqrt(jnp.maximum(square, 4.0)))
                    low, here = here, high
                pick = jnp.concatenate(picks, axis=1) if len(picks) > 1 else picks[0]
                found = jnp.dot(table[...], pick, preferred_element_type=jnp.float32)
                for m, layer in enumerate(pair):
                    lanes = slice(m * LANES, (m + 1) * LANES)
                    half_rows = rows_found * step
                    looked = [
                        found[k * step:(k + 1) * step, lanes]
                        + found[half_rows + k * step:half_rows + (k + 1) * step, lanes]
                        for k in range(rows_found)
                    ] + tilts[m]
                    tf = [looked[k] + parts[m] * looked[4 + k] for k in range(4)]
                    if layer == 0:
                        colour = [tf[k] * shades[m] for k in range(3)]
                        clear = 1.0 - tf[3]
                    else:
                        seen = shades[m] * clear
                        colour = [colour[k] + tf[k] * seen for k in range(3)]
                        clear = clear - clear * tf[3]
            for k in range(3):
                image[k, s, cols] = colour[k]
            image[3, s, cols] = 1.0 - clear
        return carry

    lax.fori_loop(0, width // LANES, strip, 0)

    @pl.when(sending)
    def _():
        send[0] = image[:, 0:unit, :]

    @pl.when(jnp.logical_not(sending))
    def _():
        keep[0] = image[:, 0:unit, :]


def merge_pair(ctl, mine, got, cols):
    theirs = [got[0, k, :, cols] for k in range(4)]
    ours = [mine[0, k, :, cols] for k in range(4)]
    behind = ctl[1] == 1
    front = [jnp.where(behind, t, o) for t, o in zip(theirs, ours)]
    back = [jnp.where(behind, o, t) for t, o in zip(theirs, ours)]
    return over(front, back)


def merge_kernel(ctl, mine, got, *refs, places, unit):
    sends, (image, tops) = refs[-2 - places:-2], refs[-2:]
    turn = pl.program_id(0)
    width = image.shape[2]

    def merge_strip(at):
        cols = pl.ds(at, LANES)
        merged = merge_pair(ctl, mine, got, cols)
        for k in range(4):
            image[k, :, cols] = merged[k]
        top = functools.reduce(jnp.maximum, merged)
        tops[0:8, cols] = jnp.max(top.reshape(unit // 8, 8, LANES), axis=0)

    each_strip(width, merge_strip)
    exponent = exponent_of(jnp.max(tops[0:8, :], axis=0, keepdims=True))
    tops[0:8, :] = jnp.broadcast_to(jnp.exp2(-exponent) * CODES, (8, width))
    row = jnp.broadcast_to(exponent, (8, width)).astype(jnp.int32)

    for k, send in enumerate(sends):
        @pl.when(turn == k)
        def _(send=send):
            def put(at):
                cols = pl.ds(at, LANES)
                factor = tops[0:1, cols]
                for k in range(2):
                    send[0, k * unit:(k + 1) * unit, cols] = pack(image[2 * k, :, cols], image[2 * k + 1, :, cols], factor)

            each_strip(width, put)
            send[0, 2 * unit:2 * unit + 8, :] = row


def gather_kernel(ctl, *refs, unit, blocks):
    parts, send, image = refs[:-2], refs[-2], refs[-1]
    width = image.shape[2]
    for me in range(len(parts)):
        @pl.when(ctl[0] == me)
        def _(me=me):
            def put(at):
                cols = pl.ds(at, LANES)
                total = None
                for j in range(len(parts)):
                    got = parts[me ^ j]
                    scale = scale_of(got[0, 2 * unit:2 * unit + 1, cols])
                    part = []
                    for k in range(2):
                        part += unpack(got[0, k * unit:(k + 1) * unit, cols], scale)
                    total = part if total is None else over(total, part)
                for k in range(4):
                    image[k, :, cols] = total[k]

            each_strip(width, put)

    part = width // blocks
    half = unit // 2
    for b in range(blocks):
        wide = jnp.concatenate([image[k, :, b * part:(b + 1) * part] for k in range(4)], axis=1)
        exponent = exponent_of(jnp.max(wide, axis=0, keepdims=True))
        factor = jnp.exp2(-exponent) * CODES
        send[b, 0, 8:8 + half, :] = pack(wide[:half], wide[half:], factor)
        send[b, 0, 0:8, :] = jnp.broadcast_to(exponent, (8, 4 * part)).astype(jnp.int32)


def compose_kernel(got, *refs, unit, blocks):
    out = refs[-1]
    part = out.shape[2]
    half = unit // 2
    total = None
    for b in range(blocks):
        scale = scale_of(got[b, 0, 0:1, :])
        wide = jnp.concatenate(unpack(got[b, 0, 8:8 + half, :], scale), axis=0)
        layer = [wide[:, k * part:(k + 1) * part] for k in range(4)]
        total = layer if total is None else over(total, layer)
    for k in range(4):
        out[k] = total[k]


def params():
    return pltpu.CompilerParams(vmem_limit_bytes=VMEM_LIMIT, dimension_semantics=("arbitrary",))


def unit_index(groups, units, bit):
    half = (groups // 2) * units

    def index(i, ctl):
        rest = lax.rem(i, half)
        parity = jnp.where(i < half, 1 - ctl[bit], ctl[bit])
        return (2 * (rest // units) + parity) * units + lax.rem(rest, units)

    return index


def split_outputs(groups, units, unit, width):
    half = (groups // 2) * units
    shapes = [
        jax.ShapeDtypeStruct((half, 4, unit, width), jnp.float32),
        jax.ShapeDtypeStruct((half, 4, unit, width), jnp.float32),
    ]
    specs = [
        pl.BlockSpec((1, 4, unit, width), lambda i, ctl: (jnp.minimum(i, half - 1), 0, 0, 0)),
        pl.BlockSpec((1, 4, unit, width), lambda i, ctl: (jnp.maximum(i - half, 0), 0, 0, 0)),
    ]
    return shapes, specs


def band(shape, dim, offset):
    place = lax.broadcasted_iota(jnp.int32, shape, dim) - lax.broadcasted_iota(jnp.int32, shape, 1 - dim) - offset
    return jnp.where(place == 1, 1.0, jnp.where(place == -1, -1.0, 0.0)).astype(jnp.bfloat16)


def render(ctl, light, table, slope, field, before, after, *, groups, units, unit, rows, offset, halo_at):
    layers, total, width = field.shape
    block = math.lcm(unit, 16)
    tall = padded_rows(unit)
    row_band = band((tall, tall + 32), 1, 16)
    place = lax.broadcasted_iota(jnp.int32, (tall, tall + 32), 1)
    top, bottom = place >= 16, place < 16 + unit
    row_bands = jnp.stack([
        jnp.where(jnp.logical_and(jnp.logical_or(top, kind % 2 == 0), jnp.logical_or(bottom, kind < 2)), row_band, 0)
        for kind in range(4)
    ])
    column_bands = jnp.stack([band((3 * LANES, LANES), 0, k * LANES) for k in range(3)])
    half = (groups // 2) * units
    index = unit_index(groups, units, 0)

    def start(i, ctl):
        unit_at = index(i, ctl)
        return (unit_at // units) * rows + offset + lax.rem(unit_at, units) * unit

    def main_at(i, ctl):
        return (0, start(i, ctl) // block, 0)

    def above_at(i, ctl):
        return (0, jnp.maximum(start(i, ctl) - 1, 0) // 16, 0)

    def below_at(i, ctl):
        return (0, jnp.minimum(start(i, ctl) + unit, total - 1) // 16, 0)

    shapes, specs = split_outputs(groups, units, unit, width)
    kernel = functools.partial(
        render_kernel, groups=groups, units=units, unit=unit, block=block, rows=rows, offset=offset, total=total
    )
    cells = layers * 2 * half * unit * width
    return pl.pallas_call(
        kernel,
        grid_spec=pltpu.PrefetchScalarGridSpec(
            num_scalar_prefetch=1,
            grid=(2 * half,),
            in_specs=[
                pl.BlockSpec(memory_space=pltpu.SMEM),
                pl.BlockSpec(table.shape, lambda i, ctl: (0, 0)),
                pl.BlockSpec(slope.shape, lambda i, ctl: (0, 0)),
                pl.BlockSpec((4, tall, tall + 32), lambda i, ctl: (0, 0, 0)),
                pl.BlockSpec((3, 3 * LANES, LANES), lambda i, ctl: (0, 0, 0)),
                pl.BlockSpec((layers, block, width), main_at),
                pl.BlockSpec((layers, 16, width), above_at),
                pl.BlockSpec((layers, 16, width), below_at),
                pl.BlockSpec((1, unit, width), lambda i, ctl: (index(i, ctl), halo_at, 0)),
                pl.BlockSpec((1, unit, width), lambda i, ctl: (index(i, ctl), halo_at, 0)),
            ],
            out_specs=specs,
            scratch_shapes=[
                pltpu.VMEM((layers, tall + 32, width) if block != unit else (1, 16, LANES), jnp.bfloat16),
                pltpu.VMEM((layers, tall, LANES), jnp.float32),
                pltpu.VMEM((layers, tall, LANES), jnp.float32),
                pltpu.VMEM((4, tall, width), jnp.float32),
                pltpu.VMEM((max(block, tall + 32), width) if block != unit else (8, LANES), jnp.float32),
                pltpu.VMEM((2, tall, width) if block != unit else (1, 8, LANES), jnp.float32),
            ],
        ),
        out_shape=shapes,
        compiler_params=params(),
        cost_estimate=pl.CostEstimate(flops=16384 * cells, bytes_accessed=6 * cells, transcendentals=cells),
        name="render",
    )(ctl, light, table, slope, row_bands, column_bands, field, field, field, before, after)


def merge(ctl, mine, got, so_far, *, at, members, places, unit):
    width = mine.shape[3]
    cells = 4 * places * unit * width
    image = pl.BlockSpec((1, 4, unit, width), lambda i, ctl: (ctl[0] ^ i, 0, 0, 0))
    return pl.pallas_call(
        functools.partial(merge_kernel, places=places, unit=unit),
        grid_spec=pltpu.PrefetchScalarGridSpec(
            num_scalar_prefetch=1,
            grid=(places,),
            in_specs=[image, image] + [pl.BlockSpec(memory_space=pl.ANY)] * len(so_far),
            out_specs=[pl.BlockSpec((1, 2 * unit + 8, width), lambda i, ctl: (at, 0, 0))] * places,
            scratch_shapes=[pltpu.VMEM((4, unit, width), jnp.float32), pltpu.VMEM((8, width), jnp.float32)],
        ),
        out_shape=[jax.ShapeDtypeStruct((members, 2 * unit + 8, width), jnp.int32)] * places,
        input_output_aliases={3 + k: k for k in range(len(so_far))},
        compiler_params=params(),
        cost_estimate=pl.CostEstimate(flops=32768 * cells, bytes_accessed=cells, transcendentals=0),
        name="merge",
    )(ctl, mine, got, *so_far)


def gather_parts(ctl, parts, *, units, unit, blocks):
    width = parts[0].shape[2]
    cells = 4 * units * unit * width
    return pl.pallas_call(
        functools.partial(gather_kernel, unit=unit, blocks=blocks),
        grid_spec=pltpu.PrefetchScalarGridSpec(
            num_scalar_prefetch=1,
            grid=(units,),
            in_specs=[pl.BlockSpec((1, 2 * unit + 8, width), lambda i, ctl: (i, 0, 0))] * len(parts),
            out_specs=pl.BlockSpec((blocks, 1, unit // 2 + 8, 4 * width // blocks), lambda i, ctl: (0, i, 0, 0)),
            scratch_shapes=[pltpu.VMEM((4, unit, width), jnp.float32)],
        ),
        out_shape=jax.ShapeDtypeStruct((blocks, units, unit // 2 + 8, 4 * width // blocks), jnp.int32),
        compiler_params=params(),
        cost_estimate=pl.CostEstimate(flops=131072 * cells, bytes_accessed=cells, transcendentals=0),
        name="gather_parts",
    )(ctl, *parts)


def compose(got, so_far, *, unit, first, rows):
    blocks, units = got.shape[:2]
    part = got.shape[3] // 4
    cells = 4 * units * unit * part * blocks
    operands = [got]
    in_specs = [pl.BlockSpec((blocks, 1, unit // 2 + 8, 4 * part), lambda i: (0, i, 0, 0))]
    if so_far is not None:
        operands.append(so_far)
        in_specs.append(pl.BlockSpec(memory_space=pl.ANY))
    return pl.pallas_call(
        functools.partial(compose_kernel, unit=unit, blocks=blocks),
        grid=(units,),
        in_specs=in_specs,
        out_specs=pl.BlockSpec((4, unit, part), lambda i: (0, first + i, 0)),
        out_shape=jax.ShapeDtypeStruct((4, rows, part), jnp.float32),
        input_output_aliases={1: 0} if so_far is not None else {},
        compiler_params=params(),
        cost_estimate=pl.CostEstimate(flops=32768 * cells, bytes_accessed=cells, transcendentals=0),
        name="compose",
    )(*operands)


def per_device(field, transfer, bin_order, light_angles):
    tiles = lax.axis_size("tile")
    blocks = lax.axis_size("depth")
    devices = tiles * blocks
    layers, total, width = field.shape
    rows = total // tiles
    unit = unit_rows(rows)
    places = tiles // 2

    table = jnp.take(transfer, bin_order, axis=1)
    table = table * jnp.array([[1.0], [1.0], [1.0], [0.01]], jnp.float32)
    bins = table.shape[1]
    slope = jnp.concatenate([table[:, 1:] - table[:, :-1], jnp.zeros_like(table[:, :1])], axis=1)
    table = jnp.concatenate([table, slope[:ON_MATRIX - 4]], axis=0)
    slope = jnp.pad(slope, ((0, 4), (0, LANES - bins)))
    coarse = lax.reduce_precision(table, exponent_bits=8, mantissa_bits=7)
    table = jnp.concatenate([coarse, table - coarse], axis=0)
    spread = jnp.eye(16, dtype=jnp.float32)
    table = (table[:, None, :, None] * spread[None, :, None, :]).reshape(2 * ON_MATRIX * 16, bins * 16)
    table = table.astype(jnp.bfloat16)
    azimuth, polar = light_angles[0], light_angles[1]
    light = 0.105 * jnp.stack(
        [jnp.cos(azimuth) * jnp.sin(polar), jnp.sin(azimuth) * jnp.sin(polar), jnp.cos(polar)]
    )

    tile = lax.axis_index("tile")
    core, place = (tile & 1).astype(jnp.int32), (tile >> 1).astype(jnp.int32)
    render_control = jnp.stack([core, core])
    merge_control = jnp.stack([place, core])
    up = [(i, i + 1) for i in range(devices - 1)]
    down = [(j, i) for i, j in up]
    both = ("depth", "tile")

    count = rows // unit
    starts = [n * unit for n in range(count)]

    def cut(layer, first, stop):
        part = field.reshape(layers, tiles, rows, width)[layer:layer + 1, :, first * unit:stop * unit]
        return part.reshape(tiles, (stop - first) * unit, width)

    halos = []
    for first, stop in [(0, 1), (1, count)][:count]:
        ends = (cut(layers - 1, first, stop), cut(0, first, stop))
        if halos:
            ends, _ = lax.optimization_barrier((ends, halos[0][:2]))
        pair = (lax.ppermute(ends[0], both, up), lax.ppermute(ends[1], both, down))
        halos += [pair + (n - first,) for n in range(first, stop)]

    def exchange(send, distance):
        return lax.ppermute(send, "tile", [(i, i ^ distance) for i in range(tiles)])

    chain = []
    waits = []

    def after_last(control):
        if chain:
            control, _, _ = lax.optimization_barrier((control, chain[-1], list(waits)))
            waits.clear()
        return control

    state = [None] * count

    def start_chunk(n):
        before, after, at = halos[n]
        send, keep = render(
            after_last(render_control), light, table, slope, field, before, after,
            groups=tiles, units=1, unit=unit, rows=rows, offset=starts[n], halo_at=at,
        )
        chain.append(send)
        state[n] = (keep, exchange(send, 1))

    def merge_group(members):
        sends = []
        for at, n in enumerate(members):
            mine, got = state[n]
            sends = merge(
                after_last(merge_control), mine, got, sends, at=at, members=len(members), places=places, unit=unit
            )
            chain.append(sends[-1])
        return [sends[0]] + [exchange(sends[k], 2 * k) for k in range(1, places)]

    def block_group(members, parts):
        send = gather_parts(after_last(merge_control), parts, units=len(members), unit=unit, blocks=blocks)
        chain.append(send)
        return lax.all_to_all(send, "depth", split_axis=0, concat_axis=0, tiled=True)

    early, late = list(range(count - 1)), [count - 1]
    results = []
    if early:
        for n in early:
            start_chunk(n)
        early_parts = merge_group(early)
        start_chunk(count - 1)
        waits.extend(early_parts)
        results.append(block_group(early, early_parts))
    else:
        start_chunk(count - 1)
    results.append(block_group(late, merge_group(late)))
    final = None
    done = 0
    for result in results:
        final = compose(result, final, unit=unit, first=done, rows=rows)
        done += result.shape[1]
    return final


def solution(mesh):
    in_specs = (P(("depth", "tile"), None, None), P(), P(), P())
    out_specs = P(None, "tile", "depth")
    return jax.shard_map(
        per_device, mesh=mesh, in_specs=in_specs, out_specs=out_specs, check_vma=False
    )
```
